32 devices in a mesh: dom: 8 (over z, x), snap: 4 (over y, core).
Axes of the slice: x: 2, y: 2, z: 4, core: 2. Of those that a mesh axis runs over, the one named last changes fastest.
Arguments:
- feat: bfloat16 [4, 1024, 512], P('snap', 'dom'), may hold values from -6 to 6
- w_struct: bfloat16 [512, 1536], replicated, may hold values from -0.25 to 0.25
- w_temp: bfloat16 [512, 1536], replicated, may hold values from -0.25 to 0.25
- pos_embed: bfloat16 [4, 512], replicated, may hold values from -3 to 3
- rel_bias: float32 [4, 8], replicated, may hold values from -1.5 to 1.5
- nbr: int32 [4, 1024, 8], P('snap', 'dom'), may hold values from 0 to 191
- rel_type: int32 [4, 1024, 8], P('snap', 'dom'), may hold values from 0 to 3
- send_idx: int32 [4, 8, 8, 8], P('snap', 'dom'), may hold values from 0 to 127
- active: int32 [4, 1024], P(None, ('dom', 'snap')), may hold values 0 or 1
- cotangent: bfloat16 [4, 1024, 512], P(None, ('dom', 'snap')), may hold values from -6 to 6
Outputs:
- grad_feat: bfloat16 [4, 1024, 512], P('snap', 'dom')
- grad_wtemp: float32 [512, 1536], P('snap')
The draws below stay inside these ranges and needn't reach their ends.
Inputs may be any that keep to these rules, and one draw needn't show every extreme that they name: `nbr`: rows of the partition's key table: its 128 own entities first, then 8 halo rows from each partition in order.
All inputs are finite; a program needn't handle non-finite values. No bound on the sum of `active` on one device may be relied on, other than what follows from the above.
Results may differ from the reference program's by a relative error of at most 0.024.
Values may be sent and summed in bfloat16 or wider, within the bound.
No kernel may reach another device: no remote copies, remote signals or barrier semaphores. Data moves between devices by JAX's collectives and lax.ppermute only.
A program may use at most 64 MiB of HBM per device.

```python
import jax
import jax.numpy as jnp
from jax import lax

D = 512
HEADS = 8
REL = 4
DEG = 8
PEER = 8
ENT_DEV = 128
ENTITIES = 1024
SNAPS = 4
KEYS = 192
N_DOM = 8


def place_ends(entries, rng, low, high):
    shape = entries.shape
    place = [jax.random.randint(jax.random.fold_in(rng, axis), (), 0, shape[axis]) for axis in range(len(shape))]
    entries = entries.at[tuple(place)].set(low)
    longest = shape.index(max(shape))
    place[longest] = (place[longest] + 1) % shape[longest]
    return entries.at[tuple(place)].set(high)


def block_scale(stream_key, shape, shards, least, high):
    def one(position, blocks):
        steps = jax.random.uniform(jax.random.fold_in(jax.random.fold_in(stream_key, 6), position), (blocks,), jnp.float32, least / len(shards), high / len(shards))
        return jnp.repeat(jnp.exp(steps), shape[position] // blocks).reshape((-1,) + (1,) * (len(shape) - position - 1))

    loudness = one(*shards[0])
    for cut in shards[1:]:
        loudness = loudness * one(*cut)
    return loudness


def noise(stream_key, dims, deviation, reach, shards=(), held_as=jnp.bfloat16):
    gain = block_scale(stream_key, dims, shards, -0.22, 0.18) if shards else 1.0
    result = jax.random.normal(stream_key, dims, jnp.float32) * deviation * gain
    return jnp.minimum(jnp.maximum(result, -reach), reach).astype(held_as)


def setup_inputs(seed: int = 0) -> dict:
    streams_of = jax.random.split(jax.random.key(seed), 11)
    feat = noise(streams_of[0], (SNAPS, ENTITIES, D), 1.0, 6.0, ((0, 4), (1, 8)))
    w_struct = noise(streams_of[1], (D, 3 * D), D ** -0.5, 0.25)
    w_temp = noise(streams_of[2], (D, 3 * D), D ** -0.5, 0.25)
    pos_embed = noise(streams_of[3], (SNAPS, D), 0.5, 3.0)
    rel_bias = jnp.clip(jax.random.uniform(streams_of[4], (REL, HEADS), jnp.float32, -1.5, 1.5), -1.5, 1.5)
    nbr = place_ends(jax.random.randint(streams_of[5], (SNAPS, ENTITIES, DEG), 0, KEYS), jax.random.fold_in(streams_of[5], 1), 0, KEYS - 1).astype(jnp.int32)
    rel_type = place_ends(jax.random.randint(streams_of[6], (SNAPS, ENTITIES, DEG), 0, REL), jax.random.fold_in(streams_of[6], 1), 0, REL - 1).astype(jnp.int32)
    send_idx = place_ends(jax.random.randint(streams_of[7], (SNAPS, N_DOM, N_DOM, PEER), 0, ENT_DEV), jax.random.fold_in(streams_of[7], 1), 0, ENT_DEV - 1).astype(jnp.int32)
    active = place_ends((jax.random.randint(streams_of[8], (SNAPS, ENTITIES), 0, 4) < 3).astype(jnp.int32), jax.random.fold_in(streams_of[8], 1), 0, 1)
    cotangent = noise(streams_of[9], (SNAPS, ENTITIES, D), 1.0, 6.0, ((1, 32),))
    return {"feat": feat, "w_struct": w_struct, "w_temp": w_temp, "pos_embed": pos_embed, "rel_bias": rel_bias, "nbr": nbr, "rel_type": rel_type, "send_idx": send_idx, "active": active, "cotangent": cotangent}


def edge_scores(rel_ids, rel_bias):
    onehot = (rel_ids[..., None] == jnp.arange(rel_bias.shape[0], dtype=jnp.int32)).astype(jnp.float32)
    return jnp.einsum('rek,kh->reh', onehot, rel_bias.astype(jnp.float32), precision=lax.Precision.HIGHEST)

def struct_core(query, key_tab, val_tab, links, edge_add):
    row_count, width = query.shape
    slots = links.shape[1]
    head_dim = width // HEADS
    keys_g = key_tab[links].reshape(row_count, slots, HEADS, head_dim)
    vals_g = val_tab[links].reshape(row_count, slots, HEADS, head_dim)
    query_h = query.reshape(row_count, HEADS, head_dim)
    scores = jnp.einsum('rhc,rehc->reh', query_h, keys_g) * head_dim ** (-0.5) + edge_add
    weights = jax.nn.softmax(scores, axis=1)
    rounded = lax.optimization_barrier(weights.astype(jnp.bfloat16)).astype(jnp.float32)
    return jnp.einsum('reh,rehc->rhc', rounded, vals_g).reshape(row_count, width)

def temp_allowed(active_blk):
    snaps = active_blk.shape[0]
    later = jnp.arange(snaps, dtype=jnp.int32)[:, None]
    earlier = jnp.arange(snaps, dtype=jnp.int32)[None, :]
    causal = (earlier <= later)[..., None]
    itself = (earlier == later)[..., None]
    return causal & (itself | (active_blk[None, :, :] == 1))

def temp_core(t_query, t_key, t_value, allowed):
    snaps, count, width = t_query.shape
    head_dim = width // HEADS
    query_h = t_query.reshape(snaps, count, HEADS, head_dim)
    key_h = t_key.reshape(snaps, count, HEADS, head_dim)
    value_h = t_value.reshape(snaps, count, HEADS, head_dim)
    scores = jnp.einsum('tmhc,umhc->tumh', query_h, key_h) * head_dim ** (-0.5)
    scores = jnp.where(allowed[..., None], scores, -1e+30)
    weights = jax.nn.softmax(scores, axis=1)
    rounded = lax.optimization_barrier(weights.astype(jnp.bfloat16)).astype(jnp.float32)
    return jnp.einsum('tumh,umhc->tmhc', rounded, value_h).reshape(snaps, count, width)

def reference(feat, w_struct, w_temp, pos_embed, rel_bias, nbr, rel_type, send_idx, active, cotangent):
    width = D
    cot_f = cotangent.astype(jnp.float32)

    def halo_index(send_s):
        offsets = (jnp.arange(N_DOM, dtype=jnp.int32) * ENT_DEV)[:, None, None]
        return jnp.transpose(send_s + offsets, (1, 0, 2)).reshape(N_DOM, N_DOM * PEER)

    def struct_inputs(x_snap, send_s):
        proj = jnp.dot(x_snap, w_struct, preferred_element_type=jnp.float32).astype(jnp.bfloat16)
        query = proj[:, :width].astype(jnp.float32).reshape(N_DOM, ENT_DEV, width)
        pairs = proj[:, width:]
        halo_ids = halo_index(send_s)
        owned = pairs.reshape(N_DOM, ENT_DEV, 2 * width)
        table = jnp.concatenate([owned, pairs[halo_ids]], axis=1).astype(jnp.float32)
        return (query, table, halo_ids)

    def forward_snap(items):
        x_snap, nbr_s, rel_s, send_s = items
        query, table, halo_ids = struct_inputs(x_snap, send_s)
        edge_add = edge_scores(rel_s, rel_bias).reshape(N_DOM, ENT_DEV, DEG, HEADS)
        links = nbr_s.reshape(N_DOM, ENT_DEV, DEG)
        summed = lax.map(lambda part: struct_core(part[0], part[1][:, :width], part[1][:, width:], part[2], part[3]), (query, table, links, edge_add)).reshape(ENTITIES, width)
        hidden = (x_snap.astype(jnp.float32) + jax.nn.elu(summed)).astype(jnp.bfloat16)
        return (hidden, summed)
    hstruct, aggs = lax.map(forward_snap, (feat, nbr, rel_type, send_idx))
    z_in = (hstruct.astype(jnp.float32) + pos_embed.astype(jnp.float32)[:, None, :]).astype(jnp.bfloat16)
    z_flat = z_in.reshape(-1, width)
    t_proj = jnp.dot(z_flat, w_temp, preferred_element_type=jnp.float32).astype(jnp.bfloat16)
    t_proj = t_proj.reshape(SNAPS, ENTITIES, 3 * width).astype(jnp.float32)
    allowed = temp_allowed(active)
    _, pull = jax.vjp(lambda a_in, b_in, c_in: temp_core(a_in, b_in, c_in, allowed), t_proj[..., :width], t_proj[..., width:2 * width], t_proj[..., 2 * width:])
    grads_t = pull(cot_f)
    dt_proj = jnp.concatenate(grads_t, axis=-1).astype(jnp.bfloat16).reshape(-1, 3 * width)
    grad_wtemp = lax.dot_general(z_flat, dt_proj, (((0,), (0,)), ((), ())), preferred_element_type=jnp.float32)
    d_z = cot_f + jnp.dot(dt_proj, w_temp.T, preferred_element_type=jnp.float32).reshape(SNAPS, ENTITIES, width)
    d_hidden = d_z.astype(jnp.bfloat16)

    def backward_snap(items):
        x_snap, nbr_s, rel_s, send_s, agg_s, dh_s = items
        query, table, halo_ids = struct_inputs(x_snap, send_s)
        edge_add = edge_scores(rel_s, rel_bias).reshape(N_DOM, ENT_DEV, DEG, HEADS)
        links = nbr_s.reshape(N_DOM, ENT_DEV, DEG)
        dh_f = dh_s.astype(jnp.float32)
        d_agg = (dh_f * jnp.where(agg_s > 0, 1.0, jnp.exp(agg_s))).reshape(N_DOM, ENT_DEV, width)

        def one_part(part):
            query_p, table_p, links_p, edge_p, grad_p = part
            _, pull_p = jax.vjp(lambda a_in, b_in, c_in: struct_core(a_in, b_in, c_in, links_p, edge_p), query_p, table_p[:, :width], table_p[:, width:])
            return pull_p(grad_p)
        d_query, d_key, d_val = lax.map(one_part, (query, table, links, edge_add, d_agg))
        d_pairs = jnp.concatenate([d_key, d_val], axis=-1)
        summed = d_pairs[:, :ENT_DEV].reshape(ENTITIES, 2 * width)
        summed = summed.at[halo_ids.reshape(-1)].add(d_pairs[:, ENT_DEV:].reshape(-1, 2 * width))
        d_proj = jnp.concatenate([d_query.reshape(ENTITIES, width), summed], axis=-1).astype(jnp.bfloat16)
        return (dh_f + jnp.dot(d_proj, w_struct.T, preferred_element_type=jnp.float32)).astype(jnp.bfloat16)
    grad_feat = lax.map(backward_snap, (feat, nbr, rel_type, send_idx, aggs, d_hidden))
    return (grad_feat, grad_wtemp)
```

```python
import functools

import jax
import jax.numpy as jnp
from jax import lax
from jax.experimental import pallas as pl
from jax.experimental.pallas import tpu as pltpu
from jax.sharding import PartitionSpec as P

F32 = jnp.float32
BF16 = jnp.bfloat16
LANES = 128
NEG = -1e30
VMEM = pl.BlockSpec(memory_space=pltpu.VMEM)
SMEM = pl.BlockSpec(memory_space=pltpu.SMEM)


def dot_nn(a, b):
    return lax.dot_general(a, b, (((1,), (0,)), ((), ())), preferred_element_type=F32)


def dot_nt(a, b):
    return lax.dot_general(a, b, (((1,), (1,)), ((), ())), preferred_element_type=F32)


def dot_tn(a, b):
    return lax.dot_general(a, b, (((0,), (0,)), ((), ())), preferred_element_type=F32)


def stack_heads(block, head_dim):
    rows, lanes = block.shape
    head = lax.broadcasted_iota(jnp.int32, (rows, lanes), 1) // head_dim
    zero = jnp.zeros_like(block)
    return jnp.concatenate(
        [jnp.where(head == g, block, zero) for g in range(lanes // head_dim)], axis=0
    )


def unstack_heads(stacked, head_dim):
    lanes = stacked.shape[1]
    groups = lanes // head_dim
    rows = stacked.shape[0] // groups
    head = lax.broadcasted_iota(jnp.int32, (rows, lanes), 1) // head_dim
    out = stacked[:rows]
    for g in range(1, groups):
        out = jnp.where(head == g, stacked[g * rows : (g + 1) * rows], out)
    return out


def own_kernel(heads, x_ref, w_ref, nbr_ref, rel_ref, bias_ref, proj_ref, weight_ref):
    rows, width = x_ref.shape
    keys = weight_ref.shape[2]
    kinds = bias_ref.shape[0]
    slots = nbr_ref.shape[1]
    scale = (width // heads) ** (-0.5)
    x = x_ref[...]
    for part in range(3):
        cols = slice(part * width, (part + 1) * width)
        out = dot_nn(x, w_ref[:, cols]).astype(BF16)
        if part == 0:
            out = (out.astype(F32) * scale).astype(BF16)
        proj_ref[:, cols] = out
    code = nbr_ref[...] * kinds + rel_ref[...]
    spot = lax.broadcasted_iota(jnp.int32, (rows, keys), 1) * kinds
    gain = jnp.exp(bias_ref[...])
    counts = []
    for r in range(kinds):
        here = spot + r
        count = jnp.zeros((rows, keys), F32)
        for k in range(slots):
            count = count + jnp.where(code[:, k : k + 1] == here, 1.0, 0.0)
        counts.append(count)
    for h in range(heads):
        total = counts[0] * gain[0:1, h : h + 1]
        for r in range(1, kinds):
            total = total + counts[r] * gain[r : r + 1, h : h + 1]
        weight_ref[h] = total


def forward_kernel(
    heads, x_ref, halo_ref, w_ref, proj_ref, weight_ref, hidden_ref, agg_ref, tab_ref, attn_ref
):
    rows, width = x_ref.shape
    keys = weight_ref.shape[2]
    halo_rows = halo_ref.shape[0]
    head_dim = width // heads
    group = LANES // head_dim
    tab_ref[:rows, :] = proj_ref[:, width:]
    tab_ref[rows : rows + halo_rows, :] = dot_nn(halo_ref[...], w_ref[:, width:]).astype(BF16)
    if keys > rows + halo_rows:
        tab_ref[rows + halo_rows :, :] = jnp.zeros((keys - rows - halo_rows, 2 * width), BF16)
    for p in range(width // LANES):
        cols = slice(p * LANES, (p + 1) * LANES)
        vcols = slice(width + p * LANES, width + (p + 1) * LANES)
        kk = stack_heads(tab_ref[:, cols], head_dim)
        vv = stack_heads(tab_ref[:, vcols], head_dim)
        score = dot_nt(proj_ref[:, cols], kk)
        parts = []
        for g in range(group):
            wt = weight_ref[p * group + g]
            s = jnp.where(wt > 0, score[:, g * keys : (g + 1) * keys], NEG)
            top = jnp.max(s, axis=1, keepdims=True)
            e = jnp.exp(s - top) * wt
            parts.append((e * (1.0 / jnp.sum(e, axis=1, keepdims=True))).astype(BF16))
        attn = jnp.concatenate(parts, axis=1)
        attn_ref[p] = attn
        agg = dot_nn(attn, vv)
        agg_ref[:, cols] = agg
        elu = jnp.where(agg > 0, agg, jnp.exp(jnp.minimum(agg, 0.0)) - 1.0)
        hidden_ref[:, cols] = (x_ref[:, cols].astype(F32) + elu).astype(BF16)


def temporal_kernel(snaps, heads, me_ref, pos_ref, w_ref, *refs):
    hid = refs[:snaps]
    cot = refs[snaps : 2 * snaps]
    terms_ref, dt_own_ref, cot_own_ref, z_s, tp_s, dt_s, *wide = refs[2 * snaps :]
    local, width = hid[0].shape
    ents = local // snaps
    rows = snaps * ents
    head_dim = width // heads
    group = LANES // head_dim
    scale = head_dim ** (-0.5)
    me = me_ref[0]
    cot_rows = [cot[m].at[:rows, :] for m in range(snaps)]
    if wide:
        for m in range(snaps):
            wide[0][m] = hid[m][...].astype(F32)
            wide[1][m] = cot[m][:rows, :].astype(F32)
        hid = [wide[0].at[m] for m in range(snaps)]
        cot_rows = [wide[1].at[m] for m in range(snaps)]
    pos = pos_ref[...].astype(F32)
    which = lax.broadcasted_iota(jnp.int32, pos.shape, 0)
    for n in range(snaps):
        t = lax.bitwise_xor(me, n)
        shift = jnp.sum(jnp.where(which == t, pos, 0.0), axis=0, keepdims=True)
        for m in range(snaps):
            b = lax.bitwise_xor(me, m)
            src = pl.ds(pl.multiple_of(b * ents, ents), ents)
            dst = pl.ds(pl.multiple_of(m * rows + t * ents, ents), ents)
            z_s[dst, :] = (hid[n][src, :].astype(F32) + shift).astype(z_s.dtype)
    z = z_s[...].astype(BF16)
    for part in range(3):
        cols = slice(part * width, (part + 1) * width)
        out = dot_nn(z, w_ref[:, cols]).astype(BF16)
        if part == 0:
            out = (out.astype(F32) * scale).astype(BF16)
        tp_s[:, cols] = out
    later = lax.broadcasted_iota(jnp.int32, (rows, rows), 0)
    early = lax.broadcasted_iota(jnp.int32, (rows, rows), 1)
    same = (later % ents) == (early % ents)
    past = same & (early < later)
    itself = early == later
    for m in range(snaps):
        blk = slice(m * rows, (m + 1) * rows)
        act = cot[m][rows : rows + 16, :rows].astype(F32)[0:1]
        allowed = itself | (past & (act > 0.5))
        for p in range(width // LANES):
            c0 = p * LANES
            q = tp_s[blk, c0 : c0 + LANES]
            kk = stack_heads(tp_s[blk, width + c0 : width + c0 + LANES], head_dim)
            vv = stack_heads(tp_s[blk, 2 * width + c0 : 2 * width + c0 + LANES], head_dim)
            ct = cot[m][:rows, c0 : c0 + LANES]
            score = dot_nt(q, kk)
            dattn = dot_nt(ct, vv).astype(BF16).astype(F32)
            attn_b, ds = [], []
            for g in range(group):
                s = jnp.where(allowed, score[:, g * rows : (g + 1) * rows], NEG)
                e = jnp.exp(s - jnp.max(s, axis=1, keepdims=True))
                a = e * (1.0 / jnp.sum(e, axis=1, keepdims=True))
                attn_b.append(a.astype(BF16))
                d = dattn[:, g * rows : (g + 1) * rows]
                ad = a * d
                ds.append((ad - a * jnp.sum(ad, axis=1, keepdims=True)).astype(BF16))
            ds = jnp.concatenate(ds, axis=1)
            attn_b = jnp.concatenate(attn_b, axis=1)
            dq = dot_nn(ds, kk) * scale
            dk = unstack_heads(dot_tn(ds, q), head_dim)
            dv = unstack_heads(dot_tn(attn_b, ct), head_dim)
            dt_s[blk, c0 : c0 + LANES] = dq.astype(BF16).astype(dt_s.dtype)
            dt_s[blk, width + c0 : width + c0 + LANES] = dk.astype(BF16).astype(dt_s.dtype)
            dt_s[blk, 2 * width + c0 : 2 * width + c0 + LANES] = dv.astype(BF16).astype(dt_s.dtype)
    share = width // snaps
    pick = (
        lax.broadcasted_iota(jnp.int32, (width, share), 0)
        == lax.broadcasted_iota(jnp.int32, (width, share), 1) + me * share
    )
    z_mine = dot_nn(z, jnp.where(pick, 1.0, 0.0).astype(BF16)).astype(BF16)
    for part in range(3):
        cols = slice(part * width, (part + 1) * width)
        terms_ref[:, cols] = dot_tn(z_mine, dt_s[:, cols].astype(BF16)).astype(BF16)
    for m in range(snaps):
        b = lax.bitwise_xor(me, m)
        dst = pl.ds(pl.multiple_of(b * ents, ents), ents)
        mine = pl.multiple_of(me * ents, ents)
        dt_own_ref[dst, :] = dt_s[pl.ds(m * rows + mine, ents), :]
        cot_own_ref[dst, :] = cot_rows[m][pl.ds(mine, ents), :]


def backward_kernel(
    heads,
    halo_rows,
    dt_ref,
    cot_ref,
    wt_ref,
    ws_ref,
    proj_ref,
    agg_ref,
    tab_ref,
    attn_ref,
    halo_ref,
    part_ref,
    dq_s,
    dtab_s,
):
    rows, width = cot_ref.shape
    keys = tab_ref.shape[0]
    head_dim = width // heads
    group = LANES // head_dim
    scale = head_dim ** (-0.5)
    dh = cot_ref[...].astype(F32) + dot_nt(dt_ref[...].astype(BF16), wt_ref[...])
    dh = dh.astype(BF16).astype(F32)
    part_ref[...] = dh
    agg = agg_ref[...]
    dagg = (dh * jnp.where(agg > 0, 1.0, jnp.exp(jnp.minimum(agg, 0.0)))).astype(BF16)
    for p in range(width // LANES):
        cols = slice(p * LANES, (p + 1) * LANES)
        vcols = slice(width + p * LANES, width + (p + 1) * LANES)
        kk = stack_heads(tab_ref[:, cols], head_dim)
        vv = stack_heads(tab_ref[:, vcols], head_dim)
        da = dagg[:, cols]
        dattn = dot_nt(da, vv).astype(BF16).astype(F32)
        attn_b = attn_ref[p]
        attn = attn_b.astype(F32)
        ad = attn * dattn
        ds = []
        for g in range(group):
            span = slice(g * keys, (g + 1) * keys)
            tot = jnp.sum(ad[:, span], axis=1, keepdims=True)
            ds.append((ad[:, span] - attn[:, span] * tot).astype(BF16))
        ds = jnp.concatenate(ds, axis=1)
        dq_s[:, cols] = (dot_nn(ds, kk) * scale).astype(BF16)
        dtab_s[:, cols] = unstack_heads(dot_tn(ds, proj_ref[:, cols]), head_dim).astype(BF16)
        dtab_s[:, vcols] = unstack_heads(dot_tn(attn_b, da), head_dim).astype(BF16)
    halo_ref[...] = dot_nt(dtab_s[rows : rows + halo_rows, :], ws_ref[:, width:]).astype(BF16)
    part_ref[...] += dot_nt(dq_s[...], ws_ref[:, :width]) + dot_nt(
        dtab_s[:rows, :], ws_ref[:, width:]
    )


def params(mib):
    return pltpu.CompilerParams(vmem_limit_bytes=mib * 1024 * 1024)


def gather_blocks(block, axis):
    count = lax.axis_size(axis)
    held = {0: block}
    bit = count // 2
    while bit:
        for m in sorted(held):
            pairs = [(i, i ^ bit) for i in range(count)]
            held[m ^ bit] = lax.ppermute(held[m], axis, pairs)
        bit //= 2
    return [held[m] for m in range(count)]


def per_device(
    feat, w_struct, w_temp, pos_embed, rel_bias, nbr, rel_type, send_idx, active, cotangent
):
    x = feat[0]
    local, width = x.shape
    heads = rel_bias.shape[1]
    doms = lax.axis_size("dom")
    snaps = lax.axis_size("snap")
    ents = local // snaps
    rows = snaps * ents
    route = send_idx[0, 0]
    halo_per = route.shape[1]
    halo_rows = doms * halo_per
    keys = -(-(local + halo_rows) // LANES) * LANES
    route_flat = route.reshape(-1)
    picks = (route_flat[:, None] == jnp.arange(local, dtype=jnp.int32)).astype(BF16)
    tiles = jnp.dot(picks, x, preferred_element_type=F32).astype(BF16)
    halo = lax.all_to_all(
        tiles.reshape(doms, halo_per, width), "dom", split_axis=0, concat_axis=0, tiled=True
    ).reshape(halo_rows, width)

    act_row = jnp.pad(active.astype(BF16).reshape(1, rows), ((0, 15), (0, width - rows)))
    cots = gather_blocks(
        jnp.concatenate([cotangent.reshape(rows, width), act_row], axis=0), "snap"
    )

    proj, weight = pl.pallas_call(
        functools.partial(own_kernel, heads),
        out_shape=(
            jax.ShapeDtypeStruct((local, 3 * width), BF16),
            jax.ShapeDtypeStruct((heads, local, keys), F32),
        ),
        in_specs=[VMEM] * 5,
        out_specs=(VMEM, VMEM),
        compiler_params=params(16),
        name="own_rows",
    )(x, w_struct, nbr[0], rel_type[0], rel_bias)

    lane_groups = width // LANES
    group = heads // lane_groups
    hidden, agg, tab, attn = pl.pallas_call(
        functools.partial(forward_kernel, heads),
        out_shape=(
            jax.ShapeDtypeStruct((local, width), BF16),
            jax.ShapeDtypeStruct((local, width), F32),
            jax.ShapeDtypeStruct((keys, 2 * width), BF16),
            jax.ShapeDtypeStruct((lane_groups, local, group * keys), BF16),
        ),
        in_specs=[VMEM] * 5,
        out_specs=(VMEM,) * 4,
        compiler_params=params(16),
        name="struct_forward",
    )(x, halo, w_struct, proj, weight)

    hids = gather_blocks(hidden, "snap")
    me = lax.axis_index("snap").astype(jnp.int32).reshape(1)
    share = width // snaps
    hold = F32 if ents % 16 else BF16
    terms, dt_own, cot_own = pl.pallas_call(
        functools.partial(temporal_kernel, snaps, heads),
        out_shape=(
            jax.ShapeDtypeStruct((share, 3 * width), BF16),
            jax.ShapeDtypeStruct((local, 3 * width), hold),
            jax.ShapeDtypeStruct((local, width), hold),
        ),
        in_specs=[SMEM, VMEM, VMEM] + [VMEM] * (2 * snaps),
        out_specs=(VMEM,) * 3,
        scratch_shapes=[
            pltpu.VMEM((snaps * rows, width), hold),
            pltpu.VMEM((snaps * rows, 3 * width), BF16),
            pltpu.VMEM((snaps * rows, 3 * width), hold),
        ]
        + ([] if hold == BF16 else [pltpu.VMEM((snaps, rows, width), F32)] * 2),
        compiler_params=params(32 if hold == BF16 else 56),
        name="temporal",
    )(me, pos_embed, w_temp, *hids, *cots)

    parts = lax.all_to_all(
        terms.reshape(doms, share // doms, 3 * width),
        "dom",
        split_axis=0,
        concat_axis=0,
        tiled=True,
    )
    halo_back, partial = pl.pallas_call(
        functools.partial(backward_kernel, heads, halo_rows),
        out_shape=(
            jax.ShapeDtypeStruct((halo_rows, width), BF16),
            jax.ShapeDtypeStruct((local, width), F32),
        ),
        in_specs=[VMEM] * 8,
        out_specs=(VMEM, VMEM),
        scratch_shapes=[
            pltpu.VMEM((local, width), BF16),
            pltpu.VMEM((keys, 2 * width), BF16),
        ],
        compiler_params=params(32),
        name="struct_backward",
    )(dt_own, cot_own, w_temp, w_struct, proj, agg, tab, attn)
    came = lax.all_to_all(
        halo_back.reshape(doms, halo_per, width), "dom", split_axis=0, concat_axis=0, tiled=True
    ).reshape(halo_rows, width)
    piece = jnp.sum(parts.astype(F32), axis=0).astype(BF16)
    whole = lax.all_to_all(
        jnp.broadcast_to(piece[None], (doms,) + piece.shape),
        "dom",
        split_axis=0,
        concat_axis=0,
        tiled=True,
    )
    grad_wtemp = whole.astype(F32).reshape(share, 3 * width)
    back = lax.dot_general(picks, came, (((0,), (0,)), ((), ())), preferred_element_type=F32)
    grad_feat = (partial + back).astype(BF16)
    return (grad_feat[None], grad_wtemp)


def solution(mesh):
    return jax.shard_map(
        per_device,
        mesh=mesh,
        in_specs=(
            P("snap", "dom", None),
            P(),
            P(),
            P(),
            P(),
            P("snap", "dom", None),
            P("snap", "dom", None),
            P("snap", "dom", None, None),
            P(None, ("dom", "snap")),
            P(None, ("dom", "snap"), None),
        ),
        out_specs=(P("snap", "dom", None), P("snap", None)),
        check_vma=False,
    )
```

```python
import functools

import jax
import jax.numpy as jnp
from jax import lax
from jax.experimental import pallas as pl
from jax.experimental.pallas import tpu as pltpu
from jax.sharding import PartitionSpec as P

F32 = jnp.float32
BF16 = jnp.bfloat16
LANES = 128
NEG = -1e30
VMEM = pl.BlockSpec(memory_space=pltpu.VMEM)
SMEM = pl.BlockSpec(memory_space=pltpu.SMEM)
ANY = pl.BlockSpec(memory_space=pl.ANY)


def dot_nn(a, b):
    return lax.dot_general(a, b, (((1,), (0,)), ((), ())), preferred_element_type=F32)


def dot_nt(a, b):
    return lax.dot_general(a, b, (((1,), (1,)), ((), ())), preferred_element_type=F32)


def dot_tn(a, b):
    return lax.dot_general(a, b, (((0,), (0,)), ((), ())), preferred_element_type=F32)


def stack_heads(block, head_dim):
    rows, lanes = block.shape
    head = lax.broadcasted_iota(jnp.int32, (rows, lanes), 1) // head_dim
    zero = jnp.zeros_like(block)
    return jnp.concatenate(
        [jnp.where(head == g, block, zero) for g in range(lanes // head_dim)], axis=0
    )


def unstack_heads(stacked, head_dim):
    lanes = stacked.shape[1]
    groups = lanes // head_dim
    rows = stacked.shape[0] // groups
    head = lax.broadcasted_iota(jnp.int32, (rows, lanes), 1) // head_dim
    out = stacked[:rows]
    for g in range(1, groups):
        out = jnp.where(head == g, stacked[g * rows : (g + 1) * rows], out)
    return out


class Fetch:

    def __init__(self, sems, *pairs):
        self.copies = [
            pltpu.make_async_copy(src, dst, sems.at[i]) for i, (src, dst) in enumerate(pairs)
        ]
        for copy in self.copies:
            copy.start()

    def wait(self, *which):
        for i in which:
            self.copies[i].wait()


def pick_rows(route_ref, local):
    doms, per = route_ref.shape
    lane = lax.broadcasted_iota(jnp.int32, (per, local), 1)
    sub = lax.broadcasted_iota(jnp.int32, (per, local), 0)
    tiles = []
    for r in range(doms):
        spot = jnp.zeros((per, local), jnp.int32)
        for j in range(per):
            spot = jnp.where(sub == j, route_ref[r, j], spot)
        tiles.append(jnp.where(lane == spot, 1.0, 0.0))
    return jnp.concatenate(tiles, axis=0).astype(BF16)


def tiles_kernel(route_ref, x_ref, out_ref):
    out_ref[...] = dot_nn(pick_rows(route_ref, x_ref.shape[0]), x_ref[...]).astype(BF16)


def own_kernel(x_ref, w_hbm, nbr_ref, rel_ref, act_ref, cot_ref, proj_ref, count_ref, load_ref, w_s, sems):
    rows, width = x_ref.shape
    kinds, _, keys = count_ref.shape
    slots = nbr_ref.shape[0]
    snaps, ents, _ = cot_ref.shape
    fetch = Fetch(sems, (w_hbm, w_s))
    for t in range(snaps):
        load_ref[t] = cot_ref[t]
    row = lax.broadcasted_iota(jnp.int32, (ents, ents), 0)
    col = lax.broadcasted_iota(jnp.int32, (ents, ents), 1)
    lane = lax.broadcasted_iota(jnp.int32, (ents, width), 1)
    flags = jnp.zeros((ents, width), F32)
    act = act_ref[...].astype(F32)
    for t in range(snaps):
        column = jnp.sum(jnp.where(row == col, act[t : t + 1, :], 0.0), axis=1, keepdims=True)
        flags = jnp.where(lane == t, column, flags)
    load_ref[snaps] = flags.astype(BF16)
    code = jnp.transpose((nbr_ref[...] * kinds + rel_ref[...]).astype(F32))
    spot = (lax.broadcasted_iota(jnp.int32, (rows, keys), 1) * kinds).astype(F32)
    for r in range(kinds):
        here = spot + float(r)
        count = jnp.zeros((rows, keys), F32)
        for k in range(slots):
            count = count + jnp.where(code[:, k : k + 1] == here, 1.0, 0.0)
        count_ref[r] = count.astype(BF16)
    fetch.wait(0)
    x = x_ref[...]
    for part in range(3):
        cols = slice(part * width, (part + 1) * width)
        proj_ref[:, cols] = dot_nn(x, w_s[:, cols]).astype(BF16)


def fill_table(tab_s, proj, halo, w_kv):
    rows, width = proj.shape[0], halo.shape[1]
    used = rows + halo.shape[0]
    tab_s[:rows, :] = proj[:, width:]
    for part in range(2):
        cols = slice(part * width, (part + 1) * width)
        tab_s[rows:used, cols] = dot_nn(halo[...], w_kv[:, cols]).astype(BF16)
    if tab_s.shape[0] > used:
        tab_s[used:, :] = jnp.zeros((tab_s.shape[0] - used, 2 * width), BF16)


def edge_attention(p, heads, proj, count, bias, tab_s, width):
    keys = tab_s.shape[0]
    head_dim = width // heads
    group = LANES // head_dim
    cols = slice(p * LANES, (p + 1) * LANES)
    kk = stack_heads(tab_s[:, cols], head_dim)
    score = dot_nt(proj[:, cols], kk) * head_dim ** (-0.5)
    gain = jnp.exp(bias[...])
    parts = []
    for g in range(group):
        h = p * group + g
        wt = count[0].astype(F32) * gain[0:1, h : h + 1]
        for r in range(1, count.shape[0]):
            wt = wt + count[r].astype(F32) * gain[r : r + 1, h : h + 1]
        s = jnp.where(wt > 0, score[:, g * keys : (g + 1) * keys], NEG)
        e = jnp.exp(s - jnp.max(s, axis=1, keepdims=True)) * wt
        parts.append(e * (1.0 / jnp.sum(e, axis=1, keepdims=True)))
    return kk, parts


def forward_kernel(
    heads, x_ref, bias_ref, halo_hbm, proj_hbm, count_hbm, w_hbm, hidden_ref,
    halo, proj, count, w_kv, tab_s, sems,
):
    width = x_ref.shape[1]
    head_dim = width // heads
    fetch = Fetch(
        sems,
        (halo_hbm, halo),
        (w_hbm.at[:, width:], w_kv),
        (proj_hbm, proj),
        (count_hbm, count),
    )
    fetch.wait(0, 1, 2, 3)
    fill_table(tab_s, proj, halo, w_kv)
    for p in range(width // LANES):
        cols = slice(p * LANES, (p + 1) * LANES)
        vcols = slice(width + p * LANES, width + (p + 1) * LANES)
        _, attn = edge_attention(p, heads, proj, count, bias_ref, tab_s, width)
        vv = stack_heads(tab_s[:, vcols], head_dim)
        agg = dot_nn(jnp.concatenate([a.astype(BF16) for a in attn], axis=1), vv)
        elu = jnp.where(agg > 0, agg, jnp.exp(jnp.minimum(agg, 0.0)) - 1.0)
        hidden_ref[:, cols] = (x_ref[:, cols].astype(F32) + elu).astype(BF16)


def each(lo, hi, unroll, body):
    if unroll:
        for i in range(lo, hi):
            body(i)
    else:
        lax.fori_loop(lo, hi, lambda i, c: (body(i), c)[1], 0)


def temporal_kernel(snaps, heads, me_ref, pos_ref, w_hbm, *refs):
    hid_hbm = refs[:snaps]
    cot_hbm = refs[snaps : 2 * snaps]
    (
        terms_ref, dt_own_ref, cot_own_ref,
        w_s, hid, cot, z_s, ct_s, tp_s, dt_s, act_s, s_s, d_s, a_s, ds_s, dk_s, dv_s, sems,
    ) = refs[2 * snaps :]
    _, local, width = hid.shape
    ents = cot.shape[2]
    head_dim = width // heads
    scale = head_dim ** (-0.5)
    unroll = snaps <= 4
    me = me_ref[0]
    fetch = Fetch(
        sems,
        *[(hid_hbm[n], hid.at[n]) for n in range(snaps)],
        (w_hbm, w_s),
        *[(cot_hbm[n], cot.at[n]) for n in range(snaps)],
    )
    pos = pos_ref[...].astype(F32)
    which = lax.broadcasted_iota(jnp.int32, pos.shape, 0)

    def rows_of(t):
        return pl.ds(t * local if isinstance(t, int) else pl.multiple_of(t * local, local), local)

    for n in range(snaps):
        t = lax.bitwise_xor(me, n)
        shift = jnp.sum(jnp.where(which == t, pos, 0.0), axis=0, keepdims=True)
        fetch.wait(n)
        z_s[rows_of(t), :] = (hid[n].astype(F32) + shift).astype(BF16)
    fetch.wait(snaps)
    for part in range(3):
        cols = slice(part * width, (part + 1) * width)
        tp_s[:, cols] = dot_nn(z_s[...], w_s[:, cols]).astype(BF16)
    fetch.wait(*range(snaps + 1, 2 * snaps + 1))
    for m in range(snaps):
        at = pl.multiple_of(lax.bitwise_xor(me, m) * ents, ents)
        for t in range(snaps):
            ct_s[pl.ds(t * local + at, ents), :] = cot[m, t].astype(ct_s.dtype)
        act_s[pl.ds(at, ents), :] = cot[m, snaps][:, :LANES].astype(F32)
    lane_head = lax.broadcasted_iota(jnp.int32, (width, LANES), 0) // head_dim
    fold = (lane_head == lax.broadcasted_iota(jnp.int32, (width, LANES), 1)).astype(F32).astype(BF16)
    head_lane = lax.broadcasted_iota(jnp.int32, (LANES, width), 1) // head_dim
    spread = (head_lane == lax.broadcasted_iota(jnp.int32, (LANES, width), 0)).astype(F32).astype(BF16)
    spread_scaled = (spread.astype(F32) * scale).astype(BF16)
    act = act_s[...]
    snap_lane = lax.broadcasted_iota(jnp.int32, act.shape, 1)
    dk_s[...] = jnp.zeros_like(dk_s)
    dv_s[...] = jnp.zeros_like(dv_s)

    def scores(t):
        def pair(u):
            q, k, v = (
                tp_s[rows_of(i), part * width : (part + 1) * width]
                for part, i in ((0, t), (1, u), (2, u))
            )
            s = dot_nn(q * k, fold) * scale
            on = jnp.sum(jnp.where(snap_lane == u, act, 0.0), axis=1, keepdims=True)
            s_s[u] = jnp.where((on > 0.5) | (u == t), s, NEG)
            d = dot_nn(ct_s[rows_of(t), :].astype(BF16) * v, fold)
            d_s[u] = d.astype(BF16).astype(F32)

        each(0, t + 1, unroll, pair)
        top = s_s[0]
        if unroll:
            for u in range(1, t + 1):
                top = jnp.maximum(top, s_s[u])
        else:
            top = lax.fori_loop(1, t + 1, lambda u, c: jnp.maximum(c, s_s[u]), top)
        zero = jnp.zeros_like(top)

        def expo(u, total):
            e = jnp.exp(s_s[u] - top)
            s_s[u] = e
            return total + e

        total = zero
        if unroll:
            for u in range(t + 1):
                total = expo(u, total)
        else:
            total = lax.fori_loop(0, t + 1, expo, total)
        inv = 1.0 / total

        def weigh(u, dot):
            a = s_s[u] * inv
            s_s[u] = a
            return dot + a * d_s[u]

        dot = zero
        if unroll:
            for u in range(t + 1):
                dot = weigh(u, dot)
        else:
            dot = lax.fori_loop(0, t + 1, weigh, dot)

        def keep(u):
            a = s_s[u]
            a_s[u] = a.astype(BF16)
            ds_s[u] = (a * (d_s[u] - dot)).astype(BF16)

        each(0, t + 1, unroll, keep)

        for p in range(width // LANES):
            c0 = p * LANES
            cols = slice(c0, c0 + LANES)
            q = tp_s[rows_of(t), cols].astype(F32)
            ct = ct_s[rows_of(t), cols].astype(F32)

            def back(u, dq):
                k = tp_s[rows_of(u), width + c0 : width + c0 + LANES].astype(F32)
                wide_ds = dot_nn(ds_s[u], spread_scaled[:, cols])
                wide_a = dot_nn(a_s[u], spread[:, cols])
                dk_s[rows_of(u), cols] += wide_ds * q
                dv_s[rows_of(u), cols] += wide_a * ct
                return dq + wide_ds * k

            dq = jnp.zeros_like(q)
            if unroll:
                for u in range(t + 1):
                    dq = back(u, dq)
            else:
                dq = lax.fori_loop(0, t + 1, back, dq)
            dt_s[rows_of(t), cols] = dq.astype(BF16)

    each(0, snaps, unroll, scores)
    dt_s[:, width : 2 * width] = dk_s[...].astype(BF16)
    dt_s[:, 2 * width :] = dv_s[...].astype(BF16)
    share = width // snaps
    pick = (
        lax.broadcasted_iota(jnp.int32, (width, share), 0)
        == lax.broadcasted_iota(jnp.int32, (width, share), 1) + me * share
    )
    z_mine = dot_nn(z_s[...], jnp.where(pick, 1.0, 0.0).astype(BF16)).astype(BF16)
    for part in range(3):
        cols = slice(part * width, (part + 1) * width)
        terms_ref[:, cols] = dot_tn(z_mine, dt_s[:, cols]).astype(BF16)
    dt_own_ref[...] = dt_s[rows_of(me), :]
    cot_own_ref[...] = ct_s[rows_of(me), :].astype(BF16)


def backward_kernel(
    heads, bias_ref, halo_hbm, proj_hbm, count_hbm, ws_hbm, wt_hbm, dt_hbm, cot_hbm, back_ref, part_ref,
    halo, proj, count, ws, wt, dt, cot, tab_s, dq_s, dtab_s, sems,
):
    rows, width = cot.shape
    halo_rows = halo.shape[0]
    keys = tab_s.shape[0]
    head_dim = width // heads
    group = LANES // head_dim
    scale = head_dim ** (-0.5)
    fetch = Fetch(
        sems,
        (halo_hbm, halo),
        (ws_hbm, ws),
        (proj_hbm, proj),
        (count_hbm, count),
        (dt_hbm, dt),
        (cot_hbm, cot),
        (wt_hbm, wt),
    )
    fetch.wait(*range(7))
    fill_table(tab_s, proj, halo, ws.at[:, width:])
    dh = cot[...].astype(F32) + dot_nt(dt[...], wt[...])
    part_ref[...] = dh.astype(BF16).astype(F32)
    for p in range(width // LANES):
        cols = slice(p * LANES, (p + 1) * LANES)
        vcols = slice(width + p * LANES, width + (p + 1) * LANES)
        kk, attn = edge_attention(p, heads, proj, count, bias_ref, tab_s, width)
        vv = stack_heads(tab_s[:, vcols], head_dim)
        attn_b = jnp.concatenate([a.astype(BF16) for a in attn], axis=1)
        agg = dot_nn(attn_b, vv)
        da = part_ref[:, cols] * jnp.where(agg > 0, 1.0, jnp.exp(jnp.minimum(agg, 0.0)))
        da = da.astype(BF16)
        dattn = dot_nt(da, vv).astype(BF16).astype(F32)
        ds = []
        for g in range(group):
            ad = attn[g] * dattn[:, g * keys : (g + 1) * keys]
            ds.append((ad - attn[g] * jnp.sum(ad, axis=1, keepdims=True)).astype(BF16))
        ds = jnp.concatenate(ds, axis=1)
        dq_s[:, cols] = (dot_nn(ds, kk) * scale).astype(BF16)
        dtab_s[:, cols] = (unstack_heads(dot_tn(ds, proj[:, cols]), head_dim) * scale).astype(BF16)
        dtab_s[:, vcols] = unstack_heads(dot_tn(attn_b, da), head_dim).astype(BF16)
    back_ref[...] = dot_nt(dtab_s[rows : rows + halo_rows, :], ws[:, width:])
    part_ref[...] += dot_nt(dq_s[...], ws[:, :width]) + dot_nt(dtab_s[:rows, :], ws[:, width:])


def sum_kernel(parts_ref, back_ref, out_ref):
    doms, rows, wide = parts_ref.shape
    per = back_ref.shape[0] // doms
    half = back_ref.shape[1] * per // rows
    total = parts_ref[0].astype(F32)
    for d in range(1, doms):
        total = total + parts_ref[d].astype(F32)
    total = total.astype(BF16)
    for d in range(doms):
        out_ref[d, :, :wide] = total
        tile = back_ref[d * per : (d + 1) * per, :]
        folded = [tile[:, i * half : (i + 1) * half] for i in range(rows // per)]
        out_ref[d, :, wide:] = jnp.concatenate(folded, axis=0).astype(BF16)


def last_kernel(route_ref, got_ref, part_ref, feat_ref, wtemp_ref, came_s):
    doms, rows, wide = got_ref.shape
    per = came_s.shape[0] // doms
    half = came_s.shape[1] * per // rows
    wide -= half
    for d in range(doms):
        wtemp_ref[d * rows : (d + 1) * rows, :] = got_ref[d, :, :wide].astype(F32)
        folded = got_ref[d, :, wide:].astype(F32)
        for i in range(rows // per):
            came_s[d * per : (d + 1) * per, i * half : (i + 1) * half] = folded[
                i * per : (i + 1) * per
            ]
    picks = pick_rows(route_ref, part_ref.shape[0])
    back = dot_tn(picks, came_s[...].astype(BF16))
    feat_ref[...] = (part_ref[...] + back).astype(BF16)


def params(mib):
    return pltpu.CompilerParams(vmem_limit_bytes=mib * 1024 * 1024)


def gather_blocks(block, axis):
    count = lax.axis_size(axis)
    held = {0: block}
    bit = count // 2
    while bit:
        for m in sorted(held):
            pairs = [(i, i ^ bit) for i in range(count)]
            held[m ^ bit] = lax.ppermute(held[m], axis, pairs)
        bit //= 2
    return [held[m] for m in range(count)]


def exchange(tiles, axis):
    return lax.all_to_all(tiles, axis, split_axis=0, concat_axis=0, tiled=True)


def per_device(
    feat, w_struct, w_temp, pos_embed, rel_bias, nbr, rel_type, send_idx, active, cotangent
):
    x = feat[0]
    local, width = x.shape
    kinds, heads = rel_bias.shape
    slots = nbr.shape[2]
    doms = lax.axis_size("dom")
    snaps = lax.axis_size("snap")
    ents = local // snaps
    route = send_idx[0, 0]
    halo_per = route.shape[1]
    halo_rows = doms * halo_per
    keys = -(-(local + halo_rows) // LANES) * LANES
    share = width // snaps
    piece = share // doms
    me = lax.axis_index("snap").astype(jnp.int32).reshape(1)

    def shape(*dims, dtype=BF16):
        return jax.ShapeDtypeStruct(dims, dtype)

    tiles = pl.pallas_call(
        tiles_kernel,
        out_shape=shape(halo_rows, width),
        in_specs=[SMEM, VMEM],
        out_specs=VMEM,
        compiler_params=params(8),
        name="halo_tiles",
    )(route, x)
    halo = exchange(tiles.reshape(doms, halo_per, width), "dom").reshape(halo_rows, width)

    proj, count, load = pl.pallas_call(
        own_kernel,
        out_shape=(
            shape(local, 3 * width),
            shape(kinds, local, keys),
            shape(snaps + 1, ents, width),
        ),
        in_specs=[VMEM, ANY, VMEM, VMEM, VMEM, VMEM],
        out_specs=(VMEM,) * 3,
        scratch_shapes=[pltpu.VMEM(w_struct.shape, BF16), pltpu.SemaphoreType.DMA((1,))],
        compiler_params=params(16),
        cost_estimate=pl.CostEstimate(flops=10**9, bytes_accessed=4 * 10**6, transcendentals=0),
        name="own_rows",
    )(x, w_struct, nbr[0].T, rel_type[0].T, active, cotangent)
    cots = gather_blocks(load, "snap")

    hidden = pl.pallas_call(
        functools.partial(forward_kernel, heads),
        out_shape=shape(local, width),
        in_specs=[VMEM, VMEM] + [ANY] * 4,
        out_specs=VMEM,
        scratch_shapes=[
            pltpu.VMEM((halo_rows, width), BF16),
            pltpu.VMEM((local, 3 * width), BF16),
            pltpu.VMEM((kinds, local, keys), BF16),
            pltpu.VMEM((width, 2 * width), BF16),
            pltpu.VMEM((keys, 2 * width), BF16),
            pltpu.SemaphoreType.DMA((4,)),
        ],
        compiler_params=params(16),
        name="struct_forward",
    )(x, rel_bias, halo, proj, count, w_struct)

    hids = gather_blocks(hidden, "snap")
    every = snaps * local
    terms, dt_own, cot_own = pl.pallas_call(
        functools.partial(temporal_kernel, snaps, heads),
        out_shape=(shape(share, 3 * width), shape(local, 3 * width), shape(local, width)),
        in_specs=[SMEM, VMEM] + [ANY] * (1 + 2 * snaps),
        out_specs=(VMEM,) * 3,
        scratch_shapes=[
            pltpu.VMEM(w_temp.shape, BF16),
            pltpu.VMEM((snaps, local, width), BF16),
            pltpu.VMEM((snaps, snaps + 1, ents, width), BF16),
            pltpu.VMEM((every, width), BF16),
            pltpu.VMEM((every, width), F32 if ents % 16 else BF16),
            pltpu.VMEM((every, 3 * width), BF16),
            pltpu.VMEM((every, 3 * width), BF16),
            pltpu.VMEM((local, LANES), F32),
            pltpu.VMEM((snaps, local, LANES), F32),
            pltpu.VMEM((snaps, local, LANES), F32),
            pltpu.VMEM((snaps, local, LANES), BF16),
            pltpu.VMEM((snaps, local, LANES), BF16),
            pltpu.VMEM((every, width), F32),
            pltpu.VMEM((every, width), F32),
            pltpu.SemaphoreType.DMA((2 * snaps + 1,)),
        ],
        compiler_params=params(24 if snaps <= 4 else 56),
        name="temporal",
    )(me, pos_embed, w_temp, *hids, *cots)

    parts = exchange(terms.reshape(doms, piece, 3 * width), "dom")
    back, partial = pl.pallas_call(
        functools.partial(backward_kernel, heads),
        out_shape=(shape(halo_rows, width, dtype=F32), shape(local, width, dtype=F32)),
        in_specs=[VMEM] + [ANY] * 7,
        out_specs=(VMEM, VMEM),
        scratch_shapes=[
            pltpu.VMEM((halo_rows, width), BF16),
            pltpu.VMEM((local, 3 * width), BF16),
            pltpu.VMEM((kinds, local, keys), BF16),
            pltpu.VMEM(w_struct.shape, BF16),
            pltpu.VMEM(w_temp.shape, BF16),
            pltpu.VMEM((local, 3 * width), BF16),
            pltpu.VMEM((local, width), BF16),
            pltpu.VMEM((keys, 2 * width), BF16),
            pltpu.VMEM((local, width), BF16),
            pltpu.VMEM((keys, 2 * width), BF16),
            pltpu.SemaphoreType.DMA((7,)),
        ],
        compiler_params=params(24),
        cost_estimate=pl.CostEstimate(flops=2 * 10**9, bytes_accessed=8 * 10**6, transcendentals=0),
        name="struct_backward",
    )(rel_bias, halo, proj, count, w_struct, w_temp, dt_own, cot_own)

    if piece % 16 == 0 and (halo_per * width) % (piece * LANES) == 0:
        side = halo_per * width // piece
        mixed = pl.pallas_call(
            sum_kernel,
            out_shape=shape(doms, piece, 3 * width + side),
            in_specs=[VMEM, VMEM],
            out_specs=VMEM,
            compiler_params=params(8),
            name="sum_parts",
        )(parts, back)
        got = exchange(mixed, "dom")
        grad_feat, grad_wtemp = pl.pallas_call(
            last_kernel,
            out_shape=(shape(local, width), shape(share, 3 * width, dtype=F32)),
            in_specs=[SMEM, VMEM, VMEM],
            out_specs=(VMEM, VMEM),
            scratch_shapes=[pltpu.VMEM((halo_rows, width), F32)],
            compiler_params=params(8),
            name="last_sums",
        )(route, got, partial)
        return (grad_feat[None], grad_wtemp)
    total = jnp.sum(parts.astype(F32), axis=0).astype(BF16)
    got = exchange(jnp.broadcast_to(total[None], (doms,) + total.shape), "dom")
    grad_wtemp = got.astype(F32).reshape(share, 3 * width)
    came = exchange(back.astype(BF16).reshape(doms, halo_per, width), "dom")
    picks = (route.reshape(-1)[:, None] == jnp.arange(local, dtype=jnp.int32)).astype(BF16)
    sums = dot_tn(picks, came.reshape(halo_rows, width))
    return ((partial + sums).astype(BF16)[None], grad_wtemp)


def solution(mesh):
    return jax.shard_map(
        per_device,
        mesh=mesh,
        in_specs=(
            P("snap", "dom", None),
            P(),
            P(),
            P(),
            P(),
            P("snap", "dom", None),
            P("snap", "dom", None),
            P("snap", "dom", None, None),
            P(None, ("dom", "snap")),
            P(None, ("dom", "snap"), None),
        ),
        out_specs=(P("snap", "dom", None), P("snap", None)),
        check_vma=False,
    )
```

```python
import functools

import jax
import jax.numpy as jnp
from jax import lax
from jax.experimental import pallas as pl
from jax.experimental.pallas import tpu as pltpu
from jax.sharding import PartitionSpec as P

F32 = jnp.float32
BF16 = jnp.bfloat16
LANES = 128
NEG = -1e30
VMEM = pl.BlockSpec(memory_space=pltpu.VMEM)
SMEM = pl.BlockSpec(memory_space=pltpu.SMEM)
HBM = pl.BlockSpec(memory_space=pltpu.HBM)


def dot_nn(a, b):
    return lax.dot_general(a, b, (((1,), (0,)), ((), ())), preferred_element_type=F32)


def dot_nt(a, b):
    return lax.dot_general(a, b, (((1,), (1,)), ((), ())), preferred_element_type=F32)


def dot_tn(a, b):
    return lax.dot_general(a, b, (((0,), (0,)), ((), ())), preferred_element_type=F32)


def stack_heads(block, head_dim):
    rows, lanes = block.shape
    head = lax.broadcasted_iota(jnp.int32, (rows, lanes), 1) // head_dim
    zero = jnp.zeros_like(block)
    return jnp.concatenate(
        [jnp.where(head == g, block, zero) for g in range(lanes // head_dim)], axis=0
    )


def unstack_heads(stacked, head_dim):
    lanes = stacked.shape[1]
    groups = lanes // head_dim
    rows = stacked.shape[0] // groups
    head = lax.broadcasted_iota(jnp.int32, (rows, lanes), 1) // head_dim
    out = stacked[:rows]
    for g in range(1, groups):
        out = jnp.where(head == g, stacked[g * rows : (g + 1) * rows], out)
    return out


class Fetch:

    def __init__(self, sems, *pairs):
        self.copies = [
            pltpu.make_async_copy(src, dst, sems.at[i]) for i, (src, dst) in enumerate(pairs)
        ]
        for copy in self.copies:
            copy.start()

    def wait(self, *which):
        for i in which:
            self.copies[i].wait()


def pick_rows(route_ref, local):
    doms, per = route_ref.shape
    lane = lax.broadcasted_iota(jnp.int32, (per, local), 1)
    sub = lax.broadcasted_iota(jnp.int32, (per, local), 0)
    tiles = []
    for r in range(doms):
        spot = jnp.zeros((per, local), jnp.int32)
        for j in range(per):
            spot = jnp.where(sub == j, route_ref[r, j], spot)
        tiles.append(jnp.where(lane == spot, 1.0, 0.0))
    return jnp.concatenate(tiles, axis=0).astype(BF16)


def tiles_kernel(route_hbm, x_hbm, out_ref, route, x, sems):
    fetch = Fetch(sems, (route_hbm, route), (x_hbm, x))
    fetch.wait(0, 1)
    out_ref[...] = dot_nn(pick_rows(route, x.shape[0]), x[...]).astype(BF16)


def own_kernel(
    x_hbm, w_hbm, nbr_hbm, rel_hbm, act_hbm, cot_hbm, proj_hbm, count_hbm, load_hbm,
    x, w, nbr, rel, act, proj, count, flags_s, sems,
):
    rows, width = x.shape
    kinds, _, keys = count.shape
    slots = nbr.shape[0]
    snaps, ents = act.shape
    fetch = Fetch(
        sems,
        (nbr_hbm, nbr),
        (rel_hbm, rel),
        (act_hbm, act),
        (cot_hbm, load_hbm.at[:snaps]),
        (x_hbm, x),
        (w_hbm, w),
    )
    row = lax.broadcasted_iota(jnp.int32, (ents, ents), 0)
    col = lax.broadcasted_iota(jnp.int32, (ents, ents), 1)
    lane = lax.broadcasted_iota(jnp.int32, (ents, width), 1)
    flags = jnp.zeros((ents, width), F32)
    fetch.wait(0, 1, 2)
    on = act[...].astype(F32)
    for t in range(snaps):
        column = jnp.sum(jnp.where(row == col, on[t : t + 1, :], 0.0), axis=1, keepdims=True)
        flags = jnp.where(lane == t, column, flags)
    flags_s[...] = flags.astype(BF16)
    code = jnp.transpose((nbr[...] * kinds + rel[...]).astype(F32))
    spot = (lax.broadcasted_iota(jnp.int32, (rows, keys), 1) * kinds).astype(F32)
    for r in range(kinds):
        here = spot + float(r)
        total = jnp.zeros((rows, keys), F32)
        for k in range(slots):
            total = total + jnp.where(code[:, k : k + 1] == here, 1.0, 0.0)
        count[r] = total.astype(BF16)
    store = Fetch(sems.at[6:], (flags_s, load_hbm.at[snaps]), (count, count_hbm))
    fetch.wait(4, 5)
    for part in range(3):
        cols = slice(part * width, (part + 1) * width)
        proj[:, cols] = dot_nn(x[...], w[:, cols]).astype(BF16)
    last = Fetch(sems.at[8:], (proj, proj_hbm))
    fetch.wait(3)
    store.wait(0, 1)
    last.wait(0)


def fill_table(tab_s, proj, halo, w_kv):
    rows, width = proj.shape[0], halo.shape[1]
    used = rows + halo.shape[0]
    tab_s[:rows, :] = proj[:, width:]
    for part in range(2):
        cols = slice(part * width, (part + 1) * width)
        tab_s[rows:used, cols] = dot_nn(halo[...], w_kv[:, cols]).astype(BF16)
    if tab_s.shape[0] > used:
        tab_s[used:, :] = jnp.zeros((tab_s.shape[0] - used, 2 * width), BF16)


def edge_attention(p, heads, proj, count, bias, tab_s, width):
    keys = tab_s.shape[0]
    head_dim = width // heads
    group = LANES // head_dim
    cols = slice(p * LANES, (p + 1) * LANES)
    kk = stack_heads(tab_s[:, cols], head_dim)
    score = dot_nt(proj[:, cols], kk) * head_dim ** (-0.5)
    gain = jnp.exp(bias[...])
    parts = []
    for g in range(group):
        h = p * group + g
        wt = count[0].astype(F32) * gain[0:1, h : h + 1]
        for r in range(1, count.shape[0]):
            wt = wt + count[r].astype(F32) * gain[r : r + 1, h : h + 1]
        s = jnp.where(wt > 0, score[:, g * keys : (g + 1) * keys], NEG)
        e = jnp.exp(s - jnp.max(s, axis=1, keepdims=True)) * wt
        parts.append(e * (1.0 / jnp.sum(e, axis=1, keepdims=True)))
    return kk, parts


def forward_kernel(heads, x, bias, halo, w, count_hbm, hidden_ref, count, proj, tab_s, sems):
    width = x.shape[1]
    head_dim = width // heads
    fetch = Fetch(sems, (count_hbm, count))
    for part in range(3):
        cols = slice(part * width, (part + 1) * width)
        proj[:, cols] = dot_nn(x[...], w[:, cols]).astype(BF16)
    fill_table(tab_s, proj, halo, w.at[:, width:])
    fetch.wait(0)
    for p in range(width // LANES):
        cols = slice(p * LANES, (p + 1) * LANES)
        vcols = slice(width + p * LANES, width + (p + 1) * LANES)
        _, attn = edge_attention(p, heads, proj, count, bias, tab_s, width)
        vv = stack_heads(tab_s[:, vcols], head_dim)
        agg = dot_nn(jnp.concatenate([a.astype(BF16) for a in attn], axis=1), vv)
        elu = jnp.where(agg > 0, agg, jnp.exp(jnp.minimum(agg, 0.0)) - 1.0)
        hidden_ref[:, cols] = (x[:, cols].astype(F32) + elu).astype(BF16)


def each(lo, hi, unroll, body):
    if unroll:
        for i in range(lo, hi):
            body(i)
    else:
        lax.fori_loop(lo, hi, lambda i, c: (body(i), c)[1], 0)


def temporal_kernel(snaps, heads, me_ref, pos_ref, w_s, *refs):
    hid = refs[:snaps]
    cot = refs[snaps : 2 * snaps]
    (
        terms_hbm, dt_own_hbm, cot_own_hbm,
        terms_s, own_s, z_s, ct_s, tp_s, dt_s, act_s, s_s, d_s, a_s, ds_s, dk_s, dv_s, sems,
    ) = refs[2 * snaps :]
    local, width = hid[0].shape
    ents = cot[0].shape[1]
    head_dim = width // heads
    scale = head_dim ** (-0.5)
    unroll = snaps <= 4
    me = me_ref[0]
    pos = pos_ref[...].astype(F32)
    which = lax.broadcasted_iota(jnp.int32, pos.shape, 0)

    def rows_of(t):
        return pl.ds(t * local if isinstance(t, int) else pl.multiple_of(t * local, local), local)

    for n in range(snaps):
        t = lax.bitwise_xor(me, n)
        shift = jnp.sum(jnp.where(which == t, pos, 0.0), axis=0, keepdims=True)
        z_s[rows_of(t), :] = (hid[n][...].astype(F32) + shift).astype(BF16)
    for part in range(3):
        cols = slice(part * width, (part + 1) * width)
        tp_s[:, cols] = dot_nn(z_s[...], w_s[:, cols]).astype(BF16)
    for m in range(snaps):
        at = pl.multiple_of(lax.bitwise_xor(me, m) * ents, ents)
        for t in range(snaps):
            ct_s[pl.ds(t * local + at, ents), :] = cot[m][t].astype(ct_s.dtype)
        act_s[pl.ds(at, ents), :] = cot[m][snaps][:, :LANES].astype(F32)
    lane_head = lax.broadcasted_iota(jnp.int32, (width, LANES), 0) // head_dim
    fold = (lane_head == lax.broadcasted_iota(jnp.int32, (width, LANES), 1)).astype(F32).astype(BF16)
    head_lane = lax.broadcasted_iota(jnp.int32, (LANES, width), 1) // head_dim
    spread = (head_lane == lax.broadcasted_iota(jnp.int32, (LANES, width), 0)).astype(F32).astype(BF16)
    spread_scaled = (spread.astype(F32) * scale).astype(BF16)
    act = act_s[...]
    snap_lane = lax.broadcasted_iota(jnp.int32, act.shape, 1)
    dk_s[...] = jnp.zeros_like(dk_s)
    dv_s[...] = jnp.zeros_like(dv_s)

    def scores(t):
        def pair(u):
            q, k, v = (
                tp_s[rows_of(i), part * width : (part + 1) * width]
                for part, i in ((0, t), (1, u), (2, u))
            )
            s = dot_nn(q * k, fold) * scale
            on = jnp.sum(jnp.where(snap_lane == u, act, 0.0), axis=1, keepdims=True)
            s_s[u] = jnp.where((on > 0.5) | (u == t), s, NEG)
            d = dot_nn(ct_s[rows_of(t), :].astype(BF16) * v, fold)
            d_s[u] = d.astype(BF16).astype(F32)

        each(0, t + 1, unroll, pair)
        top = s_s[0]
        if unroll:
            for u in range(1, t + 1):
                top = jnp.maximum(top, s_s[u])
        else:
            top = lax.fori_loop(1, t + 1, lambda u, c: jnp.maximum(c, s_s[u]), top)
        zero = jnp.zeros_like(top)

        def expo(u, total):
            e = jnp.exp(s_s[u] - top)
            s_s[u] = e
            return total + e

        total = zero
        if unroll:
            for u in range(t + 1):
                total = expo(u, total)
        else:
            total = lax.fori_loop(0, t + 1, expo, total)
        inv = 1.0 / total

        def weigh(u, dot):
            a = s_s[u] * inv
            s_s[u] = a
            return dot + a * d_s[u]

        dot = zero
        if unroll:
            for u in range(t + 1):
                dot = weigh(u, dot)
        else:
            dot = lax.fori_loop(0, t + 1, weigh, dot)

        def keep(u):
            a = s_s[u]
            a_s[u] = a.astype(BF16)
            ds_s[u] = (a * (d_s[u] - dot)).astype(BF16)

        each(0, t + 1, unroll, keep)

        for p in range(width // LANES):
            c0 = p * LANES
            cols = slice(c0, c0 + LANES)
            q = tp_s[rows_of(t), cols].astype(F32)
            ct = ct_s[rows_of(t), cols].astype(F32)

            def back(u, dq):
                k = tp_s[rows_of(u), width + c0 : width + c0 + LANES].astype(F32)
                wide_ds = dot_nn(ds_s[u], spread_scaled[:, cols])
                wide_a = dot_nn(a_s[u], spread[:, cols])
                dk_s[rows_of(u), cols] += wide_ds * q
                dv_s[rows_of(u), cols] += wide_a * ct
                return dq + wide_ds * k

            dq = jnp.zeros_like(q)
            if unroll:
                for u in range(t + 1):
                    dq = back(u, dq)
            else:
                dq = lax.fori_loop(0, t + 1, back, dq)
            dt_s[rows_of(t), cols] = dq.astype(BF16)

    each(0, snaps, unroll, scores)
    dt_s[:, width : 2 * width] = dk_s[...].astype(BF16)
    dt_s[:, 2 * width :] = dv_s[...].astype(BF16)
    own_s[...] = ct_s[rows_of(me), :].astype(BF16)
    store = Fetch(
        sems, (dt_s.at[rows_of(me), :], dt_own_hbm), (own_s, cot_own_hbm)
    )
    share = width // snaps
    pick = (
        lax.broadcasted_iota(jnp.int32, (width, share), 0)
        == lax.broadcasted_iota(jnp.int32, (width, share), 1) + me * share
    )
    z_mine = dot_nn(z_s[...], jnp.where(pick, 1.0, 0.0).astype(BF16)).astype(BF16)
    for part in range(3):
        cols = slice(part * width, (part + 1) * width)
        terms_s[:, cols] = dot_tn(z_mine, dt_s[:, cols]).astype(BF16)
    last = Fetch(sems.at[2:], (terms_s, terms_hbm))
    store.wait(0, 1)
    last.wait(0)


def backward_kernel(
    heads, bias_hbm, halo_hbm, proj_hbm, count_hbm, ws_hbm, wt_hbm, dt_hbm, cot_hbm, back_hbm, part_hbm,
    bias, back_s, part_s, halo, proj, count, ws, wt, dt, cot, tab_s, dq_s, dtab_s, sems,
):
    rows, width = cot.shape
    halo_rows = halo.shape[0]
    keys = tab_s.shape[0]
    head_dim = width // heads
    group = LANES // head_dim
    scale = head_dim ** (-0.5)
    fetch = Fetch(
        sems,
        (halo_hbm, halo),
        (ws_hbm, ws),
        (proj_hbm, proj),
        (count_hbm, count),
        (dt_hbm, dt),
        (cot_hbm, cot),
        (wt_hbm, wt),
        (bias_hbm, bias),
    )
    fetch.wait(*range(8))
    fill_table(tab_s, proj, halo, ws.at[:, width:])
    dh = cot[...].astype(F32) + dot_nt(dt[...], wt[...])
    part_s[...] = dh.astype(BF16).astype(F32)
    for p in range(width // LANES):
        cols = slice(p * LANES, (p + 1) * LANES)
        vcols = slice(width + p * LANES, width + (p + 1) * LANES)
        kk, attn = edge_attention(p, heads, proj, count, bias, tab_s, width)
        vv = stack_heads(tab_s[:, vcols], head_dim)
        attn_b = jnp.concatenate([a.astype(BF16) for a in attn], axis=1)
        agg = dot_nn(attn_b, vv)
        da = part_s[:, cols] * jnp.where(agg > 0, 1.0, jnp.exp(jnp.minimum(agg, 0.0)))
        da = da.astype(BF16)
        dattn = dot_nt(da, vv).astype(BF16).astype(F32)
        ds = []
        for g in range(group):
            ad = attn[g] * dattn[:, g * keys : (g + 1) * keys]
            ds.append((ad - attn[g] * jnp.sum(ad, axis=1, keepdims=True)).astype(BF16))
        ds = jnp.concatenate(ds, axis=1)
        dq_s[:, cols] = (dot_nn(ds, kk) * scale).astype(BF16)
        dtab_s[:, cols] = (unstack_heads(dot_tn(ds, proj[:, cols]), head_dim) * scale).astype(BF16)
        dtab_s[:, vcols] = unstack_heads(dot_tn(attn_b, da), head_dim).astype(BF16)
    back_s[...] = dot_nt(dtab_s[rows : rows + halo_rows, :], ws[:, width:])
    first = Fetch(sems.at[8:], (back_s, back_hbm))
    part_s[...] += dot_nt(dq_s[...], ws[:, :width]) + dot_nt(dtab_s[:rows, :], ws[:, width:])
    last = Fetch(sems.at[9:], (part_s, part_hbm))
    first.wait(0)
    last.wait(0)


def sum_kernel(parts_ref, back_hbm, out_ref, back_ref, sems):
    fetch = Fetch(sems, (back_hbm, back_ref))
    doms, rows, wide = parts_ref.shape
    per = back_ref.shape[0] // doms
    half = back_ref.shape[1] * per // rows
    total = parts_ref[0].astype(F32)
    for d in range(1, doms):
        total = total + parts_ref[d].astype(F32)
    total = total.astype(BF16)
    fetch.wait(0)
    for d in range(doms):
        out_ref[d, :, :wide] = total
        tile = back_ref[d * per : (d + 1) * per, :]
        folded = [tile[:, i * half : (i + 1) * half] for i in range(rows // per)]
        out_ref[d, :, wide:] = jnp.concatenate(folded, axis=0).astype(BF16)


def last_kernel(
    route_hbm, got_ref, part_hbm, feat_hbm, wtemp_hbm, route, part, feat, wtemp, came_s, sems
):
    fetch = Fetch(sems, (route_hbm, route), (part_hbm, part))
    doms, rows, wide = got_ref.shape
    per = came_s.shape[0] // doms
    half = came_s.shape[1] * per // rows
    wide -= half
    for d in range(doms):
        wtemp[d * rows : (d + 1) * rows, :] = got_ref[d, :, :wide].astype(F32)
        folded = got_ref[d, :, wide:].astype(F32)
        for i in range(rows // per):
            came_s[d * per : (d + 1) * per, i * half : (i + 1) * half] = folded[
                i * per : (i + 1) * per
            ]
    first = Fetch(sems.at[2:], (wtemp, wtemp_hbm))
    fetch.wait(0, 1)
    picks = pick_rows(route, part.shape[0])
    back = dot_tn(picks, came_s[...].astype(BF16))
    feat[...] = (part[...] + back).astype(BF16)
    last = Fetch(sems.at[3:], (feat, feat_hbm))
    first.wait(0)
    last.wait(0)


def params(mib):
    return pltpu.CompilerParams(vmem_limit_bytes=mib * 1024 * 1024)


def gather_blocks(block, axis):
    count = lax.axis_size(axis)
    held = {0: block}
    bit = count // 2
    while bit:
        for m in sorted(held):
            pairs = [(i, i ^ bit) for i in range(count)]
            held[m ^ bit] = lax.ppermute(held[m], axis, pairs)
        bit //= 2
    return [held[m] for m in range(count)]


def in_hbm(*arrays):
    return [pltpu.with_memory_space_constraint(a, pltpu.HBM) for a in arrays]


def exchange(tiles, axis):
    return lax.all_to_all(tiles, axis, split_axis=0, concat_axis=0, tiled=True)


def per_device(
    feat, w_struct, w_temp, pos_embed, rel_bias, nbr, rel_type, send_idx, active, cotangent
):
    x = feat[0]
    local, width = x.shape
    kinds, heads = rel_bias.shape
    slots = nbr.shape[2]
    doms = lax.axis_size("dom")
    snaps = lax.axis_size("snap")
    ents = local // snaps
    route = send_idx[0, 0]
    halo_per = route.shape[1]
    halo_rows = doms * halo_per
    keys = -(-(local + halo_rows) // LANES) * LANES
    share = width // snaps
    piece = share // doms
    me = lax.axis_index("snap").astype(jnp.int32).reshape(1)

    def shape(*dims, dtype=BF16):
        return jax.ShapeDtypeStruct(dims, dtype)

    def hbm(*dims, dtype=BF16):
        return pltpu.HBM(dims, dtype)

    tiles = pl.pallas_call(
        tiles_kernel,
        out_shape=shape(halo_rows, width),
        in_specs=[HBM, HBM],
        out_specs=VMEM,
        scratch_shapes=[
            pltpu.SMEM(route.shape, jnp.int32),
            pltpu.VMEM((local, width), BF16),
            pltpu.SemaphoreType.DMA((2,)),
        ],
        compiler_params=params(8),
        name="halo_tiles",
    )(*in_hbm(route, x))
    halo = exchange(tiles.reshape(doms, halo_per, width), "dom").reshape(halo_rows, width)

    proj, count, load = pl.pallas_call(
        own_kernel,
        out_shape=(
            hbm(local, 3 * width),
            hbm(kinds, local, keys),
            hbm(snaps + 1, ents, width),
        ),
        in_specs=[HBM] * 6,
        out_specs=(HBM,) * 3,
        scratch_shapes=[
            pltpu.VMEM((local, width), BF16),
            pltpu.VMEM(w_struct.shape, BF16),
            pltpu.VMEM((slots, local), jnp.int32),
            pltpu.VMEM((slots, local), jnp.int32),
            pltpu.VMEM((snaps, ents), jnp.int32),
            pltpu.VMEM((local, 3 * width), BF16),
            pltpu.VMEM((kinds, local, keys), BF16),
            pltpu.VMEM((ents, width), BF16),
            pltpu.SemaphoreType.DMA((9,)),
        ],
        compiler_params=params(16),
        cost_estimate=pl.CostEstimate(flops=10**9, bytes_accessed=4 * 10**6, transcendentals=0),
        name="own_rows",
    )(*in_hbm(x, w_struct, nbr[0].T, rel_type[0].T, active, cotangent))
    cots = gather_blocks(load, "snap")

    hidden = pl.pallas_call(
        functools.partial(forward_kernel, heads),
        out_shape=shape(local, width),
        in_specs=[VMEM] * 4 + [HBM],
        out_specs=VMEM,
        scratch_shapes=[
            pltpu.VMEM((kinds, local, keys), BF16),
            pltpu.VMEM((local, 3 * width), BF16),
            pltpu.VMEM((keys, 2 * width), BF16),
            pltpu.SemaphoreType.DMA((1,)),
        ],
        compiler_params=params(8),
        name="struct_forward",
    )(x, rel_bias, halo, w_struct, *in_hbm(count))

    hids = gather_blocks(hidden, "snap")
    every = snaps * local
    terms, dt_own, cot_own = pl.pallas_call(
        functools.partial(temporal_kernel, snaps, heads),
        out_shape=(hbm(share, 3 * width), hbm(local, 3 * width), hbm(local, width)),
        in_specs=[SMEM] + [VMEM] * (2 + 2 * snaps),
        out_specs=(HBM,) * 3,
        scratch_shapes=[
            pltpu.VMEM((share, 3 * width), BF16),
            pltpu.VMEM((local, width), BF16),
            pltpu.VMEM((every, width), BF16),
            pltpu.VMEM((every, width), F32 if ents % 16 else BF16),
            pltpu.VMEM((every, 3 * width), BF16),
            pltpu.VMEM((every, 3 * width), BF16),
            pltpu.VMEM((local, LANES), F32),
            pltpu.VMEM((snaps, local, LANES), F32),
            pltpu.VMEM((snaps, local, LANES), F32),
            pltpu.VMEM((snaps, local, LANES), BF16),
            pltpu.VMEM((snaps, local, LANES), BF16),
            pltpu.VMEM((every, width), F32),
            pltpu.VMEM((every, width), F32),
            pltpu.SemaphoreType.DMA((3,)),
        ],
        compiler_params=params(24 if snaps <= 4 else 56),
        name="temporal",
    )(me, pos_embed, w_temp, *hids, *cots)

    parts = exchange(terms.reshape(doms, piece, 3 * width), "dom")
    back, partial = pl.pallas_call(
        functools.partial(backward_kernel, heads),
        out_shape=(hbm(halo_rows, width, dtype=F32), hbm(local, width, dtype=F32)),
        in_specs=[HBM] * 8,
        out_specs=(HBM, HBM),
        scratch_shapes=[
            pltpu.VMEM(rel_bias.shape, F32),
            pltpu.VMEM((halo_rows, width), F32),
            pltpu.VMEM((local, width), F32),
            pltpu.VMEM((halo_rows, width), BF16),
            pltpu.VMEM((local, 3 * width), BF16),
            pltpu.VMEM((kinds, local, keys), BF16),
            pltpu.VMEM(w_struct.shape, BF16),
            pltpu.VMEM(w_temp.shape, BF16),
            pltpu.VMEM((local, 3 * width), BF16),
            pltpu.VMEM((local, width), BF16),
            pltpu.VMEM((keys, 2 * width), BF16),
            pltpu.VMEM((local, width), BF16),
            pltpu.VMEM((keys, 2 * width), BF16),
            pltpu.SemaphoreType.DMA((10,)),
        ],
        compiler_params=params(24),
        cost_estimate=pl.CostEstimate(flops=2 * 10**9, bytes_accessed=8 * 10**6, transcendentals=0),
        name="struct_backward",
    )(*in_hbm(rel_bias, halo, proj, count, w_struct, w_temp, dt_own, cot_own))

    if piece % 16 == 0 and (halo_per * width) % (piece * LANES) == 0:
        side = halo_per * width // piece
        mixed = pl.pallas_call(
            sum_kernel,
            out_shape=shape(doms, piece, 3 * width + side),
            in_specs=[VMEM, HBM],
            out_specs=VMEM,
            scratch_shapes=[
                pltpu.VMEM((halo_rows, width), F32),
                pltpu.SemaphoreType.DMA((1,)),
            ],
            compiler_params=params(8),
            name="sum_parts",
        )(parts, *in_hbm(back))
        got = exchange(mixed, "dom")
        grad_feat, grad_wtemp = pl.pallas_call(
            last_kernel,
            out_shape=(hbm(local, width), hbm(share, 3 * width, dtype=F32)),
            in_specs=[HBM, VMEM, HBM],
            out_specs=(HBM, HBM),
            scratch_shapes=[
                pltpu.SMEM(route.shape, jnp.int32),
                pltpu.VMEM((local, width), F32),
                pltpu.VMEM((local, width), BF16),
                pltpu.VMEM((share, 3 * width), F32),
                pltpu.VMEM((halo_rows, width), F32),
                pltpu.SemaphoreType.DMA((4,)),
            ],
            compiler_params=params(8),
            name="last_sums",
        )(*in_hbm(route), got, *in_hbm(partial))
        return (grad_feat[None], grad_wtemp)
    total = jnp.sum(parts.astype(F32), axis=0).astype(BF16)
    got = exchange(jnp.broadcast_to(total[None], (doms,) + total.shape), "dom")
    grad_wtemp = got.astype(F32).reshape(share, 3 * width)
    came = exchange(back.astype(BF16).reshape(doms, halo_per, width), "dom")
    picks = (route.reshape(-1)[:, None] == jnp.arange(local, dtype=jnp.int32)).astype(BF16)
    sums = dot_tn(picks, came.reshape(halo_rows, width))
    return ((partial + sums).astype(BF16)[None], grad_wtemp)


def solution(mesh):
    return jax.shard_map(
        per_device,
        mesh=mesh,
        in_specs=(
            P("snap", "dom", None),
            P(),
            P(),
            P(),
            P(),
            P("snap", "dom", None),
            P("snap", "dom", None),
            P("snap", "dom", None, None),
            P(None, ("dom", "snap")),
            P(None, ("dom", "snap"), None),
        ),
        out_specs=(P("snap", "dom", None), P("snap", None)),
        check_vma=False,
    )
```

```python
import functools

import jax
import jax.numpy as jnp
from jax import lax
from jax.experimental import pallas as pl
from jax.experimental.pallas import tpu as pltpu
from jax.sharding import PartitionSpec as P

F32 = jnp.float32
BF16 = jnp.bfloat16
LANES = 128
NEG = -1e30
VMEM = pl.BlockSpec(memory_space=pltpu.VMEM)
SMEM = pl.BlockSpec(memory_space=pltpu.SMEM)
HBM = pl.BlockSpec(memory_space=pltpu.HBM)


def dot_nn(a, b):
    return lax.dot_general(a, b, (((1,), (0,)), ((), ())), preferred_element_type=F32)


def dot_nt(a, b):
    return lax.dot_general(a, b, (((1,), (1,)), ((), ())), preferred_element_type=F32)


def dot_tn(a, b):
    return lax.dot_general(a, b, (((0,), (0,)), ((), ())), preferred_element_type=F32)


def stack_heads(block, head_dim):
    rows, lanes = block.shape
    head = lax.broadcasted_iota(jnp.int32, (rows, lanes), 1) // head_dim
    zero = jnp.zeros_like(block)
    return jnp.concatenate(
        [jnp.where(head == g, block, zero) for g in range(lanes // head_dim)], axis=0
    )


def unstack_heads(stacked, head_dim):
    lanes = stacked.shape[1]
    groups = lanes // head_dim
    rows = stacked.shape[0] // groups
    head = lax.broadcasted_iota(jnp.int32, (rows, lanes), 1) // head_dim
    out = stacked[:rows]
    for g in range(1, groups):
        out = jnp.where(head == g, stacked[g * rows : (g + 1) * rows], out)
    return out


class Fetch:

    def __init__(self, sems, *pairs):
        self.copies = [
            pltpu.make_async_copy(src, dst, sems.at[i]) for i, (src, dst) in enumerate(pairs)
        ]
        for copy in self.copies:
            copy.start()

    def wait(self, *which):
        for i in which:
            self.copies[i].wait()


def pick_rows(route_ref, local):
    doms, per = route_ref.shape
    lane = lax.broadcasted_iota(jnp.int32, (per, local), 1)
    sub = lax.broadcasted_iota(jnp.int32, (per, local), 0)
    tiles = []
    for r in range(doms):
        spot = jnp.zeros((per, local), jnp.int32)
        for j in range(per):
            spot = jnp.where(sub == j, route_ref[r, j], spot)
        tiles.append(jnp.where(lane == spot, 1.0, 0.0))
    return jnp.concatenate(tiles, axis=0).astype(BF16)


def tiles_kernel(route_hbm, x_hbm, out_ref, route, x, sems):
    fetch = Fetch(sems, (route_hbm, route), (x_hbm, x))
    fetch.wait(0, 1)
    out_ref[...] = dot_nn(pick_rows(route, x.shape[0]), x[...]).astype(BF16)


def own_kernel(
    nbr_hbm, rel_hbm, bias_hbm, act_hbm, cot_hbm, edge_hbm, load_ref,
    nbr, rel, bias, act, cot, edge, sems,
):
    heads, rows, keys = edge.shape
    kinds = bias.shape[0]
    slots = nbr.shape[0]
    snaps, ents, width = cot.shape
    fetch = Fetch(
        sems, (nbr_hbm, nbr), (rel_hbm, rel), (bias_hbm, bias), (act_hbm, act), (cot_hbm, cot)
    )
    row = lax.broadcasted_iota(jnp.int32, (ents, ents), 0)
    col = lax.broadcasted_iota(jnp.int32, (ents, ents), 1)
    lane = lax.broadcasted_iota(jnp.int32, (ents, width), 1)
    flags = jnp.zeros((ents, width), F32)
    fetch.wait(0, 1, 2, 3)
    on = act[...].astype(F32)
    for t in range(snaps):
        column = jnp.sum(jnp.where(row == col, on[t : t + 1, :], 0.0), axis=1, keepdims=True)
        flags = jnp.where(lane == t, column, flags)
    load_ref[snaps] = flags.astype(BF16)
    code = jnp.transpose((nbr[...] * kinds + rel[...]).astype(F32))
    spot = (lax.broadcasted_iota(jnp.int32, (rows, keys), 1) * kinds).astype(F32)
    counts = []
    for r in range(kinds):
        here = spot + float(r)
        total = jnp.zeros((rows, keys), F32)
        for k in range(slots):
            total = total + jnp.where(code[:, k : k + 1] == here, 1.0, 0.0)
        counts.append(total)
    gain = jnp.exp(bias[...])
    stores = []
    for h in range(heads):
        total = counts[0] * gain[0:1, h : h + 1]
        for r in range(1, kinds):
            total = total + counts[r] * gain[r : r + 1, h : h + 1]
        edge[h] = jnp.where(total > 0, jnp.log(total), NEG)
        stores.append(Fetch(sems.at[5 + h :], (edge.at[h], edge_hbm.at[h])))
    fetch.wait(4)
    for t in range(snaps):
        load_ref[t] = cot[t]
    for store in stores:
        store.wait(0)


def fill_table(tab_s, proj, halo, w_kv):
    rows, width = proj.shape[0], halo.shape[1]
    used = rows + halo.shape[0]
    tab_s[:rows, :] = proj[:, width:]
    for part in range(2):
        cols = slice(part * width, (part + 1) * width)
        tab_s[rows:used, cols] = dot_nn(halo[...], w_kv[:, cols]).astype(BF16)
    if tab_s.shape[0] > used:
        tab_s[used:, :] = jnp.zeros((tab_s.shape[0] - used, 2 * width), BF16)


def edge_attention(p, heads, proj, edge, tab_s, width):
    keys = tab_s.shape[0]
    head_dim = width // heads
    group = LANES // head_dim
    cols = slice(p * LANES, (p + 1) * LANES)
    kk = stack_heads(tab_s[:, cols], head_dim)
    score = dot_nt(proj[:, cols], kk)
    parts = []
    for g in range(group):
        s = score[:, g * keys : (g + 1) * keys] * head_dim ** (-0.5) + edge[p * group + g]
        e = jnp.exp(s - jnp.max(s, axis=1, keepdims=True))
        parts.append(e * (1.0 / jnp.sum(e, axis=1, keepdims=True)))
    return kk, parts


def forward_kernel(heads, x, halo, w, edge_hbm, hidden_ref, edge, proj, tab_s, sems):
    width = x.shape[1]
    head_dim = width // heads
    group = LANES // head_dim
    fetch = Fetch(sems, *[(edge_hbm.at[h], edge.at[h]) for h in range(heads)])
    for part in range(3):
        cols = slice(part * width, (part + 1) * width)
        proj[:, cols] = dot_nn(x[...], w[:, cols]).astype(BF16)
    fill_table(tab_s, proj, halo, w.at[:, width:])
    for p in range(width // LANES):
        cols = slice(p * LANES, (p + 1) * LANES)
        vcols = slice(width + p * LANES, width + (p + 1) * LANES)
        fetch.wait(*range(p * group, (p + 1) * group))
        _, attn = edge_attention(p, heads, proj, edge, tab_s, width)
        vv = stack_heads(tab_s[:, vcols], head_dim)
        agg = dot_nn(jnp.concatenate([a.astype(BF16) for a in attn], axis=1), vv)
        elu = jnp.where(agg > 0, agg, jnp.exp(jnp.minimum(agg, 0.0)) - 1.0)
        hidden_ref[:, cols] = (x[:, cols].astype(F32) + elu).astype(BF16)


def each(lo, hi, unroll, body):
    if unroll:
        for i in range(lo, hi):
            body(i)
    else:
        lax.fori_loop(lo, hi, lambda i, c: (body(i), c)[1], 0)


def temporal_kernel(snaps, heads, pieces, place_ref, pos_ref, w_s, *refs):
    hid = refs[:snaps]
    cot = refs[snaps : 2 * snaps]
    terms_ref = refs[2 * snaps : 2 * snaps + pieces]
    (
        dt_own_ref, cot_own_ref,
        z_s, ct_s, tp_s, dt_s, act_s, prod_s, s_s, d_s, a_s, ds_s, wa_s, wd_s, dk_s, dv_s, terms_s,
    ) = refs[2 * snaps + pieces :]
    local, width = hid[0].shape
    ents = cot[0].shape[1]
    head_dim = width // heads
    scale = head_dim ** (-0.5)
    unroll = snaps <= 4
    me, outer = place_ref[0], place_ref[1]
    pos = pos_ref[...].astype(F32)
    which = lax.broadcasted_iota(jnp.int32, pos.shape, 0)

    def rows_of(t):
        return pl.ds(t * local if isinstance(t, int) else pl.multiple_of(t * local, local), local)

    for n in range(snaps):
        t = lax.bitwise_xor(me, n)
        shift = jnp.sum(jnp.where(which == t, pos, 0.0), axis=0, keepdims=True)
        z_s[rows_of(t), :] = (hid[n][...].astype(F32) + shift).astype(BF16)
    for part in range(3):
        cols = slice(part * width, (part + 1) * width)
        tp_s[:, cols] = dot_nn(z_s[...], w_s[:, cols]).astype(BF16)
    for m in range(snaps):
        at = pl.multiple_of(lax.bitwise_xor(me, m) * ents, ents)
        for t in range(snaps):
            ct_s[pl.ds(t * local + at, ents), :] = cot[m][t].astype(ct_s.dtype)
        act_s[pl.ds(at, ents), :] = cot[m][snaps][:, :LANES].astype(F32)
    lane_head = lax.broadcasted_iota(jnp.int32, (width, LANES), 0) // head_dim
    fold = (lane_head == lax.broadcasted_iota(jnp.int32, (width, LANES), 1)).astype(F32)
    fold = fold.astype(BF16)
    head_lane = lax.broadcasted_iota(jnp.int32, (LANES, width), 1) // head_dim
    spread = (head_lane == lax.broadcasted_iota(jnp.int32, (LANES, width), 0)).astype(F32)
    spread_scaled = (spread * scale).astype(BF16)
    spread = spread.astype(BF16)
    act = act_s[...]
    snap_lane = lax.broadcasted_iota(jnp.int32, act.shape, 1)
    if not unroll:
        dk_s[...] = jnp.zeros_like(dk_s)
        dv_s[...] = jnp.zeros_like(dv_s)

    def one_snap(t):
        used = (t + 1 if unroll else snaps) * local
        half = snaps * local

        def product(u):
            q, k, v = (
                tp_s[rows_of(i), part * width : (part + 1) * width]
                for part, i in ((0, t), (1, u), (2, u))
            )
            prod_s[rows_of(u), :] = q * k
            prod_s[rows_of(snaps + u), :] = ct_s[rows_of(t), :].astype(BF16) * v

        each(0, t + 1, unroll, product)
        s_s[:used, :] = dot_nn(prod_s[:used, :], fold)
        d_s[:used, :] = dot_nn(prod_s[half : half + used, :], fold).astype(BF16).astype(F32)

        def mask(u):
            on = jnp.sum(jnp.where(snap_lane == u, act, 0.0), axis=1, keepdims=True)
            s_s[rows_of(u), :] = jnp.where((on > 0.5) | (u == t), s_s[rows_of(u), :] * scale, NEG)

        each(0, t + 1, unroll, mask)

        def reduced(fn, start):
            if unroll:
                for u in range(t + 1):
                    start = fn(u, start)
                return start
            return lax.fori_loop(0, t + 1, fn, start)

        top = reduced(
            lambda u, c: jnp.maximum(c, s_s[rows_of(u), :]), jnp.full((local, LANES), NEG, F32)
        )

        def expo(u, total):
            e = jnp.exp(s_s[rows_of(u), :] - top)
            s_s[rows_of(u), :] = e
            return total + e

        inv = 1.0 / reduced(expo, jnp.zeros((local, LANES), F32))

        def weigh(u, total):
            a = s_s[rows_of(u), :] * inv
            s_s[rows_of(u), :] = a
            return total + a * d_s[rows_of(u), :]

        dot = reduced(weigh, jnp.zeros((local, LANES), F32))

        def keep(u):
            a = s_s[rows_of(u), :]
            a_s[rows_of(u), :] = a.astype(BF16)
            ds_s[rows_of(u), :] = (a * (d_s[rows_of(u), :] - dot)).astype(BF16)

        each(0, t + 1, unroll, keep)
        wa_s[:used, :] = dot_nn(a_s[:used, :], spread)
        wd_s[:used, :] = dot_nn(ds_s[:used, :], spread_scaled)

        for p in range(width // LANES):
            c0 = p * LANES
            cols = slice(c0, c0 + LANES)
            q = tp_s[rows_of(t), cols].astype(F32)
            ct = ct_s[rows_of(t), cols].astype(F32)

            def back(u, dq):
                k = tp_s[rows_of(u), width + c0 : width + c0 + LANES].astype(F32)
                wide_ds = wd_s[rows_of(u), cols]
                dk, dv = wide_ds * q, wa_s[rows_of(u), cols] * ct
                if unroll and u == t:
                    dk_s[rows_of(u), cols] = dk
                    dv_s[rows_of(u), cols] = dv
                else:
                    dk_s[rows_of(u), cols] += dk
                    dv_s[rows_of(u), cols] += dv
                return dq + wide_ds * k

            dt_s[rows_of(t), cols] = reduced(back, jnp.zeros_like(q)).astype(BF16)

    each(0, snaps, unroll, one_snap)
    dt_s[:, width : 2 * width] = dk_s[...].astype(BF16)
    dt_s[:, 2 * width :] = dv_s[...].astype(BF16)
    share = width // snaps
    pick = (
        lax.broadcasted_iota(jnp.int32, (width, share), 0)
        == lax.broadcasted_iota(jnp.int32, (width, share), 1) + me * share
    )
    z_mine = dot_nn(z_s[...], pick.astype(F32).astype(BF16)).astype(BF16)
    for part in range(3):
        cols = slice(part * width, (part + 1) * width)
        terms_s[:, cols] = dot_tn(z_mine, dt_s[:, cols]).astype(BF16)
    piece = share // pieces
    for k in range(pieces):
        if pieces == 1:
            terms_ref[k][...] = terms_s[...]
        else:
            at = pl.multiple_of(lax.bitwise_xor(outer, k) * piece, piece)
            terms_ref[k][...] = terms_s[pl.ds(at, piece), :]
    dt_own_ref[...] = dt_s[rows_of(me), :]
    cot_own_ref[...] = ct_s[rows_of(me), :].astype(BF16)


def backward_kernel(
    heads, dt, cot, x_hbm, halo_hbm, edge_hbm, ws_hbm, wt_hbm, back_ref, part_ref,
    x, halo, edge, ws, wt, proj, tab_s, dq_s, dtab_s, sems,
):
    rows, width = cot.shape
    halo_rows = halo.shape[0]
    keys = tab_s.shape[0]
    head_dim = width // heads
    group = LANES // head_dim
    scale = head_dim ** (-0.5)
    fetch = Fetch(
        sems, (wt_hbm, wt), (x_hbm, x), (ws_hbm, ws), (halo_hbm, halo), (edge_hbm, edge)
    )
    fetch.wait(0)
    dh = cot[...].astype(F32) + dot_nt(dt[...], wt[...])
    part_ref[...] = dh.astype(BF16).astype(F32)
    fetch.wait(1, 2, 3)
    for part in range(3):
        cols = slice(part * width, (part + 1) * width)
        proj[:, cols] = dot_nn(x[...], ws[:, cols]).astype(BF16)
    fill_table(tab_s, proj, halo, ws.at[:, width:])
    fetch.wait(4)
    for p in range(width // LANES):
        cols = slice(p * LANES, (p + 1) * LANES)
        vcols = slice(width + p * LANES, width + (p + 1) * LANES)
        kk, attn = edge_attention(p, heads, proj, edge, tab_s, width)
        vv = stack_heads(tab_s[:, vcols], head_dim)
        attn_b = jnp.concatenate([a.astype(BF16) for a in attn], axis=1)
        agg = dot_nn(attn_b, vv)
        da = part_ref[:, cols] * jnp.where(agg > 0, 1.0, jnp.exp(jnp.minimum(agg, 0.0)))
        da = da.astype(BF16)
        dattn = dot_nt(da, vv).astype(BF16).astype(F32)
        ds = []
        for g in range(group):
            ad = attn[g] * dattn[:, g * keys : (g + 1) * keys]
            ds.append((ad - attn[g] * jnp.sum(ad, axis=1, keepdims=True)).astype(BF16))
        ds = jnp.concatenate(ds, axis=1)
        dq_s[:, cols] = (dot_nn(ds, kk) * scale).astype(BF16)
        dtab_s[:, cols] = (unstack_heads(dot_tn(ds, proj[:, cols]), head_dim) * scale).astype(BF16)
        dtab_s[:, vcols] = unstack_heads(dot_tn(attn_b, da), head_dim).astype(BF16)
    back_ref[...] = dot_nt(dtab_s[rows : rows + halo_rows, :], ws[:, width:])
    part_ref[...] += dot_nt(dq_s[...], ws[:, :width]) + dot_nt(dtab_s[:rows, :], ws[:, width:])


def tile_of(place_ref, flip, back_ref, per):
    at = lax.bitwise_xor(place_ref[2], flip) * per
    return back_ref[pl.ds(pl.multiple_of(at, per), per), :]


def outer_sum_kernel(per, place_ref, back_ref, *refs):
    *terms, out_ref = refs
    wide = terms[0].shape[1]
    total = terms[0][...].astype(F32)
    for term in terms[1:]:
        total = total + term[...].astype(F32)
    out_ref[:, :wide] = total.astype(BF16)
    tiles = [tile_of(place_ref, 2 * k + 1, back_ref, per) for k in range(len(terms))]
    out_ref[:, wide:] = jnp.concatenate(tiles, axis=0).astype(BF16)


def inner_sum_kernel(per, place_ref, back_ref, mine_ref, other_ref, *out):
    rows = mine_ref.shape[0]
    wide = mine_ref.shape[1] - back_ref.shape[1]
    lanes = out[0].shape[1] - wide
    total = (mine_ref[:, :wide].astype(F32) + other_ref[:, :wide].astype(F32)).astype(BF16)
    passing = other_ref[:, wide:].astype(F32)
    for k in range(len(out)):
        out[k][:, :wide] = total
        both = [tile_of(place_ref, 2 * k, back_ref, per), passing[k * per : (k + 1) * per]]
        folds = [
            tile[:, i * lanes : (i + 1) * lanes]
            for tile in both
            for i in range(rows // (2 * per))
        ]
        out[k][:, wide:] = jnp.concatenate(folds, axis=0).astype(BF16)


def last_kernel(per, place_ref, route_ref, part_ref, *refs):
    got = refs[:-6]
    feat_hbm, wtemp_hbm, feat, wtemp, came_s, sems = refs[-6:]
    pieces = len(got)
    rows = got[0].shape[0]
    wide = wtemp.shape[2]
    lanes = got[0].shape[1] - wide
    stores = []
    for k in range(pieces):
        wtemp[k] = got[k][:, :wide].astype(F32)
        at = pl.multiple_of(lax.bitwise_xor(place_ref[1], k) * rows, rows)
        stores.append(Fetch(sems.at[k:], (wtemp.at[k], wtemp_hbm.at[pl.ds(at, rows), :])))
        folded = got[k][:, wide:].astype(F32)
        folds = rows // (2 * per)
        for j in range(2):
            d = lax.bitwise_xor(place_ref[2], 2 * k + j) * per
            for i in range(folds):
                f = (j * folds + i) * per
                came_s[pl.ds(pl.multiple_of(d, per), per), i * lanes : (i + 1) * lanes] = folded[
                    f : f + per
                ]
    back = dot_tn(pick_rows(route_ref, part_ref.shape[0]), came_s[...].astype(BF16))
    feat[...] = (part_ref[...] + back).astype(BF16)
    stores.append(Fetch(sems.at[pieces:], (feat, feat_hbm)))
    for store in stores:
        store.wait(0)


def params(mib):
    return pltpu.CompilerParams(vmem_limit_bytes=mib * 1024 * 1024)


def gather_blocks(block, axis):
    count = lax.axis_size(axis)
    held = {0: block}
    bit = count // 2
    while bit:
        for m in sorted(held):
            pairs = [(i, i ^ bit) for i in range(count)]
            held[m ^ bit] = lax.ppermute(held[m], axis, pairs)
        bit //= 2
    return [held[m] for m in range(count)]


def in_hbm(*arrays):
    return [pltpu.with_memory_space_constraint(a, pltpu.HBM) for a in arrays]


def exchange(tiles, axis):
    return lax.all_to_all(tiles, axis, split_axis=0, concat_axis=0, tiled=True)


def flipped(block, axis, flip):
    count = lax.axis_size(axis)
    return lax.ppermute(block, axis, [(i, i ^ flip) for i in range(count)])


def per_device(
    feat, w_struct, w_temp, pos_embed, rel_bias, nbr, rel_type, send_idx, active, cotangent
):
    x = feat[0]
    local, width = x.shape
    heads = rel_bias.shape[1]
    slots = nbr.shape[2]
    doms = lax.axis_size("dom")
    snaps = lax.axis_size("snap")
    ents = local // snaps
    route = send_idx[0, 0]
    halo_per = route.shape[1]
    halo_rows = doms * halo_per
    keys = -(-(local + halo_rows) // LANES) * LANES
    share = width // snaps
    pieces = doms // 2
    piece = share // pieces
    lanes = 2 * halo_per * width // piece if piece else 0
    paired = (
        doms % 2 == 0
        and doms & (doms - 1) == 0
        and piece == pieces * halo_per
        and piece % 16 == 0
        and lanes % LANES == 0
        and lanes > 0
    )
    if not paired:
        pieces = 1
    dom = lax.axis_index("dom").astype(jnp.int32)
    snap = lax.axis_index("snap").astype(jnp.int32)
    place = jnp.stack([snap, dom // 2, dom])

    def shape(*dims, dtype=BF16):
        return jax.ShapeDtypeStruct(dims, dtype)

    def hbm(*dims, dtype=BF16):
        return pltpu.HBM(dims, dtype)

    tiles = pl.pallas_call(
        tiles_kernel,
        out_shape=shape(halo_rows, width),
        in_specs=[HBM, HBM],
        out_specs=VMEM,
        scratch_shapes=[
            pltpu.SMEM(route.shape, jnp.int32),
            pltpu.VMEM((local, width), BF16),
            pltpu.SemaphoreType.DMA((2,)),
        ],
        compiler_params=params(8),
        name="halo_tiles",
    )(*in_hbm(route, x))
    halo = exchange(tiles.reshape(doms, halo_per, width), "dom").reshape(halo_rows, width)

    edge, load = pl.pallas_call(
        own_kernel,
        out_shape=(hbm(heads, local, keys, dtype=F32), shape(snaps + 1, ents, width)),
        in_specs=[HBM] * 5,
        out_specs=(HBM, VMEM),
        scratch_shapes=[
            pltpu.VMEM((slots, local), jnp.int32),
            pltpu.VMEM((slots, local), jnp.int32),
            pltpu.VMEM(rel_bias.shape, F32),
            pltpu.VMEM((snaps, ents), jnp.int32),
            pltpu.VMEM((snaps, ents, width), BF16),
            pltpu.VMEM((heads, local, keys), F32),
            pltpu.SemaphoreType.DMA((5 + heads,)),
        ],
        compiler_params=params(16),
        cost_estimate=pl.CostEstimate(flops=10**9, bytes_accessed=4 * 10**6, transcendentals=0),
        name="own_edges",
    )(*in_hbm(nbr[0].T, rel_type[0].T, rel_bias, active, cotangent))
    cots = gather_blocks(load, "snap")

    hidden = pl.pallas_call(
        functools.partial(forward_kernel, heads),
        out_shape=shape(local, width),
        in_specs=[VMEM] * 3 + [HBM],
        out_specs=VMEM,
        scratch_shapes=[
            pltpu.VMEM((heads, local, keys), F32),
            pltpu.VMEM((local, 3 * width), BF16),
            pltpu.VMEM((keys, 2 * width), BF16),
            pltpu.SemaphoreType.DMA((heads,)),
        ],
        compiler_params=params(8),
        name="struct_forward",
    )(x, halo, w_struct, *in_hbm(edge))

    hids = gather_blocks(hidden, "snap")
    every = snaps * local
    *terms, dt_own, cot_own = pl.pallas_call(
        functools.partial(temporal_kernel, snaps, heads, pieces),
        out_shape=(shape(share // pieces, 3 * width),) * pieces
        + (shape(local, 3 * width), shape(local, width)),
        in_specs=[SMEM] + [VMEM] * (2 + 2 * snaps),
        out_specs=(VMEM,) * (pieces + 2),
        scratch_shapes=[
            pltpu.VMEM((every, width), BF16),
            pltpu.VMEM((every, width), F32 if ents % 16 else BF16),
            pltpu.VMEM((every, 3 * width), BF16),
            pltpu.VMEM((every, 3 * width), BF16),
            pltpu.VMEM((local, LANES), F32),
            pltpu.VMEM((2 * every, width), BF16),
            pltpu.VMEM((every, LANES), F32),
            pltpu.VMEM((every, LANES), F32),
            pltpu.VMEM((every, LANES), BF16),
            pltpu.VMEM((every, LANES), BF16),
            pltpu.VMEM((every, width), F32),
            pltpu.VMEM((every, width), F32),
            pltpu.VMEM((every, width), F32),
            pltpu.VMEM((every, width), F32),
            pltpu.VMEM((share, 3 * width), BF16),
        ],
        compiler_params=params(24 if snaps <= 4 else 56),
        name="temporal",
    )(place, pos_embed, w_temp, *hids, *cots)

    if paired:
        got = [terms[0]] + [flipped(terms[k], "dom", 2 * k) for k in range(1, pieces)]
    else:
        got = exchange(terms[0].reshape(doms, share // doms, 3 * width), "dom")
    back, partial = pl.pallas_call(
        functools.partial(backward_kernel, heads),
        out_shape=(shape(halo_rows, width, dtype=F32), shape(local, width, dtype=F32)),
        in_specs=[VMEM] * 2 + [HBM] * 5,
        out_specs=(VMEM, VMEM),
        scratch_shapes=[
            pltpu.VMEM((local, width), BF16),
            pltpu.VMEM((halo_rows, width), BF16),
            pltpu.VMEM((heads, local, keys), F32),
            pltpu.VMEM(w_struct.shape, BF16),
            pltpu.VMEM(w_temp.shape, BF16),
            pltpu.VMEM((local, 3 * width), BF16),
            pltpu.VMEM((keys, 2 * width), BF16),
            pltpu.VMEM((local, width), BF16),
            pltpu.VMEM((keys, 2 * width), BF16),
            pltpu.SemaphoreType.DMA((5,)),
        ],
        compiler_params=params(24),
        cost_estimate=pl.CostEstimate(flops=2 * 10**9, bytes_accessed=8 * 10**6, transcendentals=0),
        name="struct_backward",
    )(dt_own, cot_own, *in_hbm(x, halo, edge, w_struct, w_temp))

    if not paired:
        total = jnp.sum(got.astype(F32), axis=0).astype(BF16)
        full = exchange(jnp.broadcast_to(total[None], (doms,) + total.shape), "dom")
        grad_wtemp = full.astype(F32).reshape(share, 3 * width)
        came = exchange(back.astype(BF16).reshape(doms, halo_per, width), "dom")
        picks = (route.reshape(-1)[:, None] == jnp.arange(local, dtype=jnp.int32)).astype(BF16)
        sums = dot_tn(picks, came.reshape(halo_rows, width))
        return ((partial + sums).astype(BF16)[None], grad_wtemp)

    mine = pl.pallas_call(
        functools.partial(outer_sum_kernel, halo_per),
        out_shape=shape(piece, 4 * width),
        in_specs=[SMEM] + [VMEM] * (1 + pieces),
        out_specs=VMEM,
        compiler_params=params(8),
        name="outer_sum",
    )(place, back, *got)
    other = flipped(mine, "dom", 1)
    sums = pl.pallas_call(
        functools.partial(inner_sum_kernel, halo_per),
        out_shape=(shape(piece, 3 * width + lanes),) * pieces,
        in_specs=[SMEM] + [VMEM] * 3,
        out_specs=(VMEM,) * pieces,
        compiler_params=params(8),
        name="inner_sum",
    )(place, back, mine, other)
    sums = [sums[0]] + [flipped(sums[k], "dom", 2 * k) for k in range(1, pieces)]
    grad_feat, grad_wtemp = pl.pallas_call(
        functools.partial(last_kernel, halo_per),
        out_shape=(hbm(local, width), hbm(share, 3 * width, dtype=F32)),
        in_specs=[SMEM, SMEM] + [VMEM] * (1 + pieces),
        out_specs=(HBM, HBM),
        scratch_shapes=[
            pltpu.VMEM((local, width), BF16),
            pltpu.VMEM((pieces, piece, 3 * width), F32),
            pltpu.VMEM((halo_rows, width), F32),
            pltpu.SemaphoreType.DMA((pieces + 1,)),
        ],
        compiler_params=params(8),
        name="last_sums",
    )(place, route, partial, *sums)
    return (grad_feat[None], grad_wtemp)


def solution(mesh):
    return jax.shard_map(
        per_device,
        mesh=mesh,
        in_specs=(
            P("snap", "dom", None),
            P(),
            P(),
            P(),
            P(),
            P("snap", "dom", None),
            P("snap", "dom", None),
            P("snap", "dom", None, None),
            P(None, ("dom", "snap")),
            P(None, ("dom", "snap"), None),
        ),
        out_specs=(P("snap", "dom", None), P("snap", None)),
        check_vma=False,
    )
```

```python
import functools

import jax
import jax.numpy as jnp
from jax import lax
from jax.experimental import pallas as pl
from jax.experimental.pallas import tpu as pltpu
from jax.sharding import PartitionSpec as P

F32 = jnp.float32
BF16 = jnp.bfloat16
LANES = 128
NEG = -1e30
VMEM = pl.BlockSpec(memory_space=pltpu.VMEM)
SMEM = pl.BlockSpec(memory_space=pltpu.SMEM)
HBM = pl.BlockSpec(memory_space=pltpu.HBM)


def dot_nn(a, b):
    return lax.dot_general(a, b, (((1,), (0,)), ((), ())), preferred_element_type=F32)


def dot_nt(a, b):
    return lax.dot_general(a, b, (((1,), (1,)), ((), ())), preferred_element_type=F32)


def dot_tn(a, b):
    return lax.dot_general(a, b, (((0,), (0,)), ((), ())), preferred_element_type=F32)


def stack_heads(block, head_dim):
    rows, lanes = block.shape
    head = lax.broadcasted_iota(jnp.int32, (rows, lanes), 1) // head_dim
    zero = jnp.zeros_like(block)
    return jnp.concatenate(
        [jnp.where(head == g, block, zero) for g in range(lanes // head_dim)], axis=0
    )


def unstack_heads(stacked, head_dim):
    lanes = stacked.shape[1]
    groups = lanes // head_dim
    rows = stacked.shape[0] // groups
    head = lax.broadcasted_iota(jnp.int32, (rows, lanes), 1) // head_dim
    out = stacked[:rows]
    for g in range(1, groups):
        out = jnp.where(head == g, stacked[g * rows : (g + 1) * rows], out)
    return out


class Fetch:

    def __init__(self, sems, *pairs):
        self.copies = [
            pltpu.make_async_copy(src, dst, sems.at[i]) for i, (src, dst) in enumerate(pairs)
        ]
        for copy in self.copies:
            copy.start()

    def wait(self, *which):
        for i in which:
            self.copies[i].wait()


def pick_rows(route_ref, local):
    doms, per = route_ref.shape
    lane = lax.broadcasted_iota(jnp.int32, (per, local), 1)
    sub = lax.broadcasted_iota(jnp.int32, (per, local), 0)
    tiles = []
    for r in range(doms):
        spot = jnp.zeros((per, local), jnp.int32)
        for j in range(per):
            spot = jnp.where(sub == j, route_ref[r, j], spot)
        tiles.append(jnp.where(lane == spot, 1.0, 0.0))
    return jnp.concatenate(tiles, axis=0).astype(BF16)


def tiles_kernel(route_hbm, x_hbm, out_ref, route, x, sems):
    fetch = Fetch(sems, (route_hbm, route), (x_hbm, x))
    fetch.wait(0, 1)
    out_ref[...] = dot_nn(pick_rows(route, x.shape[0]), x[...]).astype(BF16)


def load_kernel(_, act_hbm, cot_hbm, load_hbm, act, cot, flags_s, sems):
    snaps, ents, width = cot.shape
    fetch = Fetch(sems, (cot_hbm, cot), (act_hbm, act))
    row = lax.broadcasted_iota(jnp.int32, (ents, ents), 0)
    col = lax.broadcasted_iota(jnp.int32, (ents, ents), 1)
    lane = lax.broadcasted_iota(jnp.int32, (ents, width), 1)
    flags = jnp.zeros((ents, width), F32)
    fetch.wait(1)
    on = act[...].astype(F32)
    for t in range(snaps):
        column = jnp.sum(jnp.where(row == col, on[t : t + 1, :], 0.0), axis=1, keepdims=True)
        flags = jnp.where(lane == t, column, flags)
    flags_s[...] = flags.astype(BF16)
    fetch.wait(0)
    store = Fetch(sems.at[2:], (flags_s, load_hbm.at[snaps]), (cot, load_hbm.at[:snaps]))
    store.wait(0, 1)


def fill_table(tab_s, proj, halo, w_kv):
    rows, width = proj.shape[0], halo.shape[1]
    used = rows + halo.shape[0]
    tab_s[:rows, :] = proj[:, width:]
    for part in range(2):
        cols = slice(part * width, (part + 1) * width)
        tab_s[rows:used, cols] = dot_nn(halo[...], w_kv[:, cols]).astype(BF16)
    if tab_s.shape[0] > used:
        tab_s[used:, :] = jnp.zeros((tab_s.shape[0] - used, 2 * width), BF16)


def edge_counts(nbr, rel, kinds, keys):
    bits = 4
    slots, rows = nbr.shape
    target = jnp.transpose(nbr[...].astype(F32))
    one = jnp.transpose(lax.shift_left(jnp.ones_like(rel[...]), bits * rel[...]).astype(F32))
    spot = lax.broadcasted_iota(jnp.int32, (rows, keys), 1).astype(F32)
    packed = jnp.zeros((rows, keys), F32)
    for k in range(slots):
        packed = packed + jnp.where(target[:, k : k + 1] == spot, one[:, k : k + 1], 0.0)
    packed = packed.astype(jnp.int32)
    low = (1 << bits) - 1
    counts = [
        lax.bitwise_and(lax.shift_right_logical(packed, bits * r), low).astype(F32)
        for r in range(kinds)
    ]
    return counts, jnp.where(packed > 0, 0.0, NEG)


def edge_attention(p, heads, proj, counts, closed, gain, tab_s, width):
    keys = tab_s.shape[0]
    head_dim = width // heads
    group = LANES // head_dim
    cols = slice(p * LANES, (p + 1) * LANES)
    kk = stack_heads(tab_s[:, cols], head_dim)
    score = dot_nt(proj[:, cols], kk)
    parts = []
    for g in range(group):
        h = p * group + g
        weight = counts[0] * gain[0:1, h : h + 1]
        for r in range(1, len(counts)):
            weight = weight + counts[r] * gain[r : r + 1, h : h + 1]
        s = score[:, g * keys : (g + 1) * keys] * head_dim ** (-0.5) + closed
        e = jnp.exp(s - jnp.max(s, axis=1, keepdims=True)) * weight
        parts.append(e * (1.0 / jnp.sum(e, axis=1, keepdims=True)))
    return kk, parts


def forward_kernel(heads, x, halo, w, nbr, rel, bias, hidden_ref, proj, tab_s):
    width = x.shape[1]
    head_dim = width // heads
    for part in range(3):
        cols = slice(part * width, (part + 1) * width)
        proj[:, cols] = dot_nn(x[...], w[:, cols]).astype(BF16)
    fill_table(tab_s, proj, halo, w.at[:, width:])
    counts, closed = edge_counts(nbr, rel, bias.shape[0], tab_s.shape[0])
    gain = jnp.exp(bias[...])
    for p in range(width // LANES):
        cols = slice(p * LANES, (p + 1) * LANES)
        vcols = slice(width + p * LANES, width + (p + 1) * LANES)
        _, attn = edge_attention(p, heads, proj, counts, closed, gain, tab_s, width)
        vv = stack_heads(tab_s[:, vcols], head_dim)
        agg = dot_nn(jnp.concatenate([a.astype(BF16) for a in attn], axis=1), vv)
        elu = jnp.where(agg > 0, agg, jnp.exp(jnp.minimum(agg, 0.0)) - 1.0)
        hidden_ref[:, cols] = (x[:, cols].astype(F32) + elu).astype(BF16)


def each(lo, hi, unroll, body):
    if unroll:
        for i in range(lo, hi):
            body(i)
    else:
        lax.fori_loop(lo, hi, lambda i, c: (body(i), c)[1], 0)


def cotangent_kernel(place_ref, *refs):
    *cot, ct_ref, act_ref = refs
    snaps = len(cot)
    ents = cot[0].shape[1]
    local = snaps * ents
    for m in range(snaps):
        at = pl.multiple_of(lax.bitwise_xor(place_ref[0], m) * ents, ents)
        for t in range(snaps):
            ct_ref[pl.ds(t * local + at, ents), :] = cot[m][t].astype(ct_ref.dtype)
        act_ref[pl.ds(at, ents), :] = cot[m][snaps][:, :LANES].astype(F32)


def temporal_kernel(snaps, heads, pieces, place_ref, pos_ref, w_s, ct_s, act_s, *refs):
    hid = refs[:snaps]
    terms_ref = refs[snaps : snaps + pieces]
    (
        dt_own_ref, cot_own_ref,
        z_s, tp_s, dt_s, prod_s, s_s, d_s, a_s, ds_s, wa_s, wd_s, dk_s, dv_s, terms_s,
    ) = refs[snaps + pieces :]
    local, width = hid[0].shape
    head_dim = width // heads
    scale = head_dim ** (-0.5)
    unroll = snaps <= 4
    me, outer = place_ref[0], place_ref[1]
    pos = pos_ref[...].astype(F32)
    which = lax.broadcasted_iota(jnp.int32, pos.shape, 0)

    def rows_of(t):
        return pl.ds(t * local if isinstance(t, int) else pl.multiple_of(t * local, local), local)

    for n in range(snaps):
        t = lax.bitwise_xor(me, n)
        shift = jnp.sum(jnp.where(which == t, pos, 0.0), axis=0, keepdims=True)
        z_s[rows_of(t), :] = (hid[n][...].astype(F32) + shift).astype(BF16)
    for part in range(3):
        cols = slice(part * width, (part + 1) * width)
        tp_s[:, cols] = dot_nn(z_s[...], w_s[:, cols]).astype(BF16)
    lane_head = lax.broadcasted_iota(jnp.int32, (width, LANES), 0) // head_dim
    fold = (lane_head == lax.broadcasted_iota(jnp.int32, (width, LANES), 1)).astype(F32)
    fold = fold.astype(BF16)
    head_lane = lax.broadcasted_iota(jnp.int32, (LANES, width), 1) // head_dim
    spread = (head_lane == lax.broadcasted_iota(jnp.int32, (LANES, width), 0)).astype(F32)
    spread_scaled = (spread * scale).astype(BF16)
    spread = spread.astype(BF16)
    act = act_s[...]
    snap_lane = lax.broadcasted_iota(jnp.int32, act.shape, 1)
    if not unroll:
        dk_s[...] = jnp.zeros_like(dk_s)
        dv_s[...] = jnp.zeros_like(dv_s)

    def one_snap(t):
        used = (t + 1 if unroll else snaps) * local
        half = snaps * local

        def product(u):
            q, k, v = (
                tp_s[rows_of(i), part * width : (part + 1) * width]
                for part, i in ((0, t), (1, u), (2, u))
            )
            prod_s[rows_of(u), :] = q * k
            prod_s[rows_of(snaps + u), :] = ct_s[rows_of(t), :].astype(BF16) * v

        each(0, t + 1, unroll, product)
        s_s[:used, :] = dot_nn(prod_s[:used, :], fold)
        d_s[:used, :] = dot_nn(prod_s[half : half + used, :], fold).astype(BF16).astype(F32)

        def mask(u):
            on = jnp.sum(jnp.where(snap_lane == u, act, 0.0), axis=1, keepdims=True)
            s_s[rows_of(u), :] = jnp.where((on > 0.5) | (u == t), s_s[rows_of(u), :] * scale, NEG)

        each(0, t + 1, unroll, mask)

        def reduced(fn, start):
            if unroll:
                for u in range(t + 1):
                    start = fn(u, start)
                return start
            return lax.fori_loop(0, t + 1, fn, start)

        top = reduced(
            lambda u, c: jnp.maximum(c, s_s[rows_of(u), :]), jnp.full((local, LANES), NEG, F32)
        )

        def expo(u, total):
            e = jnp.exp(s_s[rows_of(u), :] - top)
            s_s[rows_of(u), :] = e
            return total + e

        inv = 1.0 / reduced(expo, jnp.zeros((local, LANES), F32))

        def weigh(u, total):
            a = s_s[rows_of(u), :] * inv
            s_s[rows_of(u), :] = a
            return total + a * d_s[rows_of(u), :]

        dot = reduced(weigh, jnp.zeros((local, LANES), F32))

        def keep(u):
            a = s_s[rows_of(u), :]
            a_s[rows_of(u), :] = a.astype(BF16)
            ds_s[rows_of(u), :] = (a * (d_s[rows_of(u), :] - dot)).astype(BF16)

        each(0, t + 1, unroll, keep)
        wa_s[:used, :] = dot_nn(a_s[:used, :], spread)
        wd_s[:used, :] = dot_nn(ds_s[:used, :], spread_scaled)

        for p in range(width // LANES):
            c0 = p * LANES
            cols = slice(c0, c0 + LANES)
            q = tp_s[rows_of(t), cols].astype(F32)
            ct = ct_s[rows_of(t), cols].astype(F32)

            def back(u, dq):
                k = tp_s[rows_of(u), width + c0 : width + c0 + LANES].astype(F32)
                wide_ds = wd_s[rows_of(u), cols]
                dk, dv = wide_ds * q, wa_s[rows_of(u), cols] * ct
                if unroll and u == t:
                    dk_s[rows_of(u), cols] = dk
                    dv_s[rows_of(u), cols] = dv
                else:
                    dk_s[rows_of(u), cols] += dk
                    dv_s[rows_of(u), cols] += dv
                return dq + wide_ds * k

            dt_s[rows_of(t), cols] = reduced(back, jnp.zeros_like(q)).astype(BF16)

    each(0, snaps, unroll, one_snap)
    dt_s[:, width : 2 * width] = dk_s[...].astype(BF16)
    dt_s[:, 2 * width :] = dv_s[...].astype(BF16)
    share = width // snaps
    pick = (
        lax.broadcasted_iota(jnp.int32, (width, share), 0)
        == lax.broadcasted_iota(jnp.int32, (width, share), 1) + me * share
    )
    z_mine = dot_nn(z_s[...], pick.astype(F32).astype(BF16)).astype(BF16)
    for part in range(3):
        cols = slice(part * width, (part + 1) * width)
        terms_s[:, cols] = dot_tn(z_mine, dt_s[:, cols]).astype(BF16)
    piece = share // pieces
    for k in range(pieces):
        if pieces == 1:
            terms_ref[k][...] = terms_s[...]
        else:
            at = pl.multiple_of(lax.bitwise_xor(outer, k) * piece, piece)
            terms_ref[k][...] = terms_s[pl.ds(at, piece), :]
    dt_own_ref[...] = dt_s[rows_of(me), :]
    cot_own_ref[...] = ct_s[rows_of(me), :].astype(BF16)


def backward_kernel(
    heads, dt, cot, x, halo, nbr, rel, bias, ws, wt, back_ref, part_ref,
    proj, tab_s, dq_s, dtab_s,
):
    rows, width = cot.shape
    halo_rows = halo.shape[0]
    keys = tab_s.shape[0]
    head_dim = width // heads
    group = LANES // head_dim
    scale = head_dim ** (-0.5)
    dh = cot[...].astype(F32) + dot_nt(dt[...], wt[...])
    part_ref[...] = dh.astype(BF16).astype(F32)
    for part in range(3):
        cols = slice(part * width, (part + 1) * width)
        proj[:, cols] = dot_nn(x[...], ws[:, cols]).astype(BF16)
    fill_table(tab_s, proj, halo, ws.at[:, width:])
    counts, closed = edge_counts(nbr, rel, bias.shape[0], tab_s.shape[0])
    gain = jnp.exp(bias[...])
    for p in range(width // LANES):
        cols = slice(p * LANES, (p + 1) * LANES)
        vcols = slice(width + p * LANES, width + (p + 1) * LANES)
        kk, attn = edge_attention(p, heads, proj, counts, closed, gain, tab_s, width)
        vv = stack_heads(tab_s[:, vcols], head_dim)
        attn_b = jnp.concatenate([a.astype(BF16) for a in attn], axis=1)
        agg = dot_nn(attn_b, vv)
        da = part_ref[:, cols] * jnp.where(agg > 0, 1.0, jnp.exp(jnp.minimum(agg, 0.0)))
        da = da.astype(BF16)
        dattn = dot_nt(da, vv).astype(BF16).astype(F32)
        ds = []
        for g in range(group):
            ad = attn[g] * dattn[:, g * keys : (g + 1) * keys]
            ds.append((ad - attn[g] * jnp.sum(ad, axis=1, keepdims=True)).astype(BF16))
        ds = jnp.concatenate(ds, axis=1)
        dq_s[:, cols] = (dot_nn(ds, kk) * scale).astype(BF16)
        dtab_s[:, cols] = (unstack_heads(dot_tn(ds, proj[:, cols]), head_dim) * scale).astype(BF16)
        dtab_s[:, vcols] = unstack_heads(dot_tn(attn_b, da), head_dim).astype(BF16)
    back_ref[...] = dot_nt(dtab_s[rows : rows + halo_rows, :], ws[:, width:])
    part_ref[...] += dot_nt(dq_s[...], ws[:, :width]) + dot_nt(dtab_s[:rows, :], ws[:, width:])


def tile_of(place_ref, flip, back_ref, per):
    at = lax.bitwise_xor(place_ref[2], flip) * per
    return back_ref[pl.ds(pl.multiple_of(at, per), per), :]


def outer_sum_kernel(per, place_ref, back_ref, *refs):
    *terms, out_ref = refs
    wide = terms[0].shape[1]
    total = terms[0][...].astype(F32)
    for term in terms[1:]:
        total = total + term[...].astype(F32)
    out_ref[:, :wide] = total.astype(BF16)
    tiles = [tile_of(place_ref, 2 * k + 1, back_ref, per) for k in range(len(terms))]
    out_ref[:, wide:] = jnp.concatenate(tiles, axis=0).astype(BF16)


def inner_sum_kernel(per, place_ref, back_ref, mine_ref, other_ref, *out):
    rows = mine_ref.shape[0]
    wide = mine_ref.shape[1] - back_ref.shape[1]
    lanes = out[0].shape[1] - wide
    total = (mine_ref[:, :wide].astype(F32) + other_ref[:, :wide].astype(F32)).astype(BF16)
    passing = other_ref[:, wide:].astype(F32)
    for k in range(len(out)):
        out[k][:, :wide] = total
        both = [tile_of(place_ref, 2 * k, back_ref, per), passing[k * per : (k + 1) * per]]
        folds = [
            tile[:, i * lanes : (i + 1) * lanes]
            for tile in both
            for i in range(rows // (2 * per))
        ]
        out[k][:, wide:] = jnp.concatenate(folds, axis=0).astype(BF16)


def unpack_sums(flips, per, place_ref, got, wtemp, wtemp_hbm, came_s, sems):
    rows = got[0].shape[0]
    lanes = got[0].shape[1] - wtemp.shape[2]
    folds = rows // (2 * per)
    stores = []
    came_s[...] = jnp.zeros_like(came_s)
    for i, k in enumerate(flips):
        wtemp[i] = got[i][:, : wtemp.shape[2]].astype(F32)
        at = pl.multiple_of(lax.bitwise_xor(place_ref[1], k) * rows, rows)
        stores.append(Fetch(sems.at[i:], (wtemp.at[i], wtemp_hbm.at[pl.ds(at, rows), :])))
        folded = got[i][:, wtemp.shape[2] :].astype(F32)
        for j in range(2):
            d = pl.multiple_of(lax.bitwise_xor(place_ref[2], 2 * k + j) * per, per)
            for f in range(folds):
                row = (j * folds + f) * per
                came_s[pl.ds(d, per), f * lanes : (f + 1) * lanes] = folded[row : row + per]
    return stores


def early_kernel(flips, per, place_ref, route_ref, part_ref, *refs):
    got = refs[: len(flips)]
    sum_ref, picks_ref, wtemp_hbm, wtemp, came_s, sems = refs[len(flips) :]
    stores = unpack_sums(flips, per, place_ref, got, wtemp, wtemp_hbm, came_s, sems)
    picks = pick_rows(route_ref, part_ref.shape[0])
    picks_ref[...] = picks
    sum_ref[...] = part_ref[...] + dot_tn(picks, came_s[...].astype(BF16))
    for store in stores:
        store.wait(0)


def last_kernel(flips, per, place_ref, picks_ref, sum_ref, _, *refs):
    got = refs[: len(flips)]
    feat_hbm, wtemp_hbm, feat, wtemp, came_s, sems = refs[len(flips) :]
    stores = unpack_sums(flips, per, place_ref, got, wtemp, wtemp_hbm, came_s, sems)
    feat[...] = (sum_ref[...] + dot_tn(picks_ref[...], came_s[...].astype(BF16))).astype(BF16)
    stores.append(Fetch(sems.at[len(flips) :], (feat, feat_hbm)))
    for store in stores:
        store.wait(0)


def params(mib):
    return pltpu.CompilerParams(vmem_limit_bytes=mib * 1024 * 1024)


def gather_blocks(held, axis, bit, last):
    held = dict(held)
    while bit >= last:
        for m in sorted(held):
            held[m ^ bit] = flipped(held[m], axis, bit)
        bit //= 2
    return held


def in_hbm(*arrays):
    return [pltpu.with_memory_space_constraint(a, pltpu.HBM) for a in arrays]


def exchange(tiles, axis):
    return lax.all_to_all(tiles, axis, split_axis=0, concat_axis=0, tiled=True)


def flipped(block, axis, flip):
    count = lax.axis_size(axis)
    return lax.ppermute(block, axis, [(i, i ^ flip) for i in range(count)])


def per_device(
    feat, w_struct, w_temp, pos_embed, rel_bias, nbr, rel_type, send_idx, active, cotangent
):
    x = feat[0]
    local, width = x.shape
    heads = rel_bias.shape[1]
    doms = lax.axis_size("dom")
    snaps = lax.axis_size("snap")
    ents = local // snaps
    route = send_idx[0, 0]
    halo_per = route.shape[1]
    halo_rows = doms * halo_per
    keys = -(-(local + halo_rows) // LANES) * LANES
    share = width // snaps
    pieces = doms // 2
    piece = share // pieces
    lanes = 2 * halo_per * width // piece if piece else 0
    paired = (
        doms % 2 == 0
        and doms & (doms - 1) == 0
        and piece == pieces * halo_per
        and piece % 16 == 0
        and lanes % LANES == 0
        and lanes > 0
    )
    if not paired:
        pieces = 1
    dom = lax.axis_index("dom").astype(jnp.int32)
    snap = lax.axis_index("snap").astype(jnp.int32)
    place = jnp.stack([snap, dom // 2, dom])

    def shape(*dims, dtype=BF16):
        return jax.ShapeDtypeStruct(dims, dtype)

    def hbm(*dims, dtype=BF16):
        return pltpu.HBM(dims, dtype)

    tiles = pl.pallas_call(
        tiles_kernel,
        out_shape=shape(halo_rows, width),
        in_specs=[HBM, HBM],
        out_specs=VMEM,
        scratch_shapes=[
            pltpu.SMEM(route.shape, jnp.int32),
            pltpu.VMEM((local, width), BF16),
            pltpu.SemaphoreType.DMA((2,)),
        ],
        compiler_params=params(8),
        name="halo_tiles",
    )(*in_hbm(route, x))
    halo = exchange(tiles.reshape(doms, halo_per, width), "dom").reshape(halo_rows, width)

    load = pl.pallas_call(
        load_kernel,
        out_shape=hbm(snaps + 1, ents, width),
        in_specs=[SMEM, HBM, HBM],
        out_specs=HBM,
        scratch_shapes=[
            pltpu.VMEM((snaps, ents), jnp.int32),
            pltpu.VMEM((snaps, ents, width), BF16),
            pltpu.VMEM((ents, width), BF16),
            pltpu.SemaphoreType.DMA((4,)),
        ],
        compiler_params=params(8),
        cost_estimate=pl.CostEstimate(flops=10**9, bytes_accessed=4 * 10**6, transcendentals=0),
        name="own_load",
    )(place, *in_hbm(active, cotangent))
    edges = (nbr[0].T, rel_type[0].T, rel_bias)
    cots = gather_blocks({0: load}, "snap", snaps // 2, 1)
    cots = [cots[m] for m in range(snaps)]

    hidden = pl.pallas_call(
        functools.partial(forward_kernel, heads),
        out_shape=shape(local, width),
        in_specs=[VMEM] * 6,
        out_specs=VMEM,
        scratch_shapes=[
            pltpu.VMEM((local, 3 * width), BF16),
            pltpu.VMEM((keys, 2 * width), BF16),
        ],
        compiler_params=params(8),
        name="struct_forward",
    )(x, halo, w_struct, *edges)

    hids = gather_blocks({0: hidden}, "snap", snaps // 2, 1)
    hids = [hids[m] for m in range(snaps)]
    every = snaps * local
    ct, act = pl.pallas_call(
        cotangent_kernel,
        out_shape=(
            shape(every, width, dtype=F32 if ents % 16 else BF16),
            shape(local, LANES, dtype=F32),
        ),
        in_specs=[SMEM] + [VMEM] * snaps,
        out_specs=(VMEM, VMEM),
        compiler_params=params(8),
        name="cotangents",
    )(place, *cots)
    *terms, dt_own, cot_own = pl.pallas_call(
        functools.partial(temporal_kernel, snaps, heads, pieces),
        out_shape=(shape(share // pieces, 3 * width),) * pieces
        + (shape(local, 3 * width), shape(local, width)),
        in_specs=[SMEM] + [VMEM] * (4 + snaps),
        out_specs=(VMEM,) * (pieces + 2),
        scratch_shapes=[
            pltpu.VMEM((every, width), BF16),
            pltpu.VMEM((every, 3 * width), BF16),
            pltpu.VMEM((every, 3 * width), BF16),
            pltpu.VMEM((2 * every, width), BF16),
            pltpu.VMEM((every, LANES), F32),
            pltpu.VMEM((every, LANES), F32),
            pltpu.VMEM((every, LANES), BF16),
            pltpu.VMEM((every, LANES), BF16),
            pltpu.VMEM((every, width), F32),
            pltpu.VMEM((every, width), F32),
            pltpu.VMEM((every, width), F32),
            pltpu.VMEM((every, width), F32),
            pltpu.VMEM((share, 3 * width), BF16),
        ],
        compiler_params=params(24 if snaps <= 4 else 56),
        name="temporal",
    )(place, pos_embed, w_temp, ct, act, *hids)

    if paired:
        got = [terms[0]] + [flipped(terms[k], "dom", 2 * k) for k in range(1, pieces)]
    else:
        got = exchange(terms[0].reshape(doms, share // doms, 3 * width), "dom")
    back, partial = pl.pallas_call(
        functools.partial(backward_kernel, heads),
        out_shape=(shape(halo_rows, width, dtype=F32), shape(local, width, dtype=F32)),
        in_specs=[VMEM] * 9,
        out_specs=(VMEM, VMEM),
        scratch_shapes=[
            pltpu.VMEM((local, 3 * width), BF16),
            pltpu.VMEM((keys, 2 * width), BF16),
            pltpu.VMEM((local, width), BF16),
            pltpu.VMEM((keys, 2 * width), BF16),
        ],
        compiler_params=params(16),
        cost_estimate=pl.CostEstimate(flops=2 * 10**9, bytes_accessed=8 * 10**6, transcendentals=0),
        name="struct_backward",
    )(dt_own, cot_own, x, halo, *edges, w_struct, w_temp)

    if not paired:
        total = jnp.sum(got.astype(F32), axis=0).astype(BF16)
        full = exchange(jnp.broadcast_to(total[None], (doms,) + total.shape), "dom")
        grad_wtemp = full.astype(F32).reshape(share, 3 * width)
        came = exchange(back.astype(BF16).reshape(doms, halo_per, width), "dom")
        picks = (route.reshape(-1)[:, None] == jnp.arange(local, dtype=jnp.int32)).astype(BF16)
        sums = dot_tn(picks, came.reshape(halo_rows, width))
        return ((partial + sums).astype(BF16)[None], grad_wtemp)

    mine = pl.pallas_call(
        functools.partial(outer_sum_kernel, halo_per),
        out_shape=shape(piece, 4 * width),
        in_specs=[SMEM] + [VMEM] * (1 + pieces),
        out_specs=VMEM,
        compiler_params=params(8),
        name="outer_sum",
    )(place, back, *got)
    other = flipped(mine, "dom", 1)
    sums = pl.pallas_call(
        functools.partial(inner_sum_kernel, halo_per),
        out_shape=(shape(piece, 3 * width + lanes),) * pieces,
        in_specs=[SMEM] + [VMEM] * 3,
        out_specs=(VMEM,) * pieces,
        compiler_params=params(8),
        name="inner_sum",
    )(place, back, mine, other)
    sums = [sums[0]] + [flipped(sums[k], "dom", 2 * k) for k in range(1, pieces)]
    soon, late = list(range(pieces // 2)), list(range(pieces // 2, pieces))
    partial, picks, grad_wtemp = pl.pallas_call(
        functools.partial(early_kernel, soon, halo_per),
        out_shape=(
            shape(local, width, dtype=F32),
            shape(halo_rows, local),
            hbm(share, 3 * width, dtype=F32),
        ),
        in_specs=[SMEM, SMEM] + [VMEM] * (1 + len(soon)),
        out_specs=(VMEM, VMEM, HBM),
        scratch_shapes=[
            pltpu.VMEM((len(soon), piece, 3 * width), F32),
            pltpu.VMEM((halo_rows, width), F32),
            pltpu.SemaphoreType.DMA((len(soon),)),
        ],
        compiler_params=params(8),
        name="early_sums",
    )(place, route, partial, *[sums[k] for k in soon])
    grad_feat, grad_wtemp = pl.pallas_call(
        functools.partial(last_kernel, late, halo_per),
        out_shape=(hbm(local, width), hbm(share, 3 * width, dtype=F32)),
        in_specs=[SMEM] + [VMEM] * 2 + [HBM] + [VMEM] * len(late),
        out_specs=(HBM, HBM),
        scratch_shapes=[
            pltpu.VMEM((local, width), BF16),
            pltpu.VMEM((len(late), piece, 3 * width), F32),
            pltpu.VMEM((halo_rows, width), F32),
            pltpu.SemaphoreType.DMA((len(late) + 1,)),
        ],
        input_output_aliases={3: 1},
        compiler_params=params(8),
        name="last_sums",
    )(place, picks, partial, *in_hbm(grad_wtemp), *[sums[k] for k in late])
    return (grad_feat[None], grad_wtemp)


def solution(mesh):
    return jax.shard_map(
        per_device,
        mesh=mesh,
        in_specs=(
            P("snap", "dom", None),
            P(),
            P(),
            P(),
            P(),
            P("snap", "dom", None),
            P("snap", "dom", None),
            P("snap", "dom", None, None),
            P(None, ("dom", "snap")),
            P(None, ("dom", "snap"), None),
        ),
        out_specs=(P("snap", "dom", None), P("snap", None)),
        check_vma=False,
    )
```

```python
import functools

import jax
import jax.numpy as jnp
from jax import lax
from jax.experimental import pallas as pl
from jax.experimental.pallas import tpu as pltpu
from jax.sharding import PartitionSpec as P

F32 = jnp.float32
BF16 = jnp.bfloat16
LANES = 128
NEG = -1e30
VMEM = pl.BlockSpec(memory_space=pltpu.VMEM)
SMEM = pl.BlockSpec(memory_space=pltpu.SMEM)
HBM = pl.BlockSpec(memory_space=pltpu.HBM)


def snap_index():
    return lax.axis_index("snap")


def dom_index():
    return lax.axis_index("dom")


def dot_nn(a, b):
    return lax.dot_general(a, b, (((1,), (0,)), ((), ())), preferred_element_type=F32)


def dot_nt(a, b):
    return lax.dot_general(a, b, (((1,), (1,)), ((), ())), preferred_element_type=F32)


def dot_tn(a, b):
    return lax.dot_general(a, b, (((0,), (0,)), ((), ())), preferred_element_type=F32)


def stack_heads(block, head_dim):
    rows, lanes = block.shape
    head = lax.broadcasted_iota(jnp.int32, (rows, lanes), 1) // head_dim
    zero = jnp.zeros_like(block)
    return jnp.concatenate(
        [jnp.where(head == g, block, zero) for g in range(lanes // head_dim)], axis=0
    )


def unstack_heads(stacked, head_dim):
    lanes = stacked.shape[1]
    groups = lanes // head_dim
    rows = stacked.shape[0] // groups
    head = lax.broadcasted_iota(jnp.int32, (rows, lanes), 1) // head_dim
    out = stacked[:rows]
    for g in range(1, groups):
        out = jnp.where(head == g, stacked[g * rows : (g + 1) * rows], out)
    return out


class Fetch:

    def __init__(self, sems, *pairs):
        self.copies = [
            pltpu.make_async_copy(src, dst, sems.at[i]) for i, (src, dst) in enumerate(pairs)
        ]
        for copy in self.copies:
            copy.start()

    def wait(self, *which):
        for i in which:
            self.copies[i].wait()


def pick_rows(route_ref, local):
    doms, per = route_ref.shape
    lane = lax.broadcasted_iota(jnp.int32, (per, local), 1)
    sub = lax.broadcasted_iota(jnp.int32, (per, local), 0)
    tiles = []
    for r in range(doms):
        spot = jnp.zeros((per, local), jnp.int32)
        for j in range(per):
            spot = jnp.where(sub == j, route_ref[r, j], spot)
        tiles.append(jnp.where(lane == spot, 1.0, 0.0))
    return jnp.concatenate(tiles, axis=0).astype(BF16)


def tiles_kernel(route_hbm, x_hbm, out_ref, route, x, sems):
    fetch = Fetch(sems, (route_hbm, route), (x_hbm, x))
    fetch.wait(0, 1)
    out_ref[...] = dot_nn(pick_rows(route, x.shape[0]), x[...]).astype(BF16)


def own_kernel(
    nbr_hbm, rel_hbm, bias_hbm, act_hbm, cot_hbm, x_hbm, w_hbm,
    edge_ref, proj, x, w, load_hbm, nbr, rel, bias, act, cot, flags_s, sems,
):
    heads, rows, keys = edge_ref.shape
    kinds = bias.shape[0]
    snaps, ents, width = cot.shape
    fetch = Fetch(
        sems,
        (cot_hbm, cot),
        (act_hbm, act),
        (nbr_hbm, nbr),
        (rel_hbm, rel),
        (bias_hbm, bias),
        (x_hbm, x),
        (w_hbm, w),
    )
    row = lax.broadcasted_iota(jnp.int32, (ents, ents), 0)
    col = lax.broadcasted_iota(jnp.int32, (ents, ents), 1)
    lane = lax.broadcasted_iota(jnp.int32, (ents, width), 1)
    flags = jnp.zeros((ents, width), F32)
    fetch.wait(1)
    on = act[...].astype(F32)
    for t in range(snaps):
        column = jnp.sum(jnp.where(row == col, on[t : t + 1, :], 0.0), axis=1, keepdims=True)
        flags = jnp.where(lane == t, column, flags)
    flags_s[...] = flags.astype(BF16)
    fetch.wait(0)
    store = Fetch(sems.at[7:], (flags_s, load_hbm.at[snaps]), (cot, load_hbm.at[:snaps]))
    fetch.wait(2, 3, 4)
    counts = edge_counts(nbr, rel, kinds, keys)
    gain = jnp.exp(bias[...])
    for h in range(heads):
        weight = counts[0] * gain[0:1, h : h + 1]
        for r in range(1, kinds):
            weight = weight + counts[r] * gain[r : r + 1, h : h + 1]
        edge_ref[h] = jnp.where(weight > 0, jnp.log(weight), NEG)
    fetch.wait(5, 6)
    for part in range(3):
        cols = slice(part * width, (part + 1) * width)
        proj[:, cols] = dot_nn(x[...], w[:, cols]).astype(BF16)
    store.wait(0, 1)


def fill_table(tab_s, proj, halo, w_kv):
    rows, width = proj.shape[0], halo.shape[1]
    used = rows + halo.shape[0]
    tab_s[:rows, :] = proj[:, width:]
    for part in range(2):
        cols = slice(part * width, (part + 1) * width)
        tab_s[rows:used, cols] = dot_nn(halo[...], w_kv[:, cols]).astype(BF16)
    if tab_s.shape[0] > used:
        tab_s[used:, :] = jnp.zeros((tab_s.shape[0] - used, 2 * width), BF16)


def edge_counts(nbr, rel, kinds, keys):
    bits = 4
    slots, rows = nbr.shape
    target = jnp.transpose(nbr[...].astype(F32))
    one = jnp.transpose(lax.shift_left(jnp.ones_like(rel[...]), bits * rel[...]).astype(F32))
    spot = lax.broadcasted_iota(jnp.int32, (rows, keys), 1).astype(F32)
    packed = jnp.zeros((rows, keys), F32)
    for k in range(slots):
        packed = packed + jnp.where(target[:, k : k + 1] == spot, one[:, k : k + 1], 0.0)
    packed = packed.astype(jnp.int32)
    low = (1 << bits) - 1
    counts = [
        lax.bitwise_and(lax.shift_right_logical(packed, bits * r), low).astype(F32)
        for r in range(kinds)
    ]
    return counts


def edge_attention(p, heads, proj, edge, tab_s, width):
    keys = tab_s.shape[0]
    head_dim = width // heads
    group = LANES // head_dim
    cols = slice(p * LANES, (p + 1) * LANES)
    kk = stack_heads(tab_s[:, cols], head_dim)
    score = dot_nt(proj[:, cols], kk)
    parts = []
    for g in range(group):
        s = score[:, g * keys : (g + 1) * keys] * head_dim ** (-0.5) + edge[p * group + g]
        e = jnp.exp(s - jnp.max(s, axis=1, keepdims=True))
        parts.append(e * (1.0 / jnp.sum(e, axis=1, keepdims=True)))
    return kk, parts


def forward_kernel(heads, x, halo, w, proj, edge, hidden_ref, tab_s):
    width = x.shape[1]
    head_dim = width // heads
    fill_table(tab_s, proj, halo, w.at[:, width:])
    for p in range(width // LANES):
        cols = slice(p * LANES, (p + 1) * LANES)
        vcols = slice(width + p * LANES, width + (p + 1) * LANES)
        _, attn = edge_attention(p, heads, proj, edge, tab_s, width)
        vv = stack_heads(tab_s[:, vcols], head_dim)
        agg = dot_nn(jnp.concatenate([a.astype(BF16) for a in attn], axis=1), vv)
        elu = jnp.where(agg > 0, agg, jnp.exp(jnp.minimum(agg, 0.0)) - 1.0)
        hidden_ref[:, cols] = (x[:, cols].astype(F32) + elu).astype(BF16)


def each(lo, hi, unroll, body):
    if unroll:
        for i in range(lo, hi):
            body(i)
    else:
        lax.fori_loop(lo, hi, lambda i, c: (body(i), c)[1], 0)


def cotangent_kernel(*refs):
    *cot, ct_ref, act_ref = refs
    snaps = len(cot)
    ents = cot[0].shape[1]
    local = snaps * ents
    for m in range(snaps):
        at = pl.multiple_of(lax.bitwise_xor(snap_index(), m) * ents, ents)
        for t in range(snaps):
            ct_ref[pl.ds(t * local + at, ents), :] = cot[m][t].astype(ct_ref.dtype)
        act_ref[pl.ds(at, ents), :] = cot[m][snaps][:, :LANES].astype(F32)


def temporal_kernel(snaps, heads, pieces, pos_ref, w_s, ct_s, act_s, *refs):
    hid = refs[:snaps]
    terms_ref = refs[snaps : snaps + pieces]
    (
        dt_own_ref, cot_own_ref,
        z_s, tp_s, dt_s, prod_s, s_s, d_s, a_s, ds_s, wa_s, wd_s, dk_s, dv_s, terms_s,
    ) = refs[snaps + pieces :]
    local, width = hid[0].shape
    head_dim = width // heads
    scale = head_dim ** (-0.5)
    unroll = snaps <= 4
    me, outer = snap_index(), dom_index() // 2
    pos = pos_ref[...].astype(F32)
    which = lax.broadcasted_iota(jnp.int32, pos.shape, 0)

    def rows_of(t):
        return pl.ds(t * local if isinstance(t, int) else pl.multiple_of(t * local, local), local)

    for n in range(snaps):
        t = lax.bitwise_xor(me, n)
        shift = jnp.sum(jnp.where(which == t, pos, 0.0), axis=0, keepdims=True)
        z_s[rows_of(t), :] = (hid[n][...].astype(F32) + shift).astype(BF16)
    for part in range(3):
        cols = slice(part * width, (part + 1) * width)
        tp_s[:, cols] = dot_nn(z_s[...], w_s[:, cols]).astype(BF16)
    lane_head = lax.broadcasted_iota(jnp.int32, (width, LANES), 0) // head_dim
    fold = (lane_head == lax.broadcasted_iota(jnp.int32, (width, LANES), 1)).astype(F32)
    fold = fold.astype(BF16)
    head_lane = lax.broadcasted_iota(jnp.int32, (LANES, width), 1) // head_dim
    spread = (head_lane == lax.broadcasted_iota(jnp.int32, (LANES, width), 0)).astype(F32)
    spread_scaled = (spread * scale).astype(BF16)
    spread = spread.astype(BF16)
    act = act_s[...]
    snap_lane = lax.broadcasted_iota(jnp.int32, act.shape, 1)
    if not unroll:
        dk_s[...] = jnp.zeros_like(dk_s)
        dv_s[...] = jnp.zeros_like(dv_s)

    def one_snap(t):
        used = (t + 1 if unroll else snaps) * local
        half = snaps * local

        def product(u):
            q, k, v = (
                tp_s[rows_of(i), part * width : (part + 1) * width]
                for part, i in ((0, t), (1, u), (2, u))
            )
            prod_s[rows_of(u), :] = q * k
            prod_s[rows_of(snaps + u), :] = ct_s[rows_of(t), :].astype(BF16) * v

        each(0, t + 1, unroll, product)
        s_s[:used, :] = dot_nn(prod_s[:used, :], fold)
        d_s[:used, :] = dot_nn(prod_s[half : half + used, :], fold).astype(BF16).astype(F32)

        def mask(u):
            on = jnp.sum(jnp.where(snap_lane == u, act, 0.0), axis=1, keepdims=True)
            s_s[rows_of(u), :] = jnp.where((on > 0.5) | (u == t), s_s[rows_of(u), :] * scale, NEG)

        each(0, t + 1, unroll, mask)

        def reduced(fn, start):
            if unroll:
                for u in range(t + 1):
                    start = fn(u, start)
                return start
            return lax.fori_loop(0, t + 1, fn, start)

        top = reduced(
            lambda u, c: jnp.maximum(c, s_s[rows_of(u), :]), jnp.full((local, LANES), NEG, F32)
        )

        def expo(u, total):
            e = jnp.exp(s_s[rows_of(u), :] - top)
            s_s[rows_of(u), :] = e
            return total + e

        inv = 1.0 / reduced(expo, jnp.zeros((local, LANES), F32))

        def weigh(u, total):
            a = s_s[rows_of(u), :] * inv
            s_s[rows_of(u), :] = a
            return total + a * d_s[rows_of(u), :]

        dot = reduced(weigh, jnp.zeros((local, LANES), F32))

        def keep(u):
            a = s_s[rows_of(u), :]
            a_s[rows_of(u), :] = a.astype(BF16)
            ds_s[rows_of(u), :] = (a * (d_s[rows_of(u), :] - dot)).astype(BF16)

        each(0, t + 1, unroll, keep)
        wa_s[:used, :] = dot_nn(a_s[:used, :], spread)
        wd_s[:used, :] = dot_nn(ds_s[:used, :], spread_scaled)

        for p in range(width // LANES):
            c0 = p * LANES
            cols = slice(c0, c0 + LANES)
            q = tp_s[rows_of(t), cols].astype(F32)
            ct = ct_s[rows_of(t), cols].astype(F32)

            def back(u, dq):
                k = tp_s[rows_of(u), width + c0 : width + c0 + LANES].astype(F32)
                wide_ds = wd_s[rows_of(u), cols]
                dk, dv = wide_ds * q, wa_s[rows_of(u), cols] * ct
                if unroll and u == t:
                    dk_s[rows_of(u), cols] = dk
                    dv_s[rows_of(u), cols] = dv
                else:
                    dk_s[rows_of(u), cols] += dk
                    dv_s[rows_of(u), cols] += dv
                return dq + wide_ds * k

            dt_s[rows_of(t), cols] = reduced(back, jnp.zeros_like(q)).astype(BF16)

    each(0, snaps, unroll, one_snap)
    dt_s[:, width : 2 * width] = dk_s[...].astype(BF16)
    dt_s[:, 2 * width :] = dv_s[...].astype(BF16)
    share = width // snaps
    pick = (
        lax.broadcasted_iota(jnp.int32, (width, share), 0)
        == lax.broadcasted_iota(jnp.int32, (width, share), 1) + me * share
    )
    z_mine = dot_nn(z_s[...], pick.astype(F32).astype(BF16)).astype(BF16)
    for part in range(3):
        cols = slice(part * width, (part + 1) * width)
        terms_s[:, cols] = dot_tn(z_mine, dt_s[:, cols]).astype(BF16)
    piece = share // pieces
    for k in range(pieces):
        if pieces == 1:
            terms_ref[k][...] = terms_s[...]
        else:
            at = pl.multiple_of(lax.bitwise_xor(outer, k) * piece, piece)
            terms_ref[k][...] = terms_s[pl.ds(at, piece), :]
    dt_own_ref[...] = dt_s[rows_of(me), :]
    cot_own_ref[...] = ct_s[rows_of(me), :].astype(BF16)


def backward_kernel(
    heads, dt, cot, proj, halo, edge, ws, wt, back_ref, part_ref, tab_s, dq_s, dtab_s,
):
    rows, width = cot.shape
    halo_rows = halo.shape[0]
    keys = tab_s.shape[0]
    head_dim = width // heads
    group = LANES // head_dim
    scale = head_dim ** (-0.5)
    dh = cot[...].astype(F32) + dot_nt(dt[...], wt[...])
    part_ref[...] = dh.astype(BF16).astype(F32)
    fill_table(tab_s, proj, halo, ws.at[:, width:])
    for p in range(width // LANES):
        cols = slice(p * LANES, (p + 1) * LANES)
        vcols = slice(width + p * LANES, width + (p + 1) * LANES)
        kk, attn = edge_attention(p, heads, proj, edge, tab_s, width)
        vv = stack_heads(tab_s[:, vcols], head_dim)
        attn_b = jnp.concatenate([a.astype(BF16) for a in attn], axis=1)
        agg = dot_nn(attn_b, vv)
        da = part_ref[:, cols] * jnp.where(agg > 0, 1.0, jnp.exp(jnp.minimum(agg, 0.0)))
        da = da.astype(BF16)
        dattn = dot_nt(da, vv).astype(BF16).astype(F32)
        ds = []
        for g in range(group):
            ad = attn[g] * dattn[:, g * keys : (g + 1) * keys]
            ds.append((ad - attn[g] * jnp.sum(ad, axis=1, keepdims=True)).astype(BF16))
        ds = jnp.concatenate(ds, axis=1)
        dq_s[:, cols] = (dot_nn(ds, kk) * scale).astype(BF16)
        dtab_s[:, cols] = (unstack_heads(dot_tn(ds, proj[:, cols]), head_dim) * scale).astype(BF16)
        dtab_s[:, vcols] = unstack_heads(dot_tn(attn_b, da), head_dim).astype(BF16)
    back_ref[...] = dot_nt(dtab_s[rows : rows + halo_rows, :], ws[:, width:])
    part_ref[...] += dot_nt(dq_s[...], ws[:, :width]) + dot_nt(dtab_s[:rows, :], ws[:, width:])


def tile_of(flip, back_ref, per):
    at = lax.bitwise_xor(dom_index(), flip) * per
    return back_ref[pl.ds(pl.multiple_of(at, per), per), :]


def outer_sum_kernel(per, back_ref, *refs):
    *terms, out_ref = refs
    wide = terms[0].shape[1]
    total = terms[0][...].astype(F32)
    for term in terms[1:]:
        total = total + term[...].astype(F32)
    out_ref[:, :wide] = total.astype(BF16)
    tiles = [tile_of(2 * k + 1, back_ref, per) for k in range(len(terms))]
    out_ref[:, wide:] = jnp.concatenate(tiles, axis=0).astype(BF16)


def inner_sum_kernel(per, back_ref, mine_ref, other_ref, *out):
    rows = mine_ref.shape[0]
    wide = mine_ref.shape[1] - back_ref.shape[1]
    lanes = out[0].shape[1] - wide
    total = (mine_ref[:, :wide].astype(F32) + other_ref[:, :wide].astype(F32)).astype(BF16)
    passing = other_ref[:, wide:].astype(F32)
    for k in range(len(out)):
        out[k][:, :wide] = total
        both = [tile_of(2 * k, back_ref, per), passing[k * per : (k + 1) * per]]
        folds = [
            tile[:, i * lanes : (i + 1) * lanes]
            for tile in both
            for i in range(rows // (2 * per))
        ]
        out[k][:, wide:] = jnp.concatenate(folds, axis=0).astype(BF16)


def unpack_sums(flips, per, got, wtemp, wtemp_hbm, came_s, sems):
    rows = got[0].shape[0]
    lanes = got[0].shape[1] - wtemp.shape[2]
    folds = rows // (2 * per)
    stores = []
    came_s[...] = jnp.zeros_like(came_s)
    for i, k in enumerate(flips):
        wtemp[i] = got[i][:, : wtemp.shape[2]].astype(F32)
        at = pl.multiple_of(lax.bitwise_xor(dom_index() // 2, k) * rows, rows)
        stores.append(Fetch(sems.at[i:], (wtemp.at[i], wtemp_hbm.at[pl.ds(at, rows), :])))
        folded = got[i][:, wtemp.shape[2] :].astype(F32)
        for j in range(2):
            d = pl.multiple_of(lax.bitwise_xor(dom_index(), 2 * k + j) * per, per)
            for f in range(folds):
                row = (j * folds + f) * per
                came_s[pl.ds(d, per), f * lanes : (f + 1) * lanes] = folded[row : row + per]
    return stores


def early_kernel(flips, per, route_ref, part_ref, *refs):
    got = refs[: len(flips)]
    sum_ref, picks_ref, wtemp_hbm, wtemp, came_s, sems = refs[len(flips) :]
    stores = unpack_sums(flips, per, got, wtemp, wtemp_hbm, came_s, sems)
    picks = pick_rows(route_ref, part_ref.shape[0])
    picks_ref[...] = picks
    sum_ref[...] = part_ref[...] + dot_tn(picks, came_s[...].astype(BF16))
    for store in stores:
        store.wait(0)


def last_kernel(flips, per, picks_ref, sum_ref, _, *refs):
    got = refs[: len(flips)]
    feat_hbm, wtemp_hbm, feat, wtemp, came_s, sems = refs[len(flips) :]
    stores = unpack_sums(flips, per, got, wtemp, wtemp_hbm, came_s, sems)
    feat[...] = (sum_ref[...] + dot_tn(picks_ref[...], came_s[...].astype(BF16))).astype(BF16)
    stores.append(Fetch(sems.at[len(flips) :], (feat, feat_hbm)))
    for store in stores:
        store.wait(0)


def params(mib):
    return pltpu.CompilerParams(vmem_limit_bytes=mib * 1024 * 1024)


def gather_blocks(held, axis, bit, last):
    held = dict(held)
    while bit >= last:
        for m in sorted(held):
            held[m ^ bit] = flipped(held[m], axis, bit)
        bit //= 2
    return held


def in_hbm(*arrays):
    return [pltpu.with_memory_space_constraint(a, pltpu.HBM) for a in arrays]


def exchange(tiles, axis):
    return lax.all_to_all(tiles, axis, split_axis=0, concat_axis=0, tiled=True)


def flipped(block, axis, flip):
    count = lax.axis_size(axis)
    return lax.ppermute(block, axis, [(i, i ^ flip) for i in range(count)])


def per_device(
    feat, w_struct, w_temp, pos_embed, rel_bias, nbr, rel_type, send_idx, active, cotangent
):
    x = feat[0]
    local, width = x.shape
    heads = rel_bias.shape[1]
    slots = nbr.shape[2]
    doms = lax.axis_size("dom")
    snaps = lax.axis_size("snap")
    ents = local // snaps
    route = send_idx[0, 0]
    halo_per = route.shape[1]
    halo_rows = doms * halo_per
    keys = -(-(local + halo_rows) // LANES) * LANES
    share = width // snaps
    pieces = doms // 2
    piece = share // pieces
    lanes = 2 * halo_per * width // piece if piece else 0
    paired = (
        doms % 2 == 0
        and doms & (doms - 1) == 0
        and piece == pieces * halo_per
        and piece % 16 == 0
        and lanes % LANES == 0
        and lanes > 0
    )
    if not paired:
        pieces = 1

    def shape(*dims, dtype=BF16):
        return jax.ShapeDtypeStruct(dims, dtype)

    def vmem(*dims, dtype=BF16):
        return pltpu.VMEM(dims, dtype)

    def hbm(*dims, dtype=BF16):
        return pltpu.HBM(dims, dtype)

    tiles = pl.pallas_call(
        tiles_kernel,
        out_shape=shape(halo_rows, width),
        in_specs=[HBM, HBM],
        out_specs=VMEM,
        scratch_shapes=[
            pltpu.SMEM(route.shape, jnp.int32),
            pltpu.VMEM((local, width), BF16),
            pltpu.SemaphoreType.DMA((2,)),
        ],
        compiler_params=params(8),
        name="halo_tiles",
    )(*in_hbm(route, x))
    halo = exchange(tiles.reshape(doms, halo_per, width), "dom").reshape(halo_rows, width)

    edge, proj, x_near, w_near, load = pl.pallas_call(
        own_kernel,
        out_shape=(
            vmem(heads, local, keys, dtype=F32),
            vmem(local, 3 * width),
            vmem(local, width),
            vmem(*w_struct.shape),
            hbm(snaps + 1, ents, width),
        ),
        in_specs=[HBM] * 7,
        out_specs=(VMEM,) * 4 + (HBM,),
        scratch_shapes=[
            pltpu.VMEM((slots, local), jnp.int32),
            pltpu.VMEM((slots, local), jnp.int32),
            pltpu.VMEM(rel_bias.shape, F32),
            pltpu.VMEM((snaps, ents), jnp.int32),
            pltpu.VMEM((snaps, ents, width), BF16),
            pltpu.VMEM((ents, width), BF16),
            pltpu.SemaphoreType.DMA((9,)),
        ],
        compiler_params=params(8),
        cost_estimate=pl.CostEstimate(flops=10**9, bytes_accessed=4 * 10**6, transcendentals=0),
        name="own_rows",
    )(
        *in_hbm(nbr[0].T, rel_type[0].T, rel_bias, active, cotangent, x, w_struct),
    )
    cots = gather_blocks({0: load}, "snap", snaps // 2, 1)
    cots = [cots[m] for m in range(snaps)]

    hidden = pl.pallas_call(
        functools.partial(forward_kernel, heads),
        out_shape=shape(local, width),
        in_specs=[VMEM] * 5,
        out_specs=VMEM,
        scratch_shapes=[pltpu.VMEM((keys, 2 * width), BF16)],
        compiler_params=params(8),
        name="struct_forward",
    )(x_near, halo, w_near, proj, edge)

    hids = gather_blocks({0: hidden}, "snap", snaps // 2, 1)
    hids = [hids[m] for m in range(snaps)]
    every = snaps * local
    ct, act = pl.pallas_call(
        cotangent_kernel,
        out_shape=(
            shape(every, width, dtype=F32 if ents % 16 else BF16),
            shape(local, LANES, dtype=F32),
        ),
        in_specs=[VMEM] * snaps,
        out_specs=(VMEM, VMEM),
        compiler_params=params(8),
        name="cotangents",
    )(*cots)
    *terms, dt_own, cot_own = pl.pallas_call(
        functools.partial(temporal_kernel, snaps, heads, pieces),
        out_shape=(shape(share // pieces, 3 * width),) * pieces
        + (shape(local, 3 * width), shape(local, width)),
        in_specs=[VMEM] * (4 + snaps),
        out_specs=(VMEM,) * (pieces + 2),
        scratch_shapes=[
            pltpu.VMEM((every, width), BF16),
            pltpu.VMEM((every, 3 * width), BF16),
            pltpu.VMEM((every, 3 * width), BF16),
            pltpu.VMEM((2 * every, width), BF16),
            pltpu.VMEM((every, LANES), F32),
            pltpu.VMEM((every, LANES), F32),
            pltpu.VMEM((every, LANES), BF16),
            pltpu.VMEM((every, LANES), BF16),
            pltpu.VMEM((every, width), F32),
            pltpu.VMEM((every, width), F32),
            pltpu.VMEM((every, width), F32),
            pltpu.VMEM((every, width), F32),
            pltpu.VMEM((share, 3 * width), BF16),
        ],
        compiler_params=params(24 if snaps <= 4 else 56),
        name="temporal",
    )(pos_embed, w_temp, ct, act, *hids)

    if paired:
        got = [terms[0]] + [flipped(terms[k], "dom", 2 * k) for k in range(1, pieces)]
    else:
        got = exchange(terms[0].reshape(doms, share // doms, 3 * width), "dom")
    back, partial = pl.pallas_call(
        functools.partial(backward_kernel, heads),
        out_shape=(shape(halo_rows, width, dtype=F32), shape(local, width, dtype=F32)),
        in_specs=[VMEM] * 7,
        out_specs=(VMEM, VMEM),
        scratch_shapes=[
            pltpu.VMEM((keys, 2 * width), BF16),
            pltpu.VMEM((local, width), BF16),
            pltpu.VMEM((keys, 2 * width), BF16),
        ],
        compiler_params=params(16),
        cost_estimate=pl.CostEstimate(flops=2 * 10**9, bytes_accessed=8 * 10**6, transcendentals=0),
        name="struct_backward",
    )(dt_own, cot_own, proj, halo, edge, w_near, w_temp)

    if not paired:
        total = jnp.sum(got.astype(F32), axis=0).astype(BF16)
        full = exchange(jnp.broadcast_to(total[None], (doms,) + total.shape), "dom")
        grad_wtemp = full.astype(F32).reshape(share, 3 * width)
        came = exchange(back.astype(BF16).reshape(doms, halo_per, width), "dom")
        picks = (route.reshape(-1)[:, None] == jnp.arange(local, dtype=jnp.int32)).astype(BF16)
        sums = dot_tn(picks, came.reshape(halo_rows, width))
        return ((partial + sums).astype(BF16)[None], grad_wtemp)

    mine = pl.pallas_call(
        functools.partial(outer_sum_kernel, halo_per),
        out_shape=shape(piece, 4 * width),
        in_specs=[VMEM] * (1 + pieces),
        out_specs=VMEM,
        compiler_params=params(8),
        name="outer_sum",
    )(back, *got)
    other = flipped(mine, "dom", 1)
    sums = pl.pallas_call(
        functools.partial(inner_sum_kernel, halo_per),
        out_shape=(shape(piece, 3 * width + lanes),) * pieces,
        in_specs=[VMEM] * 3,
        out_specs=(VMEM,) * pieces,
        compiler_params=params(8),
        name="inner_sum",
    )(back, mine, other)
    sums = [sums[0]] + [flipped(sums[k], "dom", 2 * k) for k in range(1, pieces)]
    soon, late = list(range(pieces // 2)), list(range(pieces // 2, pieces))
    partial, picks, grad_wtemp = pl.pallas_call(
        functools.partial(early_kernel, soon, halo_per),
        out_shape=(
            shape(local, width, dtype=F32),
            shape(halo_rows, local),
            hbm(share, 3 * width, dtype=F32),
        ),
        in_specs=[SMEM] + [VMEM] * (1 + len(soon)),
        out_specs=(VMEM, VMEM, HBM),
        scratch_shapes=[
            pltpu.VMEM((len(soon), piece, 3 * width), F32),
            pltpu.VMEM((halo_rows, width), F32),
            pltpu.SemaphoreType.DMA((len(soon),)),
        ],
        compiler_params=params(8),
        name="early_sums",
    )(route, partial, *[sums[k] for k in soon])
    grad_feat, grad_wtemp = pl.pallas_call(
        functools.partial(last_kernel, late, halo_per),
        out_shape=(hbm(local, width), hbm(share, 3 * width, dtype=F32)),
        in_specs=[VMEM] * 2 + [HBM] + [VMEM] * len(late),
        out_specs=(HBM, HBM),
        scratch_shapes=[
            pltpu.VMEM((local, width), BF16),
            pltpu.VMEM((len(late), piece, 3 * width), F32),
            pltpu.VMEM((halo_rows, width), F32),
            pltpu.SemaphoreType.DMA((len(late) + 1,)),
        ],
        input_output_aliases={2: 1},
        compiler_params=params(8),
        name="last_sums",
    )(picks, partial, *in_hbm(grad_wtemp), *[sums[k] for k in late])
    return (grad_feat[None], grad_wtemp)


def solution(mesh):
    return jax.shard_map(
        per_device,
        mesh=mesh,
        in_specs=(
            P("snap", "dom", None),
            P(),
            P(),
            P(),
            P(),
            P("snap", "dom", None),
            P("snap", "dom", None),
            P("snap", "dom", None, None),
            P(None, ("dom", "snap")),
            P(None, ("dom", "snap"), None),
        ),
        out_specs=(P("snap", "dom", None), P("snap", None)),
        check_vma=False,
    )
```

```python
import functools

import jax
import jax.numpy as jnp
from jax import lax
from jax.experimental import pallas as pl
from jax.experimental.pallas import tpu as pltpu
from jax.sharding import PartitionSpec as P

F32 = jnp.float32
BF16 = jnp.bfloat16
LANES = 128
NEG = -1e30
VMEM = pl.BlockSpec(memory_space=pltpu.VMEM)
SMEM = pl.BlockSpec(memory_space=pltpu.SMEM)
HBM = pl.BlockSpec(memory_space=pltpu.HBM)


def snap_index():
    return lax.axis_index("snap")


def dom_index():
    return lax.axis_index("dom")


def dot_nn(a, b):
    return lax.dot_general(a, b, (((1,), (0,)), ((), ())), preferred_element_type=F32)


def dot_nt(a, b):
    return lax.dot_general(a, b, (((1,), (1,)), ((), ())), preferred_element_type=F32)


def dot_tn(a, b):
    return lax.dot_general(a, b, (((0,), (0,)), ((), ())), preferred_element_type=F32)


def stack_heads(block, head_dim):
    rows, lanes = block.shape
    head = lax.broadcasted_iota(jnp.int32, (rows, lanes), 1) // head_dim
    zero = jnp.zeros_like(block)
    return jnp.concatenate(
        [jnp.where(head == g, block, zero) for g in range(lanes // head_dim)], axis=0
    )


def unstack_heads(stacked, head_dim):
    lanes = stacked.shape[1]
    groups = lanes // head_dim
    rows = stacked.shape[0] // groups
    head = lax.broadcasted_iota(jnp.int32, (rows, lanes), 1) // head_dim
    out = stacked[:rows]
    for g in range(1, groups):
        out = jnp.where(head == g, stacked[g * rows : (g + 1) * rows], out)
    return out


class Fetch:

    def __init__(self, sems, *pairs):
        self.copies = [
            pltpu.make_async_copy(src, dst, sems.at[i]) for i, (src, dst) in enumerate(pairs)
        ]
        for copy in self.copies:
            copy.start()

    def wait(self, *which):
        for i in which:
            self.copies[i].wait()


def pick_rows(route_ref, local):
    doms, per = route_ref.shape
    lane = lax.broadcasted_iota(jnp.int32, (per, local), 1)
    sub = lax.broadcasted_iota(jnp.int32, (per, local), 0)
    tiles = []
    for r in range(doms):
        spot = jnp.zeros((per, local), jnp.int32)
        for j in range(per):
            spot = jnp.where(sub == j, route_ref[r, j], spot)
        tiles.append(jnp.where(lane == spot, 1.0, 0.0))
    return jnp.concatenate(tiles, axis=0).astype(BF16)


def tiles_kernel(route_hbm, x_hbm, out_ref, route, x, sems):
    fetch = Fetch(sems, (route_hbm, route), (x_hbm, x))
    fetch.wait(0, 1)
    out_ref[...] = dot_nn(pick_rows(route, x.shape[0]), x[...]).astype(BF16)


def own_kernel(
    nbr_hbm, rel_hbm, bias_hbm, act_hbm, cot_hbm, x_hbm, w_hbm,
    edge_ref, proj, x, w, load_hbm, nbr, rel, bias, act, cot, flags_s, sems,
):
    heads, rows, keys = edge_ref.shape
    kinds = bias.shape[0]
    snaps, ents, width = cot.shape
    fetch = Fetch(
        sems,
        (cot_hbm, cot),
        (act_hbm, act),
        (nbr_hbm, nbr),
        (rel_hbm, rel),
        (bias_hbm, bias),
        (x_hbm, x),
        (w_hbm, w),
    )
    row = lax.broadcasted_iota(jnp.int32, (ents, ents), 0)
    col = lax.broadcasted_iota(jnp.int32, (ents, ents), 1)
    lane = lax.broadcasted_iota(jnp.int32, (ents, width), 1)
    flags = jnp.zeros((ents, width), F32)
    fetch.wait(1)
    on = act[...].astype(F32)
    for t in range(snaps):
        column = jnp.sum(jnp.where(row == col, on[t : t + 1, :], 0.0), axis=1, keepdims=True)
        flags = jnp.where(lane == t, column, flags)
    flags_s[...] = flags.astype(BF16)
    fetch.wait(0)
    store = Fetch(sems.at[7:], (flags_s, load_hbm.at[snaps]), (cot, load_hbm.at[:snaps]))
    fetch.wait(2, 3, 4)
    counts = edge_counts(nbr, rel, kinds, keys)
    gain = jnp.exp(bias[...])
    for h in range(heads):
        weight = counts[0] * gain[0:1, h : h + 1]
        for r in range(1, kinds):
            weight = weight + counts[r] * gain[r : r + 1, h : h + 1]
        edge_ref[h] = jnp.where(weight > 0, jnp.log(weight), NEG)
    fetch.wait(5, 6)
    for part in range(3):
        cols = slice(part * width, (part + 1) * width)
        proj[:, cols] = dot_nn(x[...], w[:, cols]).astype(BF16)
    store.wait(0, 1)


def fill_table(tab_s, proj, halo, w_kv):
    rows, width = proj.shape[0], halo.shape[1]
    used = rows + halo.shape[0]
    tab_s[:rows, :] = proj[:, width:]
    for part in range(2):
        cols = slice(part * width, (part + 1) * width)
        tab_s[rows:used, cols] = dot_nn(halo[...], w_kv[:, cols]).astype(BF16)
    if tab_s.shape[0] > used:
        tab_s[used:, :] = jnp.zeros((tab_s.shape[0] - used, 2 * width), BF16)


def edge_counts(nbr, rel, kinds, keys):
    bits = 4
    slots, rows = nbr.shape
    target = jnp.transpose(nbr[...].astype(F32))
    one = jnp.transpose(lax.shift_left(jnp.ones_like(rel[...]), bits * rel[...]).astype(F32))
    spot = lax.broadcasted_iota(jnp.int32, (rows, keys), 1).astype(F32)
    packed = jnp.zeros((rows, keys), F32)
    for k in range(slots):
        packed = packed + jnp.where(target[:, k : k + 1] == spot, one[:, k : k + 1], 0.0)
    packed = packed.astype(jnp.int32)
    low = (1 << bits) - 1
    counts = [
        lax.bitwise_and(lax.shift_right_logical(packed, bits * r), low).astype(F32)
        for r in range(kinds)
    ]
    return counts


def edge_attention(p, heads, proj, edge, tab_s, width):
    keys = tab_s.shape[0]
    head_dim = width // heads
    group = LANES // head_dim
    cols = slice(p * LANES, (p + 1) * LANES)
    kk = stack_heads(tab_s[:, cols], head_dim)
    score = dot_nt(proj[:, cols], kk)
    parts = []
    for g in range(group):
        s = score[:, g * keys : (g + 1) * keys] * head_dim ** (-0.5) + edge[p * group + g]
        e = jnp.exp(s - jnp.max(s, axis=1, keepdims=True))
        parts.append(e * (1.0 / jnp.sum(e, axis=1, keepdims=True)))
    return kk, parts


def forward_kernel(heads, x, halo, w, proj, edge, hidden_ref, tab_s):
    width = x.shape[1]
    head_dim = width // heads
    fill_table(tab_s, proj, halo, w.at[:, width:])
    for p in range(width // LANES):
        cols = slice(p * LANES, (p + 1) * LANES)
        vcols = slice(width + p * LANES, width + (p + 1) * LANES)
        _, attn = edge_attention(p, heads, proj, edge, tab_s, width)
        vv = stack_heads(tab_s[:, vcols], head_dim)
        agg = dot_nn(jnp.concatenate([a.astype(BF16) for a in attn], axis=1), vv)
        elu = jnp.where(agg > 0, agg, jnp.exp(jnp.minimum(agg, 0.0)) - 1.0)
        hidden_ref[:, cols] = (x[:, cols].astype(F32) + elu).astype(BF16)


def each(lo, hi, unroll, body):
    if unroll:
        for i in range(lo, hi):
            body(i)
    else:
        lax.fori_loop(lo, hi, lambda i, c: (body(i), c)[1], 0)


def cotangent_kernel(*refs):
    *cot, ct_ref, act_ref = refs
    snaps = len(cot)
    ents = cot[0].shape[1]
    local = snaps * ents
    for m in range(snaps):
        at = pl.multiple_of(lax.bitwise_xor(snap_index(), m) * ents, ents)
        for t in range(snaps):
            ct_ref[pl.ds(t * local + at, ents), :] = cot[m][t].astype(ct_ref.dtype)
        act_ref[pl.ds(at, ents), :] = cot[m][snaps][:, :LANES].astype(F32)


def temporal_kernel(snaps, heads, pieces, pos_ref, w_s, ct_s, act_s, *refs):
    hid = refs[:snaps]
    terms_ref = refs[snaps : snaps + pieces]
    (
        dt_own_ref, cot_own_ref,
        z_s, tp_s, dt_s, prod_s, s_s, d_s, a_s, ds_s, wa_s, wd_s, dk_s, dv_s, terms_s,
    ) = refs[snaps + pieces :]
    local, width = hid[0].shape
    head_dim = width // heads
    scale = head_dim ** (-0.5)
    unroll = snaps <= 4
    me, outer = snap_index(), dom_index() // 2
    pos = pos_ref[...].astype(F32)
    which = lax.broadcasted_iota(jnp.int32, pos.shape, 0)

    def rows_of(t):
        return pl.ds(t * local if isinstance(t, int) else pl.multiple_of(t * local, local), local)

    for n in range(snaps):
        t = lax.bitwise_xor(me, n)
        shift = jnp.sum(jnp.where(which == t, pos, 0.0), axis=0, keepdims=True)
        z_s[rows_of(t), :] = (hid[n][...].astype(F32) + shift).astype(BF16)
    for part in range(3):
        cols = slice(part * width, (part + 1) * width)
        tp_s[:, cols] = dot_nn(z_s[...], w_s[:, cols]).astype(BF16)
    lane_head = lax.broadcasted_iota(jnp.int32, (width, LANES), 0) // head_dim
    fold = (lane_head == lax.broadcasted_iota(jnp.int32, (width, LANES), 1)).astype(F32)
    fold = fold.astype(BF16)
    head_lane = lax.broadcasted_iota(jnp.int32, (LANES, width), 1) // head_dim
    spread = (head_lane == lax.broadcasted_iota(jnp.int32, (LANES, width), 0)).astype(F32)
    spread_scaled = (spread * scale).astype(BF16)
    spread = spread.astype(BF16)
    act = act_s[...]
    snap_lane = lax.broadcasted_iota(jnp.int32, act.shape, 1)
    if not unroll:
        dk_s[...] = jnp.zeros_like(dk_s)
        dv_s[...] = jnp.zeros_like(dv_s)

    def one_snap(t):
        used = (t + 1 if unroll else snaps) * local
        half = snaps * local

        def product(u):
            q, k, v = (
                tp_s[rows_of(i), part * width : (part + 1) * width]
                for part, i in ((0, t), (1, u), (2, u))
            )
            prod_s[rows_of(u), :] = q * k
            prod_s[rows_of(snaps + u), :] = ct_s[rows_of(t), :].astype(BF16) * v

        each(0, t + 1, unroll, product)
        s_s[:used, :] = dot_nn(prod_s[:used, :], fold)
        d_s[:used, :] = dot_nn(prod_s[half : half + used, :], fold).astype(BF16).astype(F32)

        def mask(u):
            on = jnp.sum(jnp.where(snap_lane == u, act, 0.0), axis=1, keepdims=True)
            s_s[rows_of(u), :] = jnp.where((on > 0.5) | (u == t), s_s[rows_of(u), :] * scale, NEG)

        each(0, t + 1, unroll, mask)

        def reduced(fn, start):
            if unroll:
                for u in range(t + 1):
                    start = fn(u, start)
                return start
            return lax.fori_loop(0, t + 1, fn, start)

        top = reduced(
            lambda u, c: jnp.maximum(c, s_s[rows_of(u), :]), jnp.full((local, LANES), NEG, F32)
        )

        def expo(u, total):
            e = jnp.exp(s_s[rows_of(u), :] - top)
            s_s[rows_of(u), :] = e
            return total + e

        inv = 1.0 / reduced(expo, jnp.zeros((local, LANES), F32))

        def weigh(u, total):
            a = s_s[rows_of(u), :] * inv
            s_s[rows_of(u), :] = a
            return total + a * d_s[rows_of(u), :]

        dot = reduced(weigh, jnp.zeros((local, LANES), F32))

        def keep(u):
            a = s_s[rows_of(u), :]
            a_s[rows_of(u), :] = a.astype(BF16)
            ds_s[rows_of(u), :] = (a * (d_s[rows_of(u), :] - dot)).astype(BF16)

        each(0, t + 1, unroll, keep)
        wa_s[:used, :] = dot_nn(a_s[:used, :], spread)
        wd_s[:used, :] = dot_nn(ds_s[:used, :], spread_scaled)

        for p in range(width // LANES):
            c0 = p * LANES
            cols = slice(c0, c0 + LANES)
            q = tp_s[rows_of(t), cols].astype(F32)
            ct = ct_s[rows_of(t), cols].astype(F32)

            def back(u, dq):
                k = tp_s[rows_of(u), width + c0 : width + c0 + LANES].astype(F32)
                wide_ds = wd_s[rows_of(u), cols]
                dk, dv = wide_ds * q, wa_s[rows_of(u), cols] * ct
                if unroll and u == t:
                    dk_s[rows_of(u), cols] = dk
                    dv_s[rows_of(u), cols] = dv
                else:
                    dk_s[rows_of(u), cols] += dk
                    dv_s[rows_of(u), cols] += dv
                return dq + wide_ds * k

            dt_s[rows_of(t), cols] = reduced(back, jnp.zeros_like(q)).astype(BF16)

    each(0, snaps, unroll, one_snap)
    dt_s[:, width : 2 * width] = dk_s[...].astype(BF16)
    dt_s[:, 2 * width :] = dv_s[...].astype(BF16)
    share = width // snaps
    pick = (
        lax.broadcasted_iota(jnp.int32, (width, share), 0)
        == lax.broadcasted_iota(jnp.int32, (width, share), 1) + me * share
    )
    z_mine = dot_nn(z_s[...], pick.astype(F32).astype(BF16)).astype(BF16)
    for part in range(3):
        cols = slice(part * width, (part + 1) * width)
        terms_s[:, cols] = dot_tn(z_mine, dt_s[:, cols]).astype(BF16)
    piece = share // pieces
    for k in range(pieces):
        if pieces == 1:
            terms_ref[k][...] = terms_s[...]
        else:
            at = pl.multiple_of(lax.bitwise_xor(outer, k) * piece, piece)
            terms_ref[k][...] = terms_s[pl.ds(at, piece), :]
    dt_own_ref[...] = dt_s[rows_of(me), :]
    cot_own_ref[...] = ct_s[rows_of(me), :].astype(BF16)


def backward_kernel(
    heads, dt, cot, proj, halo, edge, ws, wt, back_ref, part_ref, tab_s, dq_s, dtab_s,
):
    rows, width = cot.shape
    halo_rows = halo.shape[0]
    keys = tab_s.shape[0]
    head_dim = width // heads
    group = LANES // head_dim
    scale = head_dim ** (-0.5)
    dh = cot[...].astype(F32) + dot_nt(dt[...], wt[...])
    part_ref[...] = dh.astype(BF16).astype(F32)
    fill_table(tab_s, proj, halo, ws.at[:, width:])
    for p in range(width // LANES):
        cols = slice(p * LANES, (p + 1) * LANES)
        vcols = slice(width + p * LANES, width + (p + 1) * LANES)
        kk, attn = edge_attention(p, heads, proj, edge, tab_s, width)
        vv = stack_heads(tab_s[:, vcols], head_dim)
        attn_b = jnp.concatenate([a.astype(BF16) for a in attn], axis=1)
        agg = dot_nn(attn_b, vv)
        da = part_ref[:, cols] * jnp.where(agg > 0, 1.0, jnp.exp(jnp.minimum(agg, 0.0)))
        da = da.astype(BF16)
        dattn = dot_nt(da, vv).astype(BF16).astype(F32)
        ds = []
        for g in range(group):
            ad = attn[g] * dattn[:, g * keys : (g + 1) * keys]
            ds.append((ad - attn[g] * jnp.sum(ad, axis=1, keepdims=True)).astype(BF16))
        ds = jnp.concatenate(ds, axis=1)
        dq_s[:, cols] = (dot_nn(ds, kk) * scale).astype(BF16)
        dtab_s[:, cols] = (unstack_heads(dot_tn(ds, proj[:, cols]), head_dim) * scale).astype(BF16)
        dtab_s[:, vcols] = unstack_heads(dot_tn(attn_b, da), head_dim).astype(BF16)
    back_ref[...] = dot_nt(dtab_s[rows : rows + halo_rows, :], ws[:, width:])
    part_ref[...] += dot_nt(dq_s[...], ws[:, :width]) + dot_nt(dtab_s[:rows, :], ws[:, width:])


def tile_of(flip, back_ref, per):
    at = lax.bitwise_xor(dom_index(), flip) * per
    return back_ref[pl.ds(pl.multiple_of(at, per), per), :]


def outer_sum_kernel(per, back_ref, *refs):
    *terms, out_ref = refs
    wide = terms[0].shape[1]
    total = terms[0][...].astype(F32)
    for term in terms[1:]:
        total = total + term[...].astype(F32)
    out_ref[:, :wide] = total.astype(BF16)
    tiles = [tile_of(2 * k + 1, back_ref, per) for k in range(len(terms))]
    out_ref[:, wide:] = jnp.concatenate(tiles, axis=0).astype(BF16)


def inner_sum_kernel(per, back_ref, mine_ref, other_ref, *out):
    rows = mine_ref.shape[0]
    wide = mine_ref.shape[1] - back_ref.shape[1]
    lanes = out[0].shape[1] - wide
    total = (mine_ref[:, :wide].astype(F32) + other_ref[:, :wide].astype(F32)).astype(BF16)
    passing = other_ref[:, wide:].astype(F32)
    for k in range(len(out)):
        out[k][:, :wide] = total
        both = [tile_of(2 * k, back_ref, per), passing[k * per : (k + 1) * per]]
        folds = [
            tile[:, i * lanes : (i + 1) * lanes]
            for tile in both
            for i in range(rows // (2 * per))
        ]
        out[k][:, wide:] = jnp.concatenate(folds, axis=0).astype(BF16)


def unpack_sums(flips, per, got, wtemp, wtemp_hbm, came_s, sems):
    rows = got[0].shape[0]
    lanes = got[0].shape[1] - wtemp.shape[2]
    folds = rows // (2 * per)
    stores = []
    came_s[...] = jnp.zeros_like(came_s)
    for i, k in enumerate(flips):
        wtemp[i] = got[i][:, : wtemp.shape[2]].astype(F32)
        at = pl.multiple_of(lax.bitwise_xor(dom_index() // 2, k) * rows, rows)
        stores.append(Fetch(sems.at[i:], (wtemp.at[i], wtemp_hbm.at[pl.ds(at, rows), :])))
        folded = got[i][:, wtemp.shape[2] :].astype(F32)
        for j in range(2):
            d = pl.multiple_of(lax.bitwise_xor(dom_index(), 2 * k + j) * per, per)
            for f in range(folds):
                row = (j * folds + f) * per
                came_s[pl.ds(d, per), f * lanes : (f + 1) * lanes] = folded[row : row + per]
    return stores


def early_kernel(flips, per, route_ref, part_ref, *refs):
    got = refs[: len(flips)]
    sum_ref, picks_ref, wtemp_hbm, wtemp, came_s, sems = refs[len(flips) :]
    stores = unpack_sums(flips, per, got, wtemp, wtemp_hbm, came_s, sems)
    picks = pick_rows(route_ref, part_ref.shape[0])
    picks_ref[...] = picks
    sum_ref[...] = part_ref[...] + dot_tn(picks, came_s[...].astype(BF16))
    for store in stores:
        store.wait(0)


def last_kernel(flips, per, picks_ref, sum_ref, _, *refs):
    got = refs[: len(flips)]
    feat_hbm, wtemp_hbm, feat, wtemp, came_s, sems = refs[len(flips) :]
    stores = unpack_sums(flips, per, got, wtemp, wtemp_hbm, came_s, sems)
    feat[...] = (sum_ref[...] + dot_tn(picks_ref[...], came_s[...].astype(BF16))).astype(BF16)
    stores.append(Fetch(sems.at[len(flips) :], (feat, feat_hbm)))
    for store in stores:
        store.wait(0)


def params(mib):
    return pltpu.CompilerParams(vmem_limit_bytes=mib * 1024 * 1024)


def gather_blocks(held, axis, bit, last):
    held = dict(held)
    while bit >= last:
        for m in sorted(held):
            held[m ^ bit] = flipped(held[m], axis, bit)
        bit //= 2
    return held


def in_hbm(*arrays):
    return [pltpu.with_memory_space_constraint(a, pltpu.HBM) for a in arrays]


def exchange(tiles, axis):
    return lax.all_to_all(tiles, axis, split_axis=0, concat_axis=0, tiled=True)


def flipped(block, axis, flip):
    count = lax.axis_size(axis)
    return lax.ppermute(block, axis, [(i, i ^ flip) for i in range(count)])


def per_device(
    feat, w_struct, w_temp, pos_embed, rel_bias, nbr, rel_type, send_idx, active, cotangent
):
    x = feat[0]
    local, width = x.shape
    heads = rel_bias.shape[1]
    slots = nbr.shape[2]
    doms = lax.axis_size("dom")
    snaps = lax.axis_size("snap")
    ents = local // snaps
    route = send_idx[0, 0]
    halo_per = route.shape[1]
    halo_rows = doms * halo_per
    keys = -(-(local + halo_rows) // LANES) * LANES
    share = width // snaps
    pieces = doms // 2
    piece = share // pieces
    lanes = 2 * halo_per * width // piece if piece else 0
    paired = (
        doms % 2 == 0
        and doms & (doms - 1) == 0
        and piece == pieces * halo_per
        and piece % 16 == 0
        and lanes % LANES == 0
        and lanes > 0
    )
    if not paired:
        pieces = 1

    def shape(*dims, dtype=BF16):
        return jax.ShapeDtypeStruct(dims, dtype)

    def vmem(*dims, dtype=BF16):
        return pltpu.VMEM(dims, dtype)

    def hbm(*dims, dtype=BF16):
        return pltpu.HBM(dims, dtype)

    tiles = pl.pallas_call(
        tiles_kernel,
        out_shape=shape(halo_rows, width),
        in_specs=[HBM, HBM],
        out_specs=VMEM,
        scratch_shapes=[
            pltpu.SMEM(route.shape, jnp.int32),
            pltpu.VMEM((local, width), BF16),
            pltpu.SemaphoreType.DMA((2,)),
        ],
        compiler_params=params(8),
        name="halo_tiles",
    )(*in_hbm(route, x))
    halo = exchange(tiles.reshape(doms, halo_per, width), "dom").reshape(halo_rows, width)

    edge, proj, x_near, w_near, load = pl.pallas_call(
        own_kernel,
        out_shape=(
            vmem(heads, local, keys, dtype=F32),
            vmem(local, 3 * width),
            vmem(local, width),
            vmem(*w_struct.shape),
            hbm(snaps + 1, ents, width),
        ),
        in_specs=[HBM] * 7,
        out_specs=(VMEM,) * 4 + (HBM,),
        scratch_shapes=[
            pltpu.VMEM((slots, local), jnp.int32),
            pltpu.VMEM((slots, local), jnp.int32),
            pltpu.VMEM(rel_bias.shape, F32),
            pltpu.VMEM((snaps, ents), jnp.int32),
            pltpu.VMEM((snaps, ents, width), BF16),
            pltpu.VMEM((ents, width), BF16),
            pltpu.SemaphoreType.DMA((9,)),
        ],
        compiler_params=params(8),
        cost_estimate=pl.CostEstimate(flops=10**9, bytes_accessed=4 * 10**6, transcendentals=0),
        name="own_rows",
    )(
        *in_hbm(nbr[0].T, rel_type[0].T, rel_bias, active, cotangent, x, w_struct),
    )
    cots = gather_blocks({0: load}, "snap", snaps // 2, 1)
    cots = [cots[m] for m in range(snaps)]

    hidden = pl.pallas_call(
        functools.partial(forward_kernel, heads),
        out_shape=shape(local, width),
        in_specs=[VMEM] * 5,
        out_specs=VMEM,
        scratch_shapes=[pltpu.VMEM((keys, 2 * width), BF16)],
        compiler_params=params(8),
        name="struct_forward",
    )(x_near, halo, w_near, proj, edge)

    hids = gather_blocks({0: hidden}, "snap", snaps // 2, 1)
    hids = [hids[m] for m in range(snaps)]
    every = snaps * local
    ct, act = pl.pallas_call(
        cotangent_kernel,
        out_shape=(
            shape(every, width, dtype=F32 if ents % 16 else BF16),
            shape(local, LANES, dtype=F32),
        ),
        in_specs=[VMEM] * snaps,
        out_specs=(VMEM, VMEM),
        compiler_params=params(8),
        name="cotangents",
    )(*cots)
    *terms, dt_own, cot_own = pl.pallas_call(
        functools.partial(temporal_kernel, snaps, heads, pieces),
        out_shape=(shape(share // pieces, 3 * width),) * pieces
        + (shape(local, 3 * width), shape(local, width)),
        in_specs=[VMEM] * (4 + snaps),
        out_specs=(VMEM,) * (pieces + 2),
        scratch_shapes=[
            pltpu.VMEM((every, width), BF16),
            pltpu.VMEM((every, 3 * width), BF16),
            pltpu.VMEM((every, 3 * width), BF16),
            pltpu.VMEM((2 * every, width), BF16),
            pltpu.VMEM((every, LANES), F32),
            pltpu.VMEM((every, LANES), F32),
            pltpu.VMEM((every, LANES), BF16),
            pltpu.VMEM((every, LANES), BF16),
            pltpu.VMEM((every, width), F32),
            pltpu.VMEM((every, width), F32),
            pltpu.VMEM((every, width), F32),
            pltpu.VMEM((every, width), F32),
            pltpu.VMEM((share, 3 * width), BF16),
        ],
        compiler_params=params(24 if snaps <= 4 else 56),
        name="temporal",
    )(pos_embed, w_temp, ct, act, *hids)

    if paired:
        got = [terms[0]] + [flipped(terms[k], "dom", 2 * k) for k in range(pieces - 1, 0, -1)]
    else:
        got = exchange(terms[0].reshape(doms, share // doms, 3 * width), "dom")
    back, partial = pl.pallas_call(
        functools.partial(backward_kernel, heads),
        out_shape=(shape(halo_rows, width, dtype=F32), shape(local, width, dtype=F32)),
        in_specs=[VMEM] * 7,
        out_specs=(VMEM, VMEM),
        scratch_shapes=[
            pltpu.VMEM((keys, 2 * width), BF16),
            pltpu.VMEM((local, width), BF16),
            pltpu.VMEM((keys, 2 * width), BF16),
        ],
        compiler_params=params(16),
        cost_estimate=pl.CostEstimate(flops=2 * 10**9, bytes_accessed=8 * 10**6, transcendentals=0),
        name="struct_backward",
    )(dt_own, cot_own, proj, halo, edge, w_near, w_temp)

    if not paired:
        total = jnp.sum(got.astype(F32), axis=0).astype(BF16)
        full = exchange(jnp.broadcast_to(total[None], (doms,) + total.shape), "dom")
        grad_wtemp = full.astype(F32).reshape(share, 3 * width)
        came = exchange(back.astype(BF16).reshape(doms, halo_per, width), "dom")
        picks = (route.reshape(-1)[:, None] == jnp.arange(local, dtype=jnp.int32)).astype(BF16)
        sums = dot_tn(picks, came.reshape(halo_rows, width))
        return ((partial + sums).astype(BF16)[None], grad_wtemp)

    mine = pl.pallas_call(
        functools.partial(outer_sum_kernel, halo_per),
        out_shape=shape(piece, 4 * width),
        in_specs=[VMEM] * (1 + pieces),
        out_specs=VMEM,
        compiler_params=params(8),
        name="outer_sum",
    )(back, *got)
    other = flipped(mine, "dom", 1)
    sums = pl.pallas_call(
        functools.partial(inner_sum_kernel, halo_per),
        out_shape=(shape(piece, 3 * width + lanes),) * pieces,
        in_specs=[VMEM] * 3,
        out_specs=(VMEM,) * pieces,
        compiler_params=params(8),
        name="inner_sum",
    )(back, mine, other)
    order = [*range(2, pieces), 1]
    sums = {0: sums[0]} | {k: flipped(sums[k], "dom", 2 * k) for k in order}
    soon, late = [0], order
    partial, picks, grad_wtemp = pl.pallas_call(
        functools.partial(early_kernel, soon, halo_per),
        out_shape=(
            shape(local, width, dtype=F32),
            shape(halo_rows, local),
            hbm(share, 3 * width, dtype=F32),
        ),
        in_specs=[SMEM] + [VMEM] * (1 + len(soon)),
        out_specs=(VMEM, VMEM, HBM),
        scratch_shapes=[
            pltpu.VMEM((len(soon), piece, 3 * width), F32),
            pltpu.VMEM((halo_rows, width), F32),
            pltpu.SemaphoreType.DMA((len(soon),)),
        ],
        compiler_params=params(8),
        name="early_sums",
    )(route, partial, *[sums[k] for k in soon])
    grad_feat, grad_wtemp = pl.pallas_call(
        functools.partial(last_kernel, late, halo_per),
        out_shape=(hbm(local, width), hbm(share, 3 * width, dtype=F32)),
        in_specs=[VMEM] * 2 + [HBM] + [VMEM] * len(late),
        out_specs=(HBM, HBM),
        scratch_shapes=[
            pltpu.VMEM((local, width), BF16),
            pltpu.VMEM((len(late), piece, 3 * width), F32),
            pltpu.VMEM((halo_rows, width), F32),
            pltpu.SemaphoreType.DMA((len(late) + 1,)),
        ],
        input_output_aliases={2: 1},
        compiler_params=params(8),
        name="last_sums",
    )(picks, partial, *in_hbm(grad_wtemp), *[sums[k] for k in late])
    return (grad_feat[None], grad_wtemp)


def solution(mesh):
    return jax.shard_map(
        per_device,
        mesh=mesh,
        in_specs=(
            P("snap", "dom", None),
            P(),
            P(),
            P(),
            P(),
            P("snap", "dom", None),
            P("snap", "dom", None),
            P("snap", "dom", None, None),
            P(None, ("dom", "snap")),
            P(None, ("dom", "snap"), None),
        ),
        out_specs=(P("snap", "dom", None), P("snap", None)),
        check_vma=False,
    )
```

```python
import functools

import jax
import jax.numpy as jnp
from jax import lax
from jax.experimental import pallas as pl
from jax.experimental.pallas import tpu as pltpu
from jax.sharding import PartitionSpec as P

F32 = jnp.float32
BF16 = jnp.bfloat16
LANES = 128
NEG = -1e30
VMEM = pl.BlockSpec(memory_space=pltpu.VMEM)
SMEM = pl.BlockSpec(memory_space=pltpu.SMEM)
HBM = pl.BlockSpec(memory_space=pltpu.HBM)


def snap_index():
    return lax.axis_index("snap")


def dom_index():
    return lax.axis_index("dom")


def dot_nn(a, b):
    return lax.dot_general(a, b, (((1,), (0,)), ((), ())), preferred_element_type=F32)


def dot_nt(a, b):
    return lax.dot_general(a, b, (((1,), (1,)), ((), ())), preferred_element_type=F32)


def dot_tn(a, b):
    return lax.dot_general(a, b, (((0,), (0,)), ((), ())), preferred_element_type=F32)


def stack_heads(block, head_dim):
    rows, lanes = block.shape
    head = lax.broadcasted_iota(jnp.int32, (rows, lanes), 1) // head_dim
    zero = jnp.zeros_like(block)
    return jnp.concatenate(
        [jnp.where(head == g, block, zero) for g in range(lanes // head_dim)], axis=0
    )


def unstack_heads(stacked, head_dim):
    lanes = stacked.shape[1]
    groups = lanes // head_dim
    rows = stacked.shape[0] // groups
    head = lax.broadcasted_iota(jnp.int32, (rows, lanes), 1) // head_dim
    out = stacked[:rows]
    for g in range(1, groups):
        out = jnp.where(head == g, stacked[g * rows : (g + 1) * rows], out)
    return out


class Fetch:

    def __init__(self, sems, *pairs):
        self.copies = [
            pltpu.make_async_copy(src, dst, sems.at[i]) for i, (src, dst) in enumerate(pairs)
        ]
        for copy in self.copies:
            copy.start()

    def wait(self, *which):
        for i in which:
            self.copies[i].wait()


def pick_rows(route_ref, local):
    doms, per = route_ref.shape
    lane = lax.broadcasted_iota(jnp.int32, (per, local), 1)
    sub = lax.broadcasted_iota(jnp.int32, (per, local), 0)
    tiles = []
    for r in range(doms):
        spot = jnp.zeros((per, local), jnp.int32)
        for j in range(per):
            spot = jnp.where(sub == j, route_ref[r, j], spot)
        tiles.append(jnp.where(lane == spot, 1.0, 0.0))
    return jnp.concatenate(tiles, axis=0).astype(BF16)


def tiles_kernel(route_hbm, x_hbm, out_ref, route, x, sems):
    fetch = Fetch(sems, (route_hbm, route), (x_hbm, x))
    fetch.wait(0, 1)
    out_ref[...] = dot_nn(pick_rows(route, x.shape[0]), x[...]).astype(BF16)


def own_kernel(
    nbr_hbm, rel_hbm, bias_hbm, act_hbm, cot_hbm, x_hbm, w_hbm,
    edge_ref, proj, x, w, load_hbm, nbr, rel, bias, act, cot, flags_s, sems,
):
    heads, rows, keys = edge_ref.shape
    kinds = bias.shape[0]
    snaps, ents, width = cot.shape
    fetch = Fetch(
        sems,
        (cot_hbm, cot),
        (act_hbm, act),
        (nbr_hbm, nbr),
        (rel_hbm, rel),
        (bias_hbm, bias),
        (x_hbm, x),
        (w_hbm, w),
    )
    row = lax.broadcasted_iota(jnp.int32, (ents, ents), 0)
    col = lax.broadcasted_iota(jnp.int32, (ents, ents), 1)
    lane = lax.broadcasted_iota(jnp.int32, (ents, width), 1)
    flags = jnp.zeros((ents, width), F32)
    fetch.wait(1)
    on = act[...].astype(F32)
    for t in range(snaps):
        column = jnp.sum(jnp.where(row == col, on[t : t + 1, :], 0.0), axis=1, keepdims=True)
        flags = jnp.where(lane == t, column, flags)
    flags_s[...] = flags.astype(BF16)
    fetch.wait(0)
    store = Fetch(sems.at[7:], (flags_s, load_hbm.at[snaps]), (cot, load_hbm.at[:snaps]))
    fetch.wait(2, 3, 4)
    counts = edge_counts(nbr, rel, kinds, keys)
    gain = jnp.exp(bias[...])
    for h in range(heads):
        weight = counts[0] * gain[0:1, h : h + 1]
        for r in range(1, kinds):
            weight = weight + counts[r] * gain[r : r + 1, h : h + 1]
        edge_ref[h] = jnp.where(weight > 0, jnp.log(weight), NEG)
    fetch.wait(5, 6)
    for part in range(3):
        cols = slice(part * width, (part + 1) * width)
        proj[:, cols] = dot_nn(x[...], w[:, cols]).astype(BF16)
    store.wait(0, 1)


def fill_table(tab_s, proj, halo, w_kv):
    rows, width = proj.shape[0], halo.shape[1]
    used = rows + halo.shape[0]
    tab_s[:rows, :] = proj[:, width:]
    for part in range(2):
        cols = slice(part * width, (part + 1) * width)
        tab_s[rows:used, cols] = dot_nn(halo[...], w_kv[:, cols]).astype(BF16)
    if tab_s.shape[0] > used:
        tab_s[used:, :] = jnp.zeros((tab_s.shape[0] - used, 2 * width), BF16)


def edge_counts(nbr, rel, kinds, keys):
    bits = 4
    slots, rows = nbr.shape
    target = jnp.transpose(nbr[...].astype(F32))
    one = jnp.transpose(lax.shift_left(jnp.ones_like(rel[...]), bits * rel[...]).astype(F32))
    spot = lax.broadcasted_iota(jnp.int32, (rows, keys), 1).astype(F32)
    packed = jnp.zeros((rows, keys), F32)
    for k in range(slots):
        packed = packed + jnp.where(target[:, k : k + 1] == spot, one[:, k : k + 1], 0.0)
    packed = packed.astype(jnp.int32)
    low = (1 << bits) - 1
    counts = [
        lax.bitwise_and(lax.shift_right_logical(packed, bits * r), low).astype(F32)
        for r in range(kinds)
    ]
    return counts


def edge_attention(p, heads, proj, edge, tab_s, width):
    keys = tab_s.shape[0]
    head_dim = width // heads
    group = LANES // head_dim
    cols = slice(p * LANES, (p + 1) * LANES)
    kk = stack_heads(tab_s[:, cols], head_dim)
    score = dot_nt(proj[:, cols], kk)
    parts = []
    for g in range(group):
        s = score[:, g * keys : (g + 1) * keys] * head_dim ** (-0.5) + edge[p * group + g]
        e = jnp.exp(s - jnp.max(s, axis=1, keepdims=True))
        parts.append(e * (1.0 / jnp.sum(e, axis=1, keepdims=True)))
    return kk, parts


def forward_kernel(heads, x, halo, w, proj, edge, hidden_ref, tab_s):
    width = x.shape[1]
    head_dim = width // heads
    fill_table(tab_s, proj, halo, w.at[:, width:])
    for p in range(width // LANES):
        cols = slice(p * LANES, (p + 1) * LANES)
        vcols = slice(width + p * LANES, width + (p + 1) * LANES)
        _, attn = edge_attention(p, heads, proj, edge, tab_s, width)
        vv = stack_heads(tab_s[:, vcols], head_dim)
        agg = dot_nn(jnp.concatenate([a.astype(BF16) for a in attn], axis=1), vv)
        elu = jnp.where(agg > 0, agg, jnp.exp(jnp.minimum(agg, 0.0)) - 1.0)
        hidden_ref[:, cols] = (x[:, cols].astype(F32) + elu).astype(BF16)


def each(lo, hi, unroll, body):
    if unroll:
        for i in range(lo, hi):
            body(i)
    else:
        lax.fori_loop(lo, hi, lambda i, c: (body(i), c)[1], 0)


def cotangent_kernel(*refs):
    *cot, ct_ref, act_ref = refs
    snaps = len(cot)
    ents = cot[0].shape[1]
    local = snaps * ents
    for m in range(snaps):
        at = pl.multiple_of(lax.bitwise_xor(snap_index(), m) * ents, ents)
        for t in range(snaps):
            ct_ref[pl.ds(t * local + at, ents), :] = cot[m][t].astype(ct_ref.dtype)
        act_ref[pl.ds(at, ents), :] = cot[m][snaps][:, :LANES].astype(F32)


def temporal_kernel(snaps, heads, pieces, pos_ref, w_s, ct_s, act_s, *refs):
    hid = refs[:snaps]
    terms_ref = refs[snaps : snaps + pieces]
    (
        dt_own_ref, cot_own_ref,
        z_s, tp_s, dt_s, prod_s, s_s, d_s, a_s, ds_s, terms_s,
    ) = refs[snaps + pieces :]
    local, width = hid[0].shape
    head_dim = width // heads
    scale = head_dim ** (-0.5)
    unroll = snaps <= 4
    me, outer = snap_index(), dom_index() // 2
    pos = pos_ref[...].astype(F32)
    which = lax.broadcasted_iota(jnp.int32, pos.shape, 0)

    def rows_of(t):
        return pl.ds(t * local if isinstance(t, int) else pl.multiple_of(t * local, local), local)

    for n in range(snaps):
        t = lax.bitwise_xor(me, n)
        shift = jnp.sum(jnp.where(which == t, pos, 0.0), axis=0, keepdims=True)
        z_s[rows_of(t), :] = (hid[n][...].astype(F32) + shift).astype(BF16)
    for part in range(3):
        cols = slice(part * width, (part + 1) * width)
        tp_s[:, cols] = dot_nn(z_s[...], w_s[:, cols]).astype(BF16)
    lane_head = lax.broadcasted_iota(jnp.int32, (width, LANES), 0) // head_dim
    fold = (lane_head == lax.broadcasted_iota(jnp.int32, (width, LANES), 1)).astype(F32)
    fold = fold.astype(BF16)
    head_lane = lax.broadcasted_iota(jnp.int32, (LANES, width), 1) // head_dim
    spread = (head_lane == lax.broadcasted_iota(jnp.int32, (LANES, width), 0)).astype(F32)
    spread_scaled = (spread * scale).astype(BF16)
    spread = spread.astype(BF16)
    act = act_s[...]
    snap_lane = lax.broadcasted_iota(jnp.int32, act.shape, 1)
    def pair_rows(t, u):
        return rows_of((t * t + t) // 2 + u)

    def reduced(lo, hi, fn, start):
        if unroll:
            for i in range(lo, hi):
                start = fn(i, start)
            return start
        return lax.fori_loop(lo, hi, fn, start)

    def one_snap(t):
        used = (t + 1 if unroll else snaps) * local
        half = snaps * local

        def product(u):
            q, k, v = (
                tp_s[rows_of(i), part * width : (part + 1) * width]
                for part, i in ((0, t), (1, u), (2, u))
            )
            prod_s[rows_of(u), :] = q * k
            prod_s[rows_of(snaps + u), :] = ct_s[rows_of(t), :].astype(BF16) * v

        each(0, t + 1, unroll, product)
        s_s[:used, :] = dot_nn(prod_s[:used, :], fold)
        d_s[:used, :] = dot_nn(prod_s[half : half + used, :], fold).astype(BF16).astype(F32)

        def mask(u):
            on = jnp.sum(jnp.where(snap_lane == u, act, 0.0), axis=1, keepdims=True)
            s_s[rows_of(u), :] = jnp.where((on > 0.5) | (u == t), s_s[rows_of(u), :] * scale, NEG)

        each(0, t + 1, unroll, mask)

        top = reduced(
            0,
            t + 1,
            lambda u, c: jnp.maximum(c, s_s[rows_of(u), :]),
            jnp.full((local, LANES), NEG, F32),
        )

        def expo(u, total):
            e = jnp.exp(s_s[rows_of(u), :] - top)
            s_s[rows_of(u), :] = e
            return total + e

        inv = 1.0 / reduced(0, t + 1, expo, jnp.zeros((local, LANES), F32))

        def weigh(u, total):
            a = s_s[rows_of(u), :] * inv
            s_s[rows_of(u), :] = a
            return total + a * d_s[rows_of(u), :]

        dot = reduced(0, t + 1, weigh, jnp.zeros((local, LANES), F32))

        def keep(u):
            a = s_s[rows_of(u), :]
            a_s[pair_rows(t, u), :] = a.astype(BF16)
            ds_s[pair_rows(t, u), :] = (a * (d_s[rows_of(u), :] - dot)).astype(BF16)

        each(0, t + 1, unroll, keep)

    each(0, snaps, unroll, one_snap)
    for p in range(width // LANES):
        c0 = p * LANES
        cols = slice(c0, c0 + LANES)

        def columns(part, i):
            return tp_s[rows_of(i), part * width + c0 : part * width + c0 + LANES].astype(F32)

        def query(t):
            def add(u, dq):
                return dq + dot_nn(ds_s[pair_rows(t, u), :], spread_scaled[:, cols]) * columns(1, u)

            dq = reduced(0, t + 1, add, jnp.zeros((local, LANES), F32))
            dt_s[rows_of(t), cols] = dq.astype(BF16)

        def key_value(u):
            def add(t, grads):
                dk, dv = grads
                dk = dk + dot_nn(ds_s[pair_rows(t, u), :], spread_scaled[:, cols]) * columns(0, t)
                wide = dot_nn(a_s[pair_rows(t, u), :], spread[:, cols])
                return dk, dv + wide * ct_s[rows_of(t), cols].astype(F32)

            zero = jnp.zeros((local, LANES), F32)
            dk, dv = reduced(u, snaps, add, (zero, zero))
            dt_s[rows_of(u), width + c0 : width + c0 + LANES] = dk.astype(BF16)
            dt_s[rows_of(u), 2 * width + c0 : 2 * width + c0 + LANES] = dv.astype(BF16)

        each(0, snaps, unroll, query)
        each(0, snaps, unroll, key_value)
    share = width // snaps
    pick = (
        lax.broadcasted_iota(jnp.int32, (width, share), 0)
        == lax.broadcasted_iota(jnp.int32, (width, share), 1) + me * share
    )
    z_mine = dot_nn(z_s[...], pick.astype(F32).astype(BF16)).astype(BF16)
    for part in range(3):
        cols = slice(part * width, (part + 1) * width)
        terms_s[:, cols] = dot_tn(z_mine, dt_s[:, cols]).astype(BF16)
    piece = share // pieces
    for k in range(pieces):
        if pieces == 1:
            terms_ref[k][...] = terms_s[...]
        else:
            at = pl.multiple_of(lax.bitwise_xor(outer, k) * piece, piece)
            terms_ref[k][...] = terms_s[pl.ds(at, piece), :]
    dt_own_ref[...] = dt_s[rows_of(me), :]
    cot_own_ref[...] = ct_s[rows_of(me), :].astype(BF16)


def backward_kernel(
    heads, dt, cot, proj, halo, edge, ws, wt, back_ref, part_ref, tab_s, dq_s, dtab_s,
):
    rows, width = cot.shape
    halo_rows = halo.shape[0]
    keys = tab_s.shape[0]
    head_dim = width // heads
    group = LANES // head_dim
    scale = head_dim ** (-0.5)
    dh = cot[...].astype(F32) + dot_nt(dt[...], wt[...])
    part_ref[...] = dh.astype(BF16).astype(F32)
    fill_table(tab_s, proj, halo, ws.at[:, width:])
    for p in range(width // LANES):
        cols = slice(p * LANES, (p + 1) * LANES)
        vcols = slice(width + p * LANES, width + (p + 1) * LANES)
        kk, attn = edge_attention(p, heads, proj, edge, tab_s, width)
        vv = stack_heads(tab_s[:, vcols], head_dim)
        attn_b = jnp.concatenate([a.astype(BF16) for a in attn], axis=1)
        agg = dot_nn(attn_b, vv)
        da = part_ref[:, cols] * jnp.where(agg > 0, 1.0, jnp.exp(jnp.minimum(agg, 0.0)))
        da = da.astype(BF16)
        dattn = dot_nt(da, vv).astype(BF16).astype(F32)
        ds = []
        for g in range(group):
            ad = attn[g] * dattn[:, g * keys : (g + 1) * keys]
            ds.append((ad - attn[g] * jnp.sum(ad, axis=1, keepdims=True)).astype(BF16))
        ds = jnp.concatenate(ds, axis=1)
        dq_s[:, cols] = (dot_nn(ds, kk) * scale).astype(BF16)
        dtab_s[:, cols] = (unstack_heads(dot_tn(ds, proj[:, cols]), head_dim) * scale).astype(BF16)
        dtab_s[:, vcols] = unstack_heads(dot_tn(attn_b, da), head_dim).astype(BF16)
    back_ref[...] = dot_nt(dtab_s[rows : rows + halo_rows, :], ws[:, width:])
    part_ref[...] += dot_nt(dq_s[...], ws[:, :width]) + dot_nt(dtab_s[:rows, :], ws[:, width:])


def tile_of(flip, back_ref, per):
    at = lax.bitwise_xor(dom_index(), flip) * per
    return back_ref[pl.ds(pl.multiple_of(at, per), per), :]


def outer_sum_kernel(per, back_ref, *refs):
    *terms, out_ref = refs
    wide = terms[0].shape[1]
    total = terms[0][...].astype(F32)
    for term in terms[1:]:
        total = total + term[...].astype(F32)
    out_ref[:, :wide] = total.astype(BF16)
    tiles = [tile_of(2 * k + 1, back_ref, per) for k in range(len(terms))]
    out_ref[:, wide:] = jnp.concatenate(tiles, axis=0).astype(BF16)


def inner_sum_kernel(per, back_ref, mine_ref, other_ref, *out):
    rows = mine_ref.shape[0]
    wide = mine_ref.shape[1] - back_ref.shape[1]
    lanes = out[0].shape[1] - wide
    total = (mine_ref[:, :wide].astype(F32) + other_ref[:, :wide].astype(F32)).astype(BF16)
    passing = other_ref[:, wide:].astype(F32)
    for k in range(len(out)):
        out[k][:, :wide] = total
        both = [tile_of(2 * k, back_ref, per), passing[k * per : (k + 1) * per]]
        folds = [
            tile[:, i * lanes : (i + 1) * lanes]
            for tile in both
            for i in range(rows // (2 * per))
        ]
        out[k][:, wide:] = jnp.concatenate(folds, axis=0).astype(BF16)


def unpack_sums(flips, per, got, wtemp, wtemp_hbm, came_s, sems):
    rows = got[0].shape[0]
    lanes = got[0].shape[1] - wtemp.shape[2]
    folds = rows // (2 * per)
    stores = []
    came_s[...] = jnp.zeros_like(came_s)
    for i, k in enumerate(flips):
        wtemp[i] = got[i][:, : wtemp.shape[2]].astype(F32)
        at = pl.multiple_of(lax.bitwise_xor(dom_index() // 2, k) * rows, rows)
        stores.append(Fetch(sems.at[i:], (wtemp.at[i], wtemp_hbm.at[pl.ds(at, rows), :])))
        folded = got[i][:, wtemp.shape[2] :].astype(F32)
        for j in range(2):
            d = pl.multiple_of(lax.bitwise_xor(dom_index(), 2 * k + j) * per, per)
            for f in range(folds):
                row = (j * folds + f) * per
                came_s[pl.ds(d, per), f * lanes : (f + 1) * lanes] = folded[row : row + per]
    return stores


def early_kernel(flips, per, route_ref, part_ref, *refs):
    got = refs[: len(flips)]
    sum_ref, picks_ref, wtemp_hbm, wtemp, came_s, sems = refs[len(flips) :]
    stores = unpack_sums(flips, per, got, wtemp, wtemp_hbm, came_s, sems)
    picks = pick_rows(route_ref, part_ref.shape[0])
    picks_ref[...] = picks
    sum_ref[...] = part_ref[...] + dot_tn(picks, came_s[...].astype(BF16))
    for store in stores:
        store.wait(0)


def last_kernel(flips, per, picks_ref, sum_ref, _, *refs):
    got = refs[: len(flips)]
    feat_hbm, wtemp_hbm, feat, wtemp, came_s, sems = refs[len(flips) :]
    stores = unpack_sums(flips, per, got, wtemp, wtemp_hbm, came_s, sems)
    feat[...] = (sum_ref[...] + dot_tn(picks_ref[...], came_s[...].astype(BF16))).astype(BF16)
    stores.append(Fetch(sems.at[len(flips) :], (feat, feat_hbm)))
    for store in stores:
        store.wait(0)


def params(mib):
    return pltpu.CompilerParams(vmem_limit_bytes=mib * 1024 * 1024)


def gather_blocks(held, axis, bit, last):
    held = dict(held)
    while bit >= last:
        for m in sorted(held):
            held[m ^ bit] = flipped(held[m], axis, bit)
        bit //= 2
    return held


def in_hbm(*arrays):
    return [pltpu.with_memory_space_constraint(a, pltpu.HBM) for a in arrays]


def exchange(tiles, axis):
    return lax.all_to_all(tiles, axis, split_axis=0, concat_axis=0, tiled=True)


def flipped(block, axis, flip):
    count = lax.axis_size(axis)
    return lax.ppermute(block, axis, [(i, i ^ flip) for i in range(count)])


def per_device(
    feat, w_struct, w_temp, pos_embed, rel_bias, nbr, rel_type, send_idx, active, cotangent
):
    x = feat[0]
    local, width = x.shape
    heads = rel_bias.shape[1]
    slots = nbr.shape[2]
    doms = lax.axis_size("dom")
    snaps = lax.axis_size("snap")
    ents = local // snaps
    route = send_idx[0, 0]
    halo_per = route.shape[1]
    halo_rows = doms * halo_per
    keys = -(-(local + halo_rows) // LANES) * LANES
    share = width // snaps
    pieces = doms // 2
    piece = share // pieces
    lanes = 2 * halo_per * width // piece if piece else 0
    paired = (
        doms % 2 == 0
        and doms & (doms - 1) == 0
        and piece == pieces * halo_per
        and piece % 16 == 0
        and lanes % LANES == 0
        and lanes > 0
    )
    if not paired:
        pieces = 1

    def shape(*dims, dtype=BF16):
        return jax.ShapeDtypeStruct(dims, dtype)

    def vmem(*dims, dtype=BF16):
        return pltpu.VMEM(dims, dtype)

    def hbm(*dims, dtype=BF16):
        return pltpu.HBM(dims, dtype)

    tiles = pl.pallas_call(
        tiles_kernel,
        out_shape=shape(halo_rows, width),
        in_specs=[HBM, HBM],
        out_specs=VMEM,
        scratch_shapes=[
            pltpu.SMEM(route.shape, jnp.int32),
            pltpu.VMEM((local, width), BF16),
            pltpu.SemaphoreType.DMA((2,)),
        ],
        compiler_params=params(8),
        name="halo_tiles",
    )(*in_hbm(route, x))
    halo = exchange(tiles.reshape(doms, halo_per, width), "dom").reshape(halo_rows, width)

    edge, proj, x_near, w_near, load = pl.pallas_call(
        own_kernel,
        out_shape=(
            vmem(heads, local, keys, dtype=F32),
            vmem(local, 3 * width),
            vmem(local, width),
            vmem(*w_struct.shape),
            hbm(snaps + 1, ents, width),
        ),
        in_specs=[HBM] * 7,
        out_specs=(VMEM,) * 4 + (HBM,),
        scratch_shapes=[
            pltpu.VMEM((slots, local), jnp.int32),
            pltpu.VMEM((slots, local), jnp.int32),
            pltpu.VMEM(rel_bias.shape, F32),
            pltpu.VMEM((snaps, ents), jnp.int32),
            pltpu.VMEM((snaps, ents, width), BF16),
            pltpu.VMEM((ents, width), BF16),
            pltpu.SemaphoreType.DMA((9,)),
        ],
        compiler_params=params(8),
        cost_estimate=pl.CostEstimate(flops=10**9, bytes_accessed=4 * 10**6, transcendentals=0),
        name="own_rows",
    )(
        *in_hbm(nbr[0].T, rel_type[0].T, rel_bias, active, cotangent, x, w_struct),
    )
    cots = gather_blocks({0: load}, "snap", snaps // 2, 1)
    cots = [cots[m] for m in range(snaps)]

    hidden = pl.pallas_call(
        functools.partial(forward_kernel, heads),
        out_shape=shape(local, width),
        in_specs=[VMEM] * 5,
        out_specs=VMEM,
        scratch_shapes=[pltpu.VMEM((keys, 2 * width), BF16)],
        compiler_params=params(8),
        name="struct_forward",
    )(x_near, halo, w_near, proj, edge)

    hids = gather_blocks({0: hidden}, "snap", snaps // 2, 1)
    hids = [hids[m] for m in range(snaps)]
    every = snaps * local
    pairs = snaps * (snaps + 1) // 2
    ct, act = pl.pallas_call(
        cotangent_kernel,
        out_shape=(
            shape(every, width, dtype=F32 if ents % 16 else BF16),
            shape(local, LANES, dtype=F32),
        ),
        in_specs=[VMEM] * snaps,
        out_specs=(VMEM, VMEM),
        compiler_params=params(8),
        name="cotangents",
    )(*cots)
    *terms, dt_own, cot_own = pl.pallas_call(
        functools.partial(temporal_kernel, snaps, heads, pieces),
        out_shape=(shape(share // pieces, 3 * width),) * pieces
        + (shape(local, 3 * width), shape(local, width)),
        in_specs=[VMEM] * (4 + snaps),
        out_specs=(VMEM,) * (pieces + 2),
        scratch_shapes=[
            pltpu.VMEM((every, width), BF16),
            pltpu.VMEM((every, 3 * width), BF16),
            pltpu.VMEM((every, 3 * width), BF16),
            pltpu.VMEM((2 * every, width), BF16),
            pltpu.VMEM((every, LANES), F32),
            pltpu.VMEM((every, LANES), F32),
            pltpu.VMEM((pairs * local, LANES), BF16),
            pltpu.VMEM((pairs * local, LANES), BF16),
            pltpu.VMEM((share, 3 * width), BF16),
        ],
        compiler_params=params(24 if snaps <= 4 else 56),
        name="temporal",
    )(pos_embed, w_temp, ct, act, *hids)

    if paired:
        got = [terms[0]] + [flipped(terms[k], "dom", 2 * k) for k in range(pieces - 1, 0, -1)]
    else:
        got = exchange(terms[0].reshape(doms, share // doms, 3 * width), "dom")
    back, partial = pl.pallas_call(
        functools.partial(backward_kernel, heads),
        out_shape=(shape(halo_rows, width, dtype=F32), shape(local, width, dtype=F32)),
        in_specs=[VMEM] * 7,
        out_specs=(VMEM, VMEM),
        scratch_shapes=[
            pltpu.VMEM((keys, 2 * width), BF16),
            pltpu.VMEM((local, width), BF16),
            pltpu.VMEM((keys, 2 * width), BF16),
        ],
        compiler_params=params(16),
        cost_estimate=pl.CostEstimate(flops=2 * 10**9, bytes_accessed=8 * 10**6, transcendentals=0),
        name="struct_backward",
    )(dt_own, cot_own, proj, halo, edge, w_near, w_temp)

    if not paired:
        total = jnp.sum(got.astype(F32), axis=0).astype(BF16)
        full = exchange(jnp.broadcast_to(total[None], (doms,) + total.shape), "dom")
        grad_wtemp = full.astype(F32).reshape(share, 3 * width)
        came = exchange(back.astype(BF16).reshape(doms, halo_per, width), "dom")
        picks = (route.reshape(-1)[:, None] == jnp.arange(local, dtype=jnp.int32)).astype(BF16)
        sums = dot_tn(picks, came.reshape(halo_rows, width))
        return ((partial + sums).astype(BF16)[None], grad_wtemp)

    mine = pl.pallas_call(
        functools.partial(outer_sum_kernel, halo_per),
        out_shape=shape(piece, 4 * width),
        in_specs=[VMEM] * (1 + pieces),
        out_specs=VMEM,
        compiler_params=params(8),
        name="outer_sum",
    )(back, *got)
    other = flipped(mine, "dom", 1)
    sums = pl.pallas_call(
        functools.partial(inner_sum_kernel, halo_per),
        out_shape=(shape(piece, 3 * width + lanes),) * pieces,
        in_specs=[VMEM] * 3,
        out_specs=(VMEM,) * pieces,
        compiler_params=params(8),
        name="inner_sum",
    )(back, mine, other)
    order = [*range(2, pieces), 1]
    sums = {0: sums[0]} | {k: flipped(sums[k], "dom", 2 * k) for k in order}
    soon, late = [0], order
    partial, picks, grad_wtemp = pl.pallas_call(
        functools.partial(early_kernel, soon, halo_per),
        out_shape=(
            shape(local, width, dtype=F32),
            shape(halo_rows, local),
            hbm(share, 3 * width, dtype=F32),
        ),
        in_specs=[SMEM] + [VMEM] * (1 + len(soon)),
        out_specs=(VMEM, VMEM, HBM),
        scratch_shapes=[
            pltpu.VMEM((len(soon), piece, 3 * width), F32),
            pltpu.VMEM((halo_rows, width), F32),
            pltpu.SemaphoreType.DMA((len(soon),)),
        ],
        compiler_params=params(8),
        name="early_sums",
    )(route, partial, *[sums[k] for k in soon])
    grad_feat, grad_wtemp = pl.pallas_call(
        functools.partial(last_kernel, late, halo_per),
        out_shape=(hbm(local, width), hbm(share, 3 * width, dtype=F32)),
        in_specs=[VMEM] * 2 + [HBM] + [VMEM] * len(late),
        out_specs=(HBM, HBM),
        scratch_shapes=[
            pltpu.VMEM((local, width), BF16),
            pltpu.VMEM((len(late), piece, 3 * width), F32),
            pltpu.VMEM((halo_rows, width), F32),
            pltpu.SemaphoreType.DMA((len(late) + 1,)),
        ],
        input_output_aliases={2: 1},
        compiler_params=params(8),
        name="last_sums",
    )(picks, partial, *in_hbm(grad_wtemp), *[sums[k] for k in late])
    return (grad_feat[None], grad_wtemp)


def solution(mesh):
    return jax.shard_map(
        per_device,
        mesh=mesh,
        in_specs=(
            P("snap", "dom", None),
            P(),
            P(),
            P(),
            P(),
            P("snap", "dom", None),
            P("snap", "dom", None),
            P("snap", "dom", None, None),
            P(None, ("dom", "snap")),
            P(None, ("dom", "snap"), None),
        ),
        out_specs=(P("snap", "dom", None), P("snap", None)),
        check_vma=False,
    )
```

```python
import functools

import jax
import jax.numpy as jnp
from jax import lax
from jax.experimental import pallas as pl
from jax.experimental.pallas import tpu as pltpu
from jax.sharding import PartitionSpec as P

F32 = jnp.float32
BF16 = jnp.bfloat16
LANES = 128
NEG = -1e30
VMEM = pl.BlockSpec(memory_space=pltpu.VMEM)
SMEM = pl.BlockSpec(memory_space=pltpu.SMEM)
HBM = pl.BlockSpec(memory_space=pltpu.HBM)


def snap_index():
    return lax.axis_index("snap")


def dom_index():
    return lax.axis_index("dom")


def dot_nn(a, b):
    return lax.dot_general(a, b, (((1,), (0,)), ((), ())), preferred_element_type=F32)


def dot_nt(a, b):
    return lax.dot_general(a, b, (((1,), (1,)), ((), ())), preferred_element_type=F32)


def dot_tn(a, b):
    return lax.dot_general(a, b, (((0,), (0,)), ((), ())), preferred_element_type=F32)


def stack_heads(block, head_dim):
    rows, lanes = block.shape
    head = lax.broadcasted_iota(jnp.int32, (rows, lanes), 1) // head_dim
    zero = jnp.zeros_like(block)
    return jnp.concatenate(
        [jnp.where(head == g, block, zero) for g in range(lanes // head_dim)], axis=0
    )


def unstack_heads(stacked, head_dim):
    lanes = stacked.shape[1]
    groups = lanes // head_dim
    rows = stacked.shape[0] // groups
    head = lax.broadcasted_iota(jnp.int32, (rows, lanes), 1) // head_dim
    out = stacked[:rows]
    for g in range(1, groups):
        out = jnp.where(head == g, stacked[g * rows : (g + 1) * rows], out)
    return out


class Fetch:

    def __init__(self, sems, *pairs):
        self.copies = [
            pltpu.make_async_copy(src, dst, sems.at[i]) for i, (src, dst) in enumerate(pairs)
        ]
        for copy in self.copies:
            copy.start()

    def wait(self, *which):
        for i in which:
            self.copies[i].wait()


def pick_rows(route_ref, local):
    doms, per = route_ref.shape
    lane = lax.broadcasted_iota(jnp.int32, (per, local), 1)
    sub = lax.broadcasted_iota(jnp.int32, (per, local), 0)
    tiles = []
    for r in range(doms):
        spot = jnp.zeros((per, local), jnp.int32)
        for j in range(per):
            spot = jnp.where(sub == j, route_ref[r, j], spot)
        tiles.append(jnp.where(lane == spot, 1.0, 0.0))
    return jnp.concatenate(tiles, axis=0).astype(BF16)


def tiles_kernel(route_hbm, x_hbm, out_ref, route, x, sems):
    fetch = Fetch(sems, (route_hbm, route), (x_hbm, x))
    fetch.wait(0, 1)
    out_ref[...] = dot_nn(pick_rows(route, x.shape[0]), x[...]).astype(BF16)


def own_kernel(
    nbr_hbm, rel_hbm, bias_hbm, act_hbm, cot_hbm, x_hbm, w_hbm,
    edge_ref, proj, x, w, load_hbm, nbr, rel, bias, act, cot, flags_s, sems,
):
    heads, rows, keys = edge_ref.shape
    kinds = bias.shape[0]
    snaps, ents, width = cot.shape
    fetch = Fetch(
        sems,
        (cot_hbm, cot),
        (act_hbm, act),
        (nbr_hbm, nbr),
        (rel_hbm, rel),
        (bias_hbm, bias),
        (x_hbm, x),
        (w_hbm, w),
    )
    row = lax.broadcasted_iota(jnp.int32, (ents, ents), 0)
    col = lax.broadcasted_iota(jnp.int32, (ents, ents), 1)
    lane = lax.broadcasted_iota(jnp.int32, (ents, width), 1)
    flags = jnp.zeros((ents, width), F32)
    fetch.wait(1)
    on = act[...].astype(F32)
    for t in range(snaps):
        column = jnp.sum(jnp.where(row == col, on[t : t + 1, :], 0.0), axis=1, keepdims=True)
        flags = jnp.where(lane == t, column, flags)
    flags_s[...] = flags.astype(BF16)
    fetch.wait(0)
    store = Fetch(sems.at[7:], (flags_s, load_hbm.at[snaps]), (cot, load_hbm.at[:snaps]))
    fetch.wait(2, 3, 4)
    counts = edge_counts(nbr, rel, kinds, keys)
    gain = jnp.exp(bias[...])
    for h in range(heads):
        weight = counts[0] * gain[0:1, h : h + 1]
        for r in range(1, kinds):
            weight = weight + counts[r] * gain[r : r + 1, h : h + 1]
        edge_ref[h] = jnp.where(weight > 0, jnp.log(weight), NEG)
    fetch.wait(5, 6)
    for part in range(3):
        cols = slice(part * width, (part + 1) * width)
        proj[:, cols] = dot_nn(x[...], w[:, cols]).astype(BF16)
    store.wait(0, 1)


def fill_table(tab_s, proj, halo, w_kv):
    rows, width = proj.shape[0], halo.shape[1]
    used = rows + halo.shape[0]
    tab_s[:rows, :] = proj[:, width:]
    for part in range(2):
        cols = slice(part * width, (part + 1) * width)
        tab_s[rows:used, cols] = dot_nn(halo[...], w_kv[:, cols]).astype(BF16)
    if tab_s.shape[0] > used:
        tab_s[used:, :] = jnp.zeros((tab_s.shape[0] - used, 2 * width), BF16)


def edge_counts(nbr, rel, kinds, keys):
    bits = 4
    slots, rows = nbr.shape
    target = jnp.transpose(nbr[...].astype(F32))
    one = jnp.transpose(lax.shift_left(jnp.ones_like(rel[...]), bits * rel[...]).astype(F32))
    spot = lax.broadcasted_iota(jnp.int32, (rows, keys), 1).astype(F32)
    packed = jnp.zeros((rows, keys), F32)
    for k in range(slots):
        packed = packed + jnp.where(target[:, k : k + 1] == spot, one[:, k : k + 1], 0.0)
    packed = packed.astype(jnp.int32)
    low = (1 << bits) - 1
    counts = [
        lax.bitwise_and(lax.shift_right_logical(packed, bits * r), low).astype(F32)
        for r in range(kinds)
    ]
    return counts


def edge_attention(p, heads, proj, edge, tab_s, width):
    keys = tab_s.shape[0]
    head_dim = width // heads
    group = LANES // head_dim
    cols = slice(p * LANES, (p + 1) * LANES)
    kk = stack_heads(tab_s[:, cols], head_dim)
    score = dot_nt(proj[:, cols], kk)
    parts = []
    for g in range(group):
        s = score[:, g * keys : (g + 1) * keys] * head_dim ** (-0.5) + edge[p * group + g]
        e = jnp.exp(s - jnp.max(s, axis=1, keepdims=True))
        parts.append(e * (1.0 / jnp.sum(e, axis=1, keepdims=True)))
    return kk, parts


def forward_kernel(heads, x, halo, w, proj, edge, hidden_ref, tab_s):
    width = x.shape[1]
    head_dim = width // heads
    fill_table(tab_s, proj, halo, w.at[:, width:])
    for p in range(width // LANES):
        cols = slice(p * LANES, (p + 1) * LANES)
        vcols = slice(width + p * LANES, width + (p + 1) * LANES)
        _, attn = edge_attention(p, heads, proj, edge, tab_s, width)
        vv = stack_heads(tab_s[:, vcols], head_dim)
        agg = dot_nn(jnp.concatenate([a.astype(BF16) for a in attn], axis=1), vv)
        elu = jnp.where(agg > 0, agg, jnp.exp(jnp.minimum(agg, 0.0)) - 1.0)
        hidden_ref[:, cols] = (x[:, cols].astype(F32) + elu).astype(BF16)


def each(lo, hi, unroll, body):
    if unroll:
        for i in range(lo, hi):
            body(i)
    else:
        lax.fori_loop(lo, hi, lambda i, c: (body(i), c)[1], 0)


def position_of(pos_ref, t):
    pos = pos_ref[...].astype(F32)
    which = lax.broadcasted_iota(jnp.int32, pos.shape, 0)
    return jnp.sum(jnp.where(which == t, pos, 0.0), axis=0, keepdims=True)


def arrived_kernel(snaps, flips, pos_ref, w, *refs):
    cot, hid = refs[:snaps], refs[snaps : snaps + len(flips)]
    ct_ref, act_ref, z_ref, tp_ref = refs[snaps + len(flips) :]
    ents = cot[0].shape[1]
    local, width = hid[0].shape
    me = snap_index()
    for m in range(snaps):
        at = pl.multiple_of(lax.bitwise_xor(me, m) * ents, ents)
        for t in range(snaps):
            ct_ref[pl.ds(t * local + at, ents), :] = cot[m][t].astype(ct_ref.dtype)
        act_ref[pl.ds(at, ents), :] = cot[m][snaps][:, :LANES].astype(F32)
    for i, n in enumerate(flips):
        shift = position_of(pos_ref, lax.bitwise_xor(me, n))
        z_ref[i * local : (i + 1) * local, :] = (hid[i][...].astype(F32) + shift).astype(BF16)
    for part in range(3):
        cols = slice(part * width, (part + 1) * width)
        tp_ref[:, cols] = dot_nn(z_ref[...], w[:, cols]).astype(BF16)


def temporal_kernel(
    snaps, heads, pieces, soon, late, pos_ref, w_s, ct_s, act_s, z_soon, tp_soon, *refs
):
    hid, refs = refs[: len(late)], refs[len(late) :]
    terms_ref = refs[:pieces]
    (
        dt_own_ref, cot_own_ref,
        z_s, tp_s, dt_s, prod_s, s_s, d_s, a_s, ds_s, terms_s, z_late, tp_late,
    ) = refs[pieces:]
    local, width = hid[0].shape
    head_dim = width // heads
    scale = head_dim ** (-0.5)
    unroll = snaps <= 4
    me, outer = snap_index(), dom_index() // 2
    def rows_of(t):
        return pl.ds(t * local if isinstance(t, int) else pl.multiple_of(t * local, local), local)

    for i, n in enumerate(late):
        shift = position_of(pos_ref, lax.bitwise_xor(me, n))
        z_late[i * local : (i + 1) * local, :] = (hid[i][...].astype(F32) + shift).astype(BF16)
    for part in range(3):
        cols = slice(part * width, (part + 1) * width)
        tp_late[:, cols] = dot_nn(z_late[...], w_s[:, cols]).astype(BF16)
    for flips, z_ref, tp_ref in ((soon, z_soon, tp_soon), (late, z_late, tp_late)):
        for i, n in enumerate(flips):
            t = lax.bitwise_xor(me, n)
            z_s[rows_of(t), :] = z_ref[i * local : (i + 1) * local, :]
            tp_s[rows_of(t), :] = tp_ref[i * local : (i + 1) * local, :]
    lane_head = lax.broadcasted_iota(jnp.int32, (width, LANES), 0) // head_dim
    fold = (lane_head == lax.broadcasted_iota(jnp.int32, (width, LANES), 1)).astype(F32)
    fold = fold.astype(BF16)
    head_lane = lax.broadcasted_iota(jnp.int32, (LANES, width), 1) // head_dim
    spread = (head_lane == lax.broadcasted_iota(jnp.int32, (LANES, width), 0)).astype(F32)
    spread_scaled = (spread * scale).astype(BF16)
    spread = spread.astype(BF16)
    act = act_s[...]
    snap_lane = lax.broadcasted_iota(jnp.int32, act.shape, 1)
    def pair_rows(t, u):
        return rows_of((t * t + t) // 2 + u)

    def reduced(lo, hi, fn, start):
        if unroll:
            for i in range(lo, hi):
                start = fn(i, start)
            return start
        return lax.fori_loop(lo, hi, fn, start)

    def one_snap(t):
        used = (t + 1 if unroll else snaps) * local
        half = snaps * local

        def product(u):
            q, k, v = (
                tp_s[rows_of(i), part * width : (part + 1) * width]
                for part, i in ((0, t), (1, u), (2, u))
            )
            prod_s[rows_of(u), :] = q * k
            prod_s[rows_of(snaps + u), :] = ct_s[rows_of(t), :].astype(BF16) * v

        each(0, t + 1, unroll, product)
        s_s[:used, :] = dot_nn(prod_s[:used, :], fold)
        d_s[:used, :] = dot_nn(prod_s[half : half + used, :], fold).astype(BF16).astype(F32)

        def mask(u):
            on = jnp.sum(jnp.where(snap_lane == u, act, 0.0), axis=1, keepdims=True)
            s_s[rows_of(u), :] = jnp.where((on > 0.5) | (u == t), s_s[rows_of(u), :] * scale, NEG)

        each(0, t + 1, unroll, mask)

        top = reduced(
            0,
            t + 1,
            lambda u, c: jnp.maximum(c, s_s[rows_of(u), :]),
            jnp.full((local, LANES), NEG, F32),
        )

        def expo(u, total):
            e = jnp.exp(s_s[rows_of(u), :] - top)
            s_s[rows_of(u), :] = e
            return total + e

        inv = 1.0 / reduced(0, t + 1, expo, jnp.zeros((local, LANES), F32))

        def weigh(u, total):
            a = s_s[rows_of(u), :] * inv
            s_s[rows_of(u), :] = a
            return total + a * d_s[rows_of(u), :]

        dot = reduced(0, t + 1, weigh, jnp.zeros((local, LANES), F32))

        def keep(u):
            a = s_s[rows_of(u), :]
            a_s[pair_rows(t, u), :] = a.astype(BF16)
            ds_s[pair_rows(t, u), :] = (a * (d_s[rows_of(u), :] - dot)).astype(BF16)

        each(0, t + 1, unroll, keep)

    each(0, snaps, unroll, one_snap)
    for p in range(width // LANES):
        c0 = p * LANES
        cols = slice(c0, c0 + LANES)

        def columns(part, i):
            return tp_s[rows_of(i), part * width + c0 : part * width + c0 + LANES].astype(F32)

        def query(t):
            def add(u, dq):
                return dq + dot_nn(ds_s[pair_rows(t, u), :], spread_scaled[:, cols]) * columns(1, u)

            dq = reduced(0, t + 1, add, jnp.zeros((local, LANES), F32))
            dt_s[rows_of(t), cols] = dq.astype(BF16)

        def key_value(u):
            def add(t, grads):
                dk, dv = grads
                dk = dk + dot_nn(ds_s[pair_rows(t, u), :], spread_scaled[:, cols]) * columns(0, t)
                wide = dot_nn(a_s[pair_rows(t, u), :], spread[:, cols])
                return dk, dv + wide * ct_s[rows_of(t), cols].astype(F32)

            zero = jnp.zeros((local, LANES), F32)
            dk, dv = reduced(u, snaps, add, (zero, zero))
            dt_s[rows_of(u), width + c0 : width + c0 + LANES] = dk.astype(BF16)
            dt_s[rows_of(u), 2 * width + c0 : 2 * width + c0 + LANES] = dv.astype(BF16)

        each(0, snaps, unroll, query)
        each(0, snaps, unroll, key_value)
    share = width // snaps
    pick = (
        lax.broadcasted_iota(jnp.int32, (width, share), 0)
        == lax.broadcasted_iota(jnp.int32, (width, share), 1) + me * share
    )
    z_mine = dot_nn(z_s[...], pick.astype(F32).astype(BF16)).astype(BF16)
    for part in range(3):
        cols = slice(part * width, (part + 1) * width)
        terms_s[:, cols] = dot_tn(z_mine, dt_s[:, cols]).astype(BF16)
    piece = share // pieces
    for k in range(pieces):
        if pieces == 1:
            terms_ref[k][...] = terms_s[...]
        else:
            at = pl.multiple_of(lax.bitwise_xor(outer, k) * piece, piece)
            terms_ref[k][...] = terms_s[pl.ds(at, piece), :]
    dt_own_ref[...] = dt_s[rows_of(me), :]
    cot_own_ref[...] = ct_s[rows_of(me), :].astype(BF16)


def backward_kernel(
    heads, dt, cot, proj, halo, edge, ws, wt, back_ref, part_ref, tab_s, dq_s, dtab_s,
):
    rows, width = cot.shape
    halo_rows = halo.shape[0]
    keys = tab_s.shape[0]
    head_dim = width // heads
    group = LANES // head_dim
    scale = head_dim ** (-0.5)
    dh = cot[...].astype(F32) + dot_nt(dt[...], wt[...])
    part_ref[...] = dh.astype(BF16).astype(F32)
    fill_table(tab_s, proj, halo, ws.at[:, width:])
    for p in range(width // LANES):
        cols = slice(p * LANES, (p + 1) * LANES)
        vcols = slice(width + p * LANES, width + (p + 1) * LANES)
        kk, attn = edge_attention(p, heads, proj, edge, tab_s, width)
        vv = stack_heads(tab_s[:, vcols], head_dim)
        attn_b = jnp.concatenate([a.astype(BF16) for a in attn], axis=1)
        agg = dot_nn(attn_b, vv)
        da = part_ref[:, cols] * jnp.where(agg > 0, 1.0, jnp.exp(jnp.minimum(agg, 0.0)))
        da = da.astype(BF16)
        dattn = dot_nt(da, vv).astype(BF16).astype(F32)
        ds = []
        for g in range(group):
            ad = attn[g] * dattn[:, g * keys : (g + 1) * keys]
            ds.append((ad - attn[g] * jnp.sum(ad, axis=1, keepdims=True)).astype(BF16))
        ds = jnp.concatenate(ds, axis=1)
        dq_s[:, cols] = (dot_nn(ds, kk) * scale).astype(BF16)
        dtab_s[:, cols] = (unstack_heads(dot_tn(ds, proj[:, cols]), head_dim) * scale).astype(BF16)
        dtab_s[:, vcols] = unstack_heads(dot_tn(attn_b, da), head_dim).astype(BF16)
    back_ref[...] = dot_nt(dtab_s[rows : rows + halo_rows, :], ws[:, width:])
    part_ref[...] += dot_nt(dq_s[...], ws[:, :width]) + dot_nt(dtab_s[:rows, :], ws[:, width:])


def tile_of(flip, back_ref, per):
    at = lax.bitwise_xor(dom_index(), flip) * per
    return back_ref[pl.ds(pl.multiple_of(at, per), per), :]


def outer_sum_kernel(per, back_ref, *refs):
    *terms, out_ref = refs
    wide = terms[0].shape[1]
    total = terms[0][...].astype(F32)
    for term in terms[1:]:
        total = total + term[...].astype(F32)
    out_ref[:, :wide] = total.astype(BF16)
    tiles = [tile_of(2 * k + 1, back_ref, per) for k in range(len(terms))]
    out_ref[:, wide:] = jnp.concatenate(tiles, axis=0).astype(BF16)


def inner_sum_kernel(per, back_ref, mine_ref, other_ref, *out):
    rows = mine_ref.shape[0]
    wide = mine_ref.shape[1] - back_ref.shape[1]
    lanes = out[0].shape[1] - wide
    total = (mine_ref[:, :wide].astype(F32) + other_ref[:, :wide].astype(F32)).astype(BF16)
    passing = other_ref[:, wide:].astype(F32)
    for k in range(len(out)):
        out[k][:, :wide] = total
        both = [tile_of(2 * k, back_ref, per), passing[k * per : (k + 1) * per]]
        folds = [
            tile[:, i * lanes : (i + 1) * lanes]
            for tile in both
            for i in range(rows // (2 * per))
        ]
        out[k][:, wide:] = jnp.concatenate(folds, axis=0).astype(BF16)


def unpack_sums(flips, per, got, wtemp, wtemp_hbm, came_s, sems):
    rows = got[0].shape[0]
    lanes = got[0].shape[1] - wtemp.shape[2]
    folds = rows // (2 * per)
    stores = []
    came_s[...] = jnp.zeros_like(came_s)
    for i, k in enumerate(flips):
        wtemp[i] = got[i][:, : wtemp.shape[2]].astype(F32)
        at = pl.multiple_of(lax.bitwise_xor(dom_index() // 2, k) * rows, rows)
        stores.append(Fetch(sems.at[i:], (wtemp.at[i], wtemp_hbm.at[pl.ds(at, rows), :])))
        folded = got[i][:, wtemp.shape[2] :].astype(F32)
        for j in range(2):
            d = pl.multiple_of(lax.bitwise_xor(dom_index(), 2 * k + j) * per, per)
            for f in range(folds):
                row = (j * folds + f) * per
                came_s[pl.ds(d, per), f * lanes : (f + 1) * lanes] = folded[row : row + per]
    return stores


def early_kernel(flips, per, route_ref, part_ref, *refs):
    got = refs[: len(flips)]
    sum_ref, picks_ref, wtemp_hbm, wtemp, came_s, sems = refs[len(flips) :]
    stores = unpack_sums(flips, per, got, wtemp, wtemp_hbm, came_s, sems)
    picks = pick_rows(route_ref, part_ref.shape[0])
    picks_ref[...] = picks
    sum_ref[...] = part_ref[...] + dot_tn(picks, came_s[...].astype(BF16))
    for store in stores:
        store.wait(0)


def last_kernel(flips, per, picks_ref, sum_ref, _, *refs):
    got = refs[: len(flips)]
    feat_hbm, wtemp_hbm, feat, wtemp, came_s, sems = refs[len(flips) :]
    stores = unpack_sums(flips, per, got, wtemp, wtemp_hbm, came_s, sems)
    feat[...] = (sum_ref[...] + dot_tn(picks_ref[...], came_s[...].astype(BF16))).astype(BF16)
    stores.append(Fetch(sems.at[len(flips) :], (feat, feat_hbm)))
    for store in stores:
        store.wait(0)


def params(mib):
    return pltpu.CompilerParams(vmem_limit_bytes=mib * 1024 * 1024)


def gather_blocks(held, axis, bit, last):
    held = dict(held)
    while bit >= last:
        for m in sorted(held):
            held[m ^ bit] = flipped(held[m], axis, bit)
        bit //= 2
    return held


def in_hbm(*arrays):
    return [pltpu.with_memory_space_constraint(a, pltpu.HBM) for a in arrays]


def exchange(tiles, axis):
    return lax.all_to_all(tiles, axis, split_axis=0, concat_axis=0, tiled=True)


def flipped(block, axis, flip):
    count = lax.axis_size(axis)
    return lax.ppermute(block, axis, [(i, i ^ flip) for i in range(count)])


def per_device(
    feat, w_struct, w_temp, pos_embed, rel_bias, nbr, rel_type, send_idx, active, cotangent
):
    x = feat[0]
    local, width = x.shape
    heads = rel_bias.shape[1]
    slots = nbr.shape[2]
    doms = lax.axis_size("dom")
    snaps = lax.axis_size("snap")
    ents = local // snaps
    route = send_idx[0, 0]
    halo_per = route.shape[1]
    halo_rows = doms * halo_per
    keys = -(-(local + halo_rows) // LANES) * LANES
    share = width // snaps
    pieces = doms // 2
    piece = share // pieces
    lanes = 2 * halo_per * width // piece if piece else 0
    paired = (
        doms % 2 == 0
        and doms & (doms - 1) == 0
        and piece == pieces * halo_per
        and piece % 16 == 0
        and lanes % LANES == 0
        and lanes > 0
    )
    if not paired:
        pieces = 1

    def shape(*dims, dtype=BF16):
        return jax.ShapeDtypeStruct(dims, dtype)

    def vmem(*dims, dtype=BF16):
        return pltpu.VMEM(dims, dtype)

    def hbm(*dims, dtype=BF16):
        return pltpu.HBM(dims, dtype)

    tiles = pl.pallas_call(
        tiles_kernel,
        out_shape=shape(halo_rows, width),
        in_specs=[HBM, HBM],
        out_specs=VMEM,
        scratch_shapes=[
            pltpu.SMEM(route.shape, jnp.int32),
            pltpu.VMEM((local, width), BF16),
            pltpu.SemaphoreType.DMA((2,)),
        ],
        compiler_params=params(8),
        name="halo_tiles",
    )(*in_hbm(route, x))
    halo = exchange(tiles.reshape(doms, halo_per, width), "dom").reshape(halo_rows, width)

    edge, proj, x_near, w_near, load = pl.pallas_call(
        own_kernel,
        out_shape=(
            vmem(heads, local, keys, dtype=F32),
            vmem(local, 3 * width),
            vmem(local, width),
            vmem(*w_struct.shape),
            hbm(snaps + 1, ents, width),
        ),
        in_specs=[HBM] * 7,
        out_specs=(VMEM,) * 4 + (HBM,),
        scratch_shapes=[
            pltpu.VMEM((slots, local), jnp.int32),
            pltpu.VMEM((slots, local), jnp.int32),
            pltpu.VMEM(rel_bias.shape, F32),
            pltpu.VMEM((snaps, ents), jnp.int32),
            pltpu.VMEM((snaps, ents, width), BF16),
            pltpu.VMEM((ents, width), BF16),
            pltpu.SemaphoreType.DMA((9,)),
        ],
        compiler_params=params(8),
        cost_estimate=pl.CostEstimate(flops=10**9, bytes_accessed=4 * 10**6, transcendentals=0),
        name="own_rows",
    )(
        *in_hbm(nbr[0].T, rel_type[0].T, rel_bias, active, cotangent, x, w_struct),
    )
    cots = gather_blocks({0: load}, "snap", snaps // 2, 1)
    cots = [cots[m] for m in range(snaps)]

    hidden = pl.pallas_call(
        functools.partial(forward_kernel, heads),
        out_shape=shape(local, width),
        in_specs=[VMEM] * 5,
        out_specs=VMEM,
        scratch_shapes=[pltpu.VMEM((keys, 2 * width), BF16)],
        compiler_params=params(8),
        name="struct_forward",
    )(x_near, halo, w_near, proj, edge)

    hids = gather_blocks({0: hidden}, "snap", snaps // 2, 1)
    hids = [hids[m] for m in range(snaps)]
    every = snaps * local
    pairs = snaps * (snaps + 1) // 2
    ahead = min(3, snaps - 1)
    soon, late = list(range(ahead)), list(range(ahead, snaps))
    ct, act, *begun = pl.pallas_call(
        functools.partial(arrived_kernel, snaps, soon),
        out_shape=(
            shape(every, width, dtype=F32 if ents % 16 else BF16),
            shape(local, LANES, dtype=F32),
            shape(len(soon) * local, width),
            shape(len(soon) * local, 3 * width),
        ),
        in_specs=[VMEM] * (2 + snaps + len(soon)),
        out_specs=(VMEM,) * 4,
        compiler_params=params(8),
        name="arrived",
    )(pos_embed, w_temp, *cots, *[hids[n] for n in soon])
    *terms, dt_own, cot_own = pl.pallas_call(
        functools.partial(temporal_kernel, snaps, heads, pieces, soon, late),
        out_shape=(shape(share // pieces, 3 * width),) * pieces
        + (shape(local, 3 * width), shape(local, width)),
        in_specs=[VMEM] * (6 + len(late)),
        out_specs=(VMEM,) * (pieces + 2),
        scratch_shapes=[
            pltpu.VMEM((every, width), BF16),
            pltpu.VMEM((every, 3 * width), BF16),
            pltpu.VMEM((every, 3 * width), BF16),
            pltpu.VMEM((2 * every, width), BF16),
            pltpu.VMEM((every, LANES), F32),
            pltpu.VMEM((every, LANES), F32),
            pltpu.VMEM((pairs * local, LANES), BF16),
            pltpu.VMEM((pairs * local, LANES), BF16),
            pltpu.VMEM((share, 3 * width), BF16),
            pltpu.VMEM((len(late) * local, width), BF16),
            pltpu.VMEM((len(late) * local, 3 * width), BF16),
        ],
        compiler_params=params(24 if snaps <= 4 else 56),
        name="temporal",
    )(pos_embed, w_temp, ct, act, *begun, *[hids[n] for n in late])

    if paired:
        got = [terms[0]] + [flipped(terms[k], "dom", 2 * k) for k in range(pieces - 1, 0, -1)]
    else:
        got = exchange(terms[0].reshape(doms, share // doms, 3 * width), "dom")
    back, partial = pl.pallas_call(
        functools.partial(backward_kernel, heads),
        out_shape=(shape(halo_rows, width, dtype=F32), shape(local, width, dtype=F32)),
        in_specs=[VMEM] * 7,
        out_specs=(VMEM, VMEM),
        scratch_shapes=[
            pltpu.VMEM((keys, 2 * width), BF16),
            pltpu.VMEM((local, width), BF16),
            pltpu.VMEM((keys, 2 * width), BF16),
        ],
        compiler_params=params(16),
        cost_estimate=pl.CostEstimate(flops=2 * 10**9, bytes_accessed=8 * 10**6, transcendentals=0),
        name="struct_backward",
    )(dt_own, cot_own, proj, halo, edge, w_near, w_temp)

    if not paired:
        total = jnp.sum(got.astype(F32), axis=0).astype(BF16)
        full = exchange(jnp.broadcast_to(total[None], (doms,) + total.shape), "dom")
        grad_wtemp = full.astype(F32).reshape(share, 3 * width)
        came = exchange(back.astype(BF16).reshape(doms, halo_per, width), "dom")
        picks = (route.reshape(-1)[:, None] == jnp.arange(local, dtype=jnp.int32)).astype(BF16)
        sums = dot_tn(picks, came.reshape(halo_rows, width))
        return ((partial + sums).astype(BF16)[None], grad_wtemp)

    mine = pl.pallas_call(
        functools.partial(outer_sum_kernel, halo_per),
        out_shape=shape(piece, 4 * width),
        in_specs=[VMEM] * (1 + pieces),
        out_specs=VMEM,
        compiler_params=params(8),
        name="outer_sum",
    )(back, *got)
    other = flipped(mine, "dom", 1)
    sums = pl.pallas_call(
        functools.partial(inner_sum_kernel, halo_per),
        out_shape=(shape(piece, 3 * width + lanes),) * pieces,
        in_specs=[VMEM] * 3,
        out_specs=(VMEM,) * pieces,
        compiler_params=params(8),
        name="inner_sum",
    )(back, mine, other)
    order = [*range(2, pieces), 1]
    sums = {0: sums[0]} | {k: flipped(sums[k], "dom", 2 * k) for k in order}
    soon, late = [0], order
    partial, picks, grad_wtemp = pl.pallas_call(
        functools.partial(early_kernel, soon, halo_per),
        out_shape=(
            shape(local, width, dtype=F32),
            shape(halo_rows, local),
            hbm(share, 3 * width, dtype=F32),
        ),
        in_specs=[SMEM] + [VMEM] * (1 + len(soon)),
        out_specs=(VMEM, VMEM, HBM),
        scratch_shapes=[
            pltpu.VMEM((len(soon), piece, 3 * width), F32),
            pltpu.VMEM((halo_rows, width), F32),
            pltpu.SemaphoreType.DMA((len(soon),)),
        ],
        compiler_params=params(8),
        name="early_sums",
    )(route, partial, *[sums[k] for k in soon])
    grad_feat, grad_wtemp = pl.pallas_call(
        functools.partial(last_kernel, late, halo_per),
        out_shape=(hbm(local, width), hbm(share, 3 * width, dtype=F32)),
        in_specs=[VMEM] * 2 + [HBM] + [VMEM] * len(late),
        out_specs=(HBM, HBM),
        scratch_shapes=[
            pltpu.VMEM((local, width), BF16),
            pltpu.VMEM((len(late), piece, 3 * width), F32),
            pltpu.VMEM((halo_rows, width), F32),
            pltpu.SemaphoreType.DMA((len(late) + 1,)),
        ],
        input_output_aliases={2: 1},
        compiler_params=params(8),
        name="last_sums",
    )(picks, partial, *in_hbm(grad_wtemp), *[sums[k] for k in late])
    return (grad_feat[None], grad_wtemp)


def solution(mesh):
    return jax.shard_map(
        per_device,
        mesh=mesh,
        in_specs=(
            P("snap", "dom", None),
            P(),
            P(),
            P(),
            P(),
            P("snap", "dom", None),
            P("snap", "dom", None),
            P("snap", "dom", None, None),
            P(None, ("dom", "snap")),
            P(None, ("dom", "snap"), None),
        ),
        out_specs=(P("snap", "dom", None), P("snap", None)),
        check_vma=False,
    )
```

```python
import functools

import jax
import jax.numpy as jnp
from jax import lax
from jax.experimental import pallas as pl
from jax.experimental.pallas import tpu as pltpu
from jax.sharding import PartitionSpec as P

F32 = jnp.float32
BF16 = jnp.bfloat16
LANES = 128
NEG = -1e30
VMEM = pl.BlockSpec(memory_space=pltpu.VMEM)
SMEM = pl.BlockSpec(memory_space=pltpu.SMEM)
HBM = pl.BlockSpec(memory_space=pltpu.HBM)


def snap_index():
    return lax.axis_index("snap")


def dom_index():
    return lax.axis_index("dom")


def dot_nn(a, b):
    return lax.dot_general(a, b, (((1,), (0,)), ((), ())), preferred_element_type=F32)


def dot_nt(a, b):
    return lax.dot_general(a, b, (((1,), (1,)), ((), ())), preferred_element_type=F32)


def dot_tn(a, b):
    return lax.dot_general(a, b, (((0,), (0,)), ((), ())), preferred_element_type=F32)


def stack_heads(block, head_dim):
    rows, lanes = block.shape
    head = lax.broadcasted_iota(jnp.int32, (rows, lanes), 1) // head_dim
    zero = jnp.zeros_like(block)
    return jnp.concatenate(
        [jnp.where(head == g, block, zero) for g in range(lanes // head_dim)], axis=0
    )


def unstack_heads(stacked, head_dim):
    lanes = stacked.shape[1]
    groups = lanes // head_dim
    rows = stacked.shape[0] // groups
    head = lax.broadcasted_iota(jnp.int32, (rows, lanes), 1) // head_dim
    out = stacked[:rows]
    for g in range(1, groups):
        out = jnp.where(head == g, stacked[g * rows : (g + 1) * rows], out)
    return out


class Fetch:

    def __init__(self, sems, *pairs):
        self.copies = [
            pltpu.make_async_copy(src, dst, sems.at[i]) for i, (src, dst) in enumerate(pairs)
        ]
        for copy in self.copies:
            copy.start()

    def wait(self, *which):
        for i in which:
            self.copies[i].wait()


def pick_rows(route_ref, local):
    doms, per = route_ref.shape
    lane = lax.broadcasted_iota(jnp.int32, (per, local), 1)
    sub = lax.broadcasted_iota(jnp.int32, (per, local), 0)
    tiles = []
    for r in range(doms):
        spot = jnp.zeros((per, local), jnp.int32)
        for j in range(per):
            spot = jnp.where(sub == j, route_ref[r, j], spot)
        tiles.append(jnp.where(lane == spot, 1.0, 0.0))
    return jnp.concatenate(tiles, axis=0).astype(BF16)


def tiles_kernel(route_hbm, x_hbm, out_ref, route, x, sems):
    fetch = Fetch(sems, (route_hbm, route), (x_hbm, x))
    fetch.wait(0, 1)
    out_ref[...] = dot_nn(pick_rows(route, x.shape[0]), x[...]).astype(BF16)


def own_kernel(
    nbr_hbm, rel_hbm, bias_hbm, act_hbm, cot_hbm, x_hbm, w_hbm,
    edge_ref, proj, x, w, load_hbm, nbr, rel, bias, act, cot, flags_s, sems,
):
    heads, rows, keys = edge_ref.shape
    kinds = bias.shape[0]
    snaps, ents, width = cot.shape
    fetch = Fetch(
        sems,
        (cot_hbm, cot),
        (act_hbm, act),
        (nbr_hbm, nbr),
        (rel_hbm, rel),
        (bias_hbm, bias),
        (x_hbm, x),
        (w_hbm, w),
    )
    row = lax.broadcasted_iota(jnp.int32, (ents, ents), 0)
    col = lax.broadcasted_iota(jnp.int32, (ents, ents), 1)
    lane = lax.broadcasted_iota(jnp.int32, (ents, width), 1)
    flags = jnp.zeros((ents, width), F32)
    fetch.wait(1)
    on = act[...].astype(F32)
    for t in range(snaps):
        column = jnp.sum(jnp.where(row == col, on[t : t + 1, :], 0.0), axis=1, keepdims=True)
        flags = jnp.where(lane == t, column, flags)
    flags_s[...] = flags.astype(BF16)
    fetch.wait(0)
    store = Fetch(sems.at[7:], (flags_s, load_hbm.at[snaps]), (cot, load_hbm.at[:snaps]))
    fetch.wait(2, 3, 4)
    counts = edge_counts(nbr, rel, kinds, keys)
    gain = jnp.exp(bias[...])
    for h in range(heads):
        weight = counts[0] * gain[0:1, h : h + 1]
        for r in range(1, kinds):
            weight = weight + counts[r] * gain[r : r + 1, h : h + 1]
        edge_ref[h] = jnp.where(weight > 0, jnp.log(weight), NEG)
    fetch.wait(5, 6)
    for part in range(3):
        cols = slice(part * width, (part + 1) * width)
        proj[:, cols] = dot_nn(x[...], w[:, cols]).astype(BF16)
    store.wait(0, 1)


def fill_table(tab_s, proj, halo, w_kv):
    rows, width = proj.shape[0], halo.shape[1]
    used = rows + halo.shape[0]
    tab_s[:rows, :] = proj[:, width:]
    for part in range(2):
        cols = slice(part * width, (part + 1) * width)
        tab_s[rows:used, cols] = dot_nn(halo[...], w_kv[:, cols]).astype(BF16)
    if tab_s.shape[0] > used:
        tab_s[used:, :] = jnp.zeros((tab_s.shape[0] - used, 2 * width), BF16)


def edge_counts(nbr, rel, kinds, keys):
    bits = 4
    slots, rows = nbr.shape
    target = jnp.transpose(nbr[...].astype(F32))
    one = jnp.transpose(lax.shift_left(jnp.ones_like(rel[...]), bits * rel[...]).astype(F32))
    spot = lax.broadcasted_iota(jnp.int32, (rows, keys), 1).astype(F32)
    packed = jnp.zeros((rows, keys), F32)
    for k in range(slots):
        packed = packed + jnp.where(target[:, k : k + 1] == spot, one[:, k : k + 1], 0.0)
    packed = packed.astype(jnp.int32)
    low = (1 << bits) - 1
    counts = [
        lax.bitwise_and(lax.shift_right_logical(packed, bits * r), low).astype(F32)
        for r in range(kinds)
    ]
    return counts


def edge_attention(p, heads, proj, edge, tab_s, width):
    keys = tab_s.shape[0]
    head_dim = width // heads
    group = LANES // head_dim
    cols = slice(p * LANES, (p + 1) * LANES)
    kk = stack_heads(tab_s[:, cols], head_dim)
    score = dot_nt(proj[:, cols], kk)
    parts = []
    for g in range(group):
        s = score[:, g * keys : (g + 1) * keys] * head_dim ** (-0.5) + edge[p * group + g]
        e = jnp.exp(s - jnp.max(s, axis=1, keepdims=True))
        parts.append(e * (1.0 / jnp.sum(e, axis=1, keepdims=True)))
    return kk, parts


def forward_kernel(heads, x, halo, w, proj, edge, hidden_ref, tab_s):
    width = x.shape[1]
    head_dim = width // heads
    fill_table(tab_s, proj, halo, w.at[:, width:])
    for p in range(width // LANES):
        cols = slice(p * LANES, (p + 1) * LANES)
        vcols = slice(width + p * LANES, width + (p + 1) * LANES)
        _, attn = edge_attention(p, heads, proj, edge, tab_s, width)
        vv = stack_heads(tab_s[:, vcols], head_dim)
        agg = dot_nn(jnp.concatenate([a.astype(BF16) for a in attn], axis=1), vv)
        elu = jnp.where(agg > 0, agg, jnp.exp(jnp.minimum(agg, 0.0)) - 1.0)
        hidden_ref[:, cols] = (x[:, cols].astype(F32) + elu).astype(BF16)


def each(lo, hi, unroll, body):
    if unroll:
        for i in range(lo, hi):
            body(i)
    else:
        lax.fori_loop(lo, hi, lambda i, c: (body(i), c)[1], 0)


def position_of(pos_ref, t):
    pos = pos_ref[...].astype(F32)
    which = lax.broadcasted_iota(jnp.int32, pos.shape, 0)
    return jnp.sum(jnp.where(which == t, pos, 0.0), axis=0, keepdims=True)


def arrived_kernel(snaps, flips, pos_ref, w, *refs):
    cot, hid = refs[:snaps], refs[snaps : snaps + len(flips)]
    ct_ref, act_ref, z_ref, tp_ref = refs[snaps + len(flips) :]
    ents = cot[0].shape[1]
    local, width = hid[0].shape
    me = snap_index()
    for m in range(snaps):
        at = pl.multiple_of(lax.bitwise_xor(me, m) * ents, ents)
        for t in range(snaps):
            ct_ref[pl.ds(t * local + at, ents), :] = cot[m][t].astype(ct_ref.dtype)
        act_ref[pl.ds(at, ents), :] = cot[m][snaps][:, :LANES].astype(F32)
    for i, n in enumerate(flips):
        shift = position_of(pos_ref, lax.bitwise_xor(me, n))
        z_ref[i * local : (i + 1) * local, :] = (hid[i][...].astype(F32) + shift).astype(BF16)
    for part in range(3):
        cols = slice(part * width, (part + 1) * width)
        tp_ref[:, cols] = dot_nn(z_ref[...], w[:, cols]).astype(BF16)


def temporal_kernel(
    snaps, heads, pieces, soon, late, pos_ref, w_s, ct_s, act_s, z_soon, tp_soon, *refs
):
    hid, refs = refs[: len(late)], refs[len(late) :]
    terms_ref = refs[:pieces]
    (
        dt_own_ref, cot_own_ref,
        z_s, tp_s, dt_s, prod_s, s_s, d_s, a_s, ds_s, terms_s, z_late, tp_late,
    ) = refs[pieces:]
    local, width = hid[0].shape
    head_dim = width // heads
    scale = head_dim ** (-0.5)
    unroll = snaps <= 4
    me, outer = snap_index(), dom_index() // 2
    def rows_of(t):
        return pl.ds(t * local if isinstance(t, int) else pl.multiple_of(t * local, local), local)

    for i, n in enumerate(late):
        shift = position_of(pos_ref, lax.bitwise_xor(me, n))
        z_late[i * local : (i + 1) * local, :] = (hid[i][...].astype(F32) + shift).astype(BF16)
    for part in range(3):
        cols = slice(part * width, (part + 1) * width)
        tp_late[:, cols] = dot_nn(z_late[...], w_s[:, cols]).astype(BF16)
    for flips, z_ref, tp_ref in ((soon, z_soon, tp_soon), (late, z_late, tp_late)):
        for i, n in enumerate(flips):
            t = lax.bitwise_xor(me, n)
            z_s[rows_of(t), :] = z_ref[i * local : (i + 1) * local, :]
            tp_s[rows_of(t), :] = tp_ref[i * local : (i + 1) * local, :]
    lane_head = lax.broadcasted_iota(jnp.int32, (width, LANES), 0) // head_dim
    fold = (lane_head == lax.broadcasted_iota(jnp.int32, (width, LANES), 1)).astype(F32)
    fold = fold.astype(BF16)
    head_lane = lax.broadcasted_iota(jnp.int32, (LANES, width), 1) // head_dim
    spread = (head_lane == lax.broadcasted_iota(jnp.int32, (LANES, width), 0)).astype(F32)
    spread_scaled = (spread * scale).astype(BF16)
    spread = spread.astype(BF16)
    act = act_s[...]
    snap_lane = lax.broadcasted_iota(jnp.int32, act.shape, 1)
    def pair_rows(t, u):
        return rows_of((t * t + t) // 2 + u)

    def reduced(lo, hi, fn, start):
        if unroll:
            for i in range(lo, hi):
                start = fn(i, start)
            return start
        return lax.fori_loop(lo, hi, fn, start)

    def one_snap(t):
        used = (t + 1 if unroll else snaps) * local
        half = snaps * local

        def product(u):
            q, k, v = (
                tp_s[rows_of(i), part * width : (part + 1) * width]
                for part, i in ((0, t), (1, u), (2, u))
            )
            prod_s[rows_of(u), :] = q * k
            prod_s[rows_of(snaps + u), :] = ct_s[rows_of(t), :].astype(BF16) * v

        each(0, t + 1, unroll, product)
        s_s[:used, :] = dot_nn(prod_s[:used, :], fold)
        d_s[:used, :] = dot_nn(prod_s[half : half + used, :], fold).astype(BF16).astype(F32)

        def mask(u):
            on = jnp.sum(jnp.where(snap_lane == u, act, 0.0), axis=1, keepdims=True)
            s_s[rows_of(u), :] = jnp.where((on > 0.5) | (u == t), s_s[rows_of(u), :] * scale, NEG)

        each(0, t + 1, unroll, mask)

        top = reduced(
            0,
            t + 1,
            lambda u, c: jnp.maximum(c, s_s[rows_of(u), :]),
            jnp.full((local, LANES), NEG, F32),
        )

        def expo(u, total):
            e = jnp.exp(s_s[rows_of(u), :] - top)
            s_s[rows_of(u), :] = e
            return total + e

        inv = 1.0 / reduced(0, t + 1, expo, jnp.zeros((local, LANES), F32))

        def weigh(u, total):
            a = s_s[rows_of(u), :] * inv
            s_s[rows_of(u), :] = a
            return total + a * d_s[rows_of(u), :]

        dot = reduced(0, t + 1, weigh, jnp.zeros((local, LANES), F32))

        def keep(u):
            a = s_s[rows_of(u), :]
            a_s[pair_rows(t, u), :] = a.astype(BF16)
            ds_s[pair_rows(t, u), :] = (a * (d_s[rows_of(u), :] - dot)).astype(BF16)

        each(0, t + 1, unroll, keep)

    each(0, snaps, unroll, one_snap)
    for p in range(width // LANES):
        c0 = p * LANES
        cols = slice(c0, c0 + LANES)

        def columns(part, i):
            return tp_s[rows_of(i), part * width + c0 : part * width + c0 + LANES].astype(F32)

        def query(t):
            def add(u, dq):
                return dq + dot_nn(ds_s[pair_rows(t, u), :], spread_scaled[:, cols]) * columns(1, u)

            dq = reduced(0, t + 1, add, jnp.zeros((local, LANES), F32))
            dt_s[rows_of(t), cols] = dq.astype(BF16)

        def key_value(u):
            def add(t, grads):
                dk, dv = grads
                dk = dk + dot_nn(ds_s[pair_rows(t, u), :], spread_scaled[:, cols]) * columns(0, t)
                wide = dot_nn(a_s[pair_rows(t, u), :], spread[:, cols])
                return dk, dv + wide * ct_s[rows_of(t), cols].astype(F32)

            zero = jnp.zeros((local, LANES), F32)
            dk, dv = reduced(u, snaps, add, (zero, zero))
            dt_s[rows_of(u), width + c0 : width + c0 + LANES] = dk.astype(BF16)
            dt_s[rows_of(u), 2 * width + c0 : 2 * width + c0 + LANES] = dv.astype(BF16)

        each(0, snaps, unroll, query)
        each(0, snaps, unroll, key_value)
    share = width // snaps
    if share % LANES == 0:
        z_mine = z_s[:, pl.ds(pl.multiple_of(me * share, LANES), share)]
    else:
        pick = (
            lax.broadcasted_iota(jnp.int32, (width, share), 0)
            == lax.broadcasted_iota(jnp.int32, (width, share), 1) + me * share
        )
        z_mine = dot_nn(z_s[...], pick.astype(F32).astype(BF16)).astype(BF16)
    for part in range(3):
        cols = slice(part * width, (part + 1) * width)
        terms_s[:, cols] = dot_tn(z_mine, dt_s[:, cols]).astype(BF16)
    piece = share // pieces
    for k in range(pieces):
        if pieces == 1:
            terms_ref[k][...] = terms_s[...]
        else:
            at = pl.multiple_of(lax.bitwise_xor(outer, k) * piece, piece)
            terms_ref[k][...] = terms_s[pl.ds(at, piece), :]
    dt_own_ref[...] = dt_s[rows_of(me), :]
    cot_own_ref[...] = ct_s[rows_of(me), :].astype(BF16)


def backward_kernel(
    heads, dt, cot, proj, halo, edge, ws, wt, back_ref, part_ref, tab_s, dq_s, dtab_s,
):
    rows, width = cot.shape
    halo_rows = halo.shape[0]
    keys = tab_s.shape[0]
    head_dim = width // heads
    group = LANES // head_dim
    scale = head_dim ** (-0.5)
    dh = cot[...].astype(F32) + dot_nt(dt[...], wt[...])
    part_ref[...] = dh.astype(BF16).astype(F32)
    fill_table(tab_s, proj, halo, ws.at[:, width:])
    for p in range(width // LANES):
        cols = slice(p * LANES, (p + 1) * LANES)
        vcols = slice(width + p * LANES, width + (p + 1) * LANES)
        kk, attn = edge_attention(p, heads, proj, edge, tab_s, width)
        vv = stack_heads(tab_s[:, vcols], head_dim)
        attn_b = jnp.concatenate([a.astype(BF16) for a in attn], axis=1)
        agg = dot_nn(attn_b, vv)
        da = part_ref[:, cols] * jnp.where(agg > 0, 1.0, jnp.exp(jnp.minimum(agg, 0.0)))
        da = da.astype(BF16)
        dattn = dot_nt(da, vv).astype(BF16).astype(F32)
        ds = []
        for g in range(group):
            ad = attn[g] * dattn[:, g * keys : (g + 1) * keys]
            ds.append((ad - attn[g] * jnp.sum(ad, axis=1, keepdims=True)).astype(BF16))
        ds = jnp.concatenate(ds, axis=1)
        dq_s[:, cols] = (dot_nn(ds, kk) * scale).astype(BF16)
        dtab_s[:, cols] = (unstack_heads(dot_tn(ds, proj[:, cols]), head_dim) * scale).astype(BF16)
        dtab_s[:, vcols] = unstack_heads(dot_tn(attn_b, da), head_dim).astype(BF16)
    back_ref[...] = dot_nt(dtab_s[rows : rows + halo_rows, :], ws[:, width:])
    part_ref[...] += dot_nt(dq_s[...], ws[:, :width]) + dot_nt(dtab_s[:rows, :], ws[:, width:])


def tile_of(flip, back_ref, per):
    at = lax.bitwise_xor(dom_index(), flip) * per
    return back_ref[pl.ds(pl.multiple_of(at, per), per), :]


def outer_sum_kernel(per, back_ref, *refs):
    *terms, out_ref = refs
    wide = terms[0].shape[1]
    total = terms[0][...].astype(F32)
    for term in terms[1:]:
        total = total + term[...].astype(F32)
    out_ref[:, :wide] = total.astype(BF16)
    tiles = [tile_of(2 * k + 1, back_ref, per) for k in range(len(terms))]
    out_ref[:, wide:] = jnp.concatenate(tiles, axis=0).astype(BF16)


def inner_sum_kernel(per, back_ref, mine_ref, other_ref, *out):
    rows = mine_ref.shape[0]
    wide = mine_ref.shape[1] - back_ref.shape[1]
    lanes = out[0].shape[1] - wide
    total = (mine_ref[:, :wide].astype(F32) + other_ref[:, :wide].astype(F32)).astype(BF16)
    passing = other_ref[:, wide:].astype(F32)
    for k in range(len(out)):
        out[k][:, :wide] = total
        both = [tile_of(2 * k, back_ref, per), passing[k * per : (k + 1) * per]]
        folds = [
            tile[:, i * lanes : (i + 1) * lanes]
            for tile in both
            for i in range(rows // (2 * per))
        ]
        out[k][:, wide:] = jnp.concatenate(folds, axis=0).astype(BF16)


def unpack_sums(flips, per, got, wtemp, wtemp_hbm, came_s, sems):
    rows = got[0].shape[0]
    lanes = got[0].shape[1] - wtemp.shape[2]
    folds = rows // (2 * per)
    stores = []
    came_s[...] = jnp.zeros_like(came_s)
    for i, k in enumerate(flips):
        wtemp[i] = got[i][:, : wtemp.shape[2]].astype(F32)
        at = pl.multiple_of(lax.bitwise_xor(dom_index() // 2, k) * rows, rows)
        stores.append(Fetch(sems.at[i:], (wtemp.at[i], wtemp_hbm.at[pl.ds(at, rows), :])))
        folded = got[i][:, wtemp.shape[2] :].astype(F32)
        for j in range(2):
            d = pl.multiple_of(lax.bitwise_xor(dom_index(), 2 * k + j) * per, per)
            for f in range(folds):
                row = (j * folds + f) * per
                came_s[pl.ds(d, per), f * lanes : (f + 1) * lanes] = folded[row : row + per]
    return stores


def early_kernel(flips, per, route_ref, part_ref, *refs):
    got = refs[: len(flips)]
    sum_ref, picks_ref, wtemp_hbm, wtemp, came_s, sems = refs[len(flips) :]
    stores = unpack_sums(flips, per, got, wtemp, wtemp_hbm, came_s, sems)
    picks = pick_rows(route_ref, part_ref.shape[0])
    picks_ref[...] = picks
    sum_ref[...] = part_ref[...] + dot_tn(picks, came_s[...].astype(BF16))
    for store in stores:
        store.wait(0)


def last_kernel(flips, per, picks_ref, sum_ref, _, *refs):
    got = refs[: len(flips)]
    feat_hbm, wtemp_hbm, feat, wtemp, came_s, sems = refs[len(flips) :]
    stores = unpack_sums(flips, per, got, wtemp, wtemp_hbm, came_s, sems)
    feat[...] = (sum_ref[...] + dot_tn(picks_ref[...], came_s[...].astype(BF16))).astype(BF16)
    stores.append(Fetch(sems.at[len(flips) :], (feat, feat_hbm)))
    for store in stores:
        store.wait(0)


def params(mib):
    return pltpu.CompilerParams(vmem_limit_bytes=mib * 1024 * 1024)


def gather_blocks(held, axis, bit, last):
    held = dict(held)
    while bit >= last:
        for m in sorted(held):
            held[m ^ bit] = flipped(held[m], axis, bit)
        bit //= 2
    return held


def in_hbm(*arrays):
    return [pltpu.with_memory_space_constraint(a, pltpu.HBM) for a in arrays]


def exchange(tiles, axis):
    return lax.all_to_all(tiles, axis, split_axis=0, concat_axis=0, tiled=True)


def flipped(block, axis, flip):
    count = lax.axis_size(axis)
    return lax.ppermute(block, axis, [(i, i ^ flip) for i in range(count)])


def per_device(
    feat, w_struct, w_temp, pos_embed, rel_bias, nbr, rel_type, send_idx, active, cotangent
):
    x = feat[0]
    local, width = x.shape
    heads = rel_bias.shape[1]
    slots = nbr.shape[2]
    doms = lax.axis_size("dom")
    snaps = lax.axis_size("snap")
    ents = local // snaps
    route = send_idx[0, 0]
    halo_per = route.shape[1]
    halo_rows = doms * halo_per
    keys = -(-(local + halo_rows) // LANES) * LANES
    share = width // snaps
    pieces = doms // 2
    piece = share // pieces
    lanes = 2 * halo_per * width // piece if piece else 0
    paired = (
        doms % 2 == 0
        and doms & (doms - 1) == 0
        and piece == pieces * halo_per
        and piece % 16 == 0
        and lanes % LANES == 0
        and lanes > 0
    )
    if not paired:
        pieces = 1

    def shape(*dims, dtype=BF16):
        return jax.ShapeDtypeStruct(dims, dtype)

    def vmem(*dims, dtype=BF16):
        return pltpu.VMEM(dims, dtype)

    def hbm(*dims, dtype=BF16):
        return pltpu.HBM(dims, dtype)

    tiles = pl.pallas_call(
        tiles_kernel,
        out_shape=shape(halo_rows, width),
        in_specs=[HBM, HBM],
        out_specs=VMEM,
        scratch_shapes=[
            pltpu.SMEM(route.shape, jnp.int32),
            pltpu.VMEM((local, width), BF16),
            pltpu.SemaphoreType.DMA((2,)),
        ],
        compiler_params=params(8),
        name="halo_tiles",
    )(*in_hbm(route, x))
    halo = exchange(tiles.reshape(doms, halo_per, width), "dom").reshape(halo_rows, width)

    edge, proj, x_near, w_near, load = pl.pallas_call(
        own_kernel,
        out_shape=(
            vmem(heads, local, keys, dtype=F32),
            vmem(local, 3 * width),
            vmem(local, width),
            vmem(*w_struct.shape),
            hbm(snaps + 1, ents, width),
        ),
        in_specs=[HBM] * 7,
        out_specs=(VMEM,) * 4 + (HBM,),
        scratch_shapes=[
            pltpu.VMEM((slots, local), jnp.int32),
            pltpu.VMEM((slots, local), jnp.int32),
            pltpu.VMEM(rel_bias.shape, F32),
            pltpu.VMEM((snaps, ents), jnp.int32),
            pltpu.VMEM((snaps, ents, width), BF16),
            pltpu.VMEM((ents, width), BF16),
            pltpu.SemaphoreType.DMA((9,)),
        ],
        compiler_params=params(8),
        cost_estimate=pl.CostEstimate(flops=10**9, bytes_accessed=4 * 10**6, transcendentals=0),
        name="own_rows",
    )(
        *in_hbm(nbr[0].T, rel_type[0].T, rel_bias, active, cotangent, x, w_struct),
    )
    cots = gather_blocks({0: load}, "snap", snaps // 2, 1)
    cots = [cots[m] for m in range(snaps)]

    hidden = pl.pallas_call(
        functools.partial(forward_kernel, heads),
        out_shape=shape(local, width),
        in_specs=[VMEM] * 5,
        out_specs=VMEM,
        scratch_shapes=[pltpu.VMEM((keys, 2 * width), BF16)],
        compiler_params=params(8),
        name="struct_forward",
    )(x_near, halo, w_near, proj, edge)

    hids = gather_blocks({0: hidden}, "snap", snaps // 2, 1)
    hids = [hids[m] for m in range(snaps)]
    every = snaps * local
    pairs = snaps * (snaps + 1) // 2
    ahead = min(3, snaps - 1)
    soon, late = list(range(ahead)), list(range(ahead, snaps))
    ct, act, *begun = pl.pallas_call(
        functools.partial(arrived_kernel, snaps, soon),
        out_shape=(
            shape(every, width, dtype=F32 if ents % 16 else BF16),
            shape(local, LANES, dtype=F32),
            shape(len(soon) * local, width),
            shape(len(soon) * local, 3 * width),
        ),
        in_specs=[VMEM] * (2 + snaps + len(soon)),
        out_specs=(VMEM,) * 4,
        compiler_params=params(8),
        name="arrived",
    )(pos_embed, w_temp, *cots, *[hids[n] for n in soon])
    *terms, dt_own, cot_own = pl.pallas_call(
        functools.partial(temporal_kernel, snaps, heads, pieces, soon, late),
        out_shape=(shape(share // pieces, 3 * width),) * pieces
        + (shape(local, 3 * width), shape(local, width)),
        in_specs=[VMEM] * (6 + len(late)),
        out_specs=(VMEM,) * (pieces + 2),
        scratch_shapes=[
            pltpu.VMEM((every, width), BF16),
            pltpu.VMEM((every, 3 * width), BF16),
            pltpu.VMEM((every, 3 * width), BF16),
            pltpu.VMEM((2 * every, width), BF16),
            pltpu.VMEM((every, LANES), F32),
            pltpu.VMEM((every, LANES), F32),
            pltpu.VMEM((pairs * local, LANES), BF16),
            pltpu.VMEM((pairs * local, LANES), BF16),
            pltpu.VMEM((share, 3 * width), BF16),
            pltpu.VMEM((len(late) * local, width), BF16),
            pltpu.VMEM((len(late) * local, 3 * width), BF16),
        ],
        compiler_params=params(24 if snaps <= 4 else 56),
        name="temporal",
    )(pos_embed, w_temp, ct, act, *begun, *[hids[n] for n in late])

    if paired:
        got = [terms[0]] + [flipped(terms[k], "dom", 2 * k) for k in range(pieces - 1, 0, -1)]
    else:
        got = exchange(terms[0].reshape(doms, share // doms, 3 * width), "dom")
    back, partial = pl.pallas_call(
        functools.partial(backward_kernel, heads),
        out_shape=(shape(halo_rows, width, dtype=F32), shape(local, width, dtype=F32)),
        in_specs=[VMEM] * 7,
        out_specs=(VMEM, VMEM),
        scratch_shapes=[
            pltpu.VMEM((keys, 2 * width), BF16),
            pltpu.VMEM((local, width), BF16),
            pltpu.VMEM((keys, 2 * width), BF16),
        ],
        compiler_params=params(16),
        cost_estimate=pl.CostEstimate(flops=2 * 10**9, bytes_accessed=8 * 10**6, transcendentals=0),
        name="struct_backward",
    )(dt_own, cot_own, proj, halo, edge, w_near, w_temp)

    if not paired:
        total = jnp.sum(got.astype(F32), axis=0).astype(BF16)
        full = exchange(jnp.broadcast_to(total[None], (doms,) + total.shape), "dom")
        grad_wtemp = full.astype(F32).reshape(share, 3 * width)
        came = exchange(back.astype(BF16).reshape(doms, halo_per, width), "dom")
        picks = (route.reshape(-1)[:, None] == jnp.arange(local, dtype=jnp.int32)).astype(BF16)
        sums = dot_tn(picks, came.reshape(halo_rows, width))
        return ((partial + sums).astype(BF16)[None], grad_wtemp)

    mine = pl.pallas_call(
        functools.partial(outer_sum_kernel, halo_per),
        out_shape=shape(piece, 4 * width),
        in_specs=[VMEM] * (1 + pieces),
        out_specs=VMEM,
        compiler_params=params(8),
        name="outer_sum",
    )(back, *got)
    other = flipped(mine, "dom", 1)
    sums = pl.pallas_call(
        functools.partial(inner_sum_kernel, halo_per),
        out_shape=(shape(piece, 3 * width + lanes),) * pieces,
        in_specs=[VMEM] * 3,
        out_specs=(VMEM,) * pieces,
        compiler_params=params(8),
        name="inner_sum",
    )(back, mine, other)
    order = [*range(2, pieces), 1]
    sums = {0: sums[0]} | {k: flipped(sums[k], "dom", 2 * k) for k in order}
    soon, late = [0], order
    partial, picks, grad_wtemp = pl.pallas_call(
        functools.partial(early_kernel, soon, halo_per),
        out_shape=(
            shape(local, width, dtype=F32),
            shape(halo_rows, local),
            hbm(share, 3 * width, dtype=F32),
        ),
        in_specs=[SMEM] + [VMEM] * (1 + len(soon)),
        out_specs=(VMEM, VMEM, HBM),
        scratch_shapes=[
            pltpu.VMEM((len(soon), piece, 3 * width), F32),
            pltpu.VMEM((halo_rows, width), F32),
            pltpu.SemaphoreType.DMA((len(soon),)),
        ],
        compiler_params=params(8),
        name="early_sums",
    )(route, partial, *[sums[k] for k in soon])
    grad_feat, grad_wtemp = pl.pallas_call(
        functools.partial(last_kernel, late, halo_per),
        out_shape=(hbm(local, width), hbm(share, 3 * width, dtype=F32)),
        in_specs=[VMEM] * 2 + [HBM] + [VMEM] * len(late),
        out_specs=(HBM, HBM),
        scratch_shapes=[
            pltpu.VMEM((local, width), BF16),
            pltpu.VMEM((len(late), piece, 3 * width), F32),
            pltpu.VMEM((halo_rows, width), F32),
            pltpu.SemaphoreType.DMA((len(late) + 1,)),
        ],
        input_output_aliases={2: 1},
        compiler_params=params(8),
        name="last_sums",
    )(picks, partial, *in_hbm(grad_wtemp), *[sums[k] for k in late])
    return (grad_feat[None], grad_wtemp)


def solution(mesh):
    return jax.shard_map(
        per_device,
        mesh=mesh,
        in_specs=(
            P("snap", "dom", None),
            P(),
            P(),
            P(),
            P(),
            P("snap", "dom", None),
            P("snap", "dom", None),
            P("snap", "dom", None, None),
            P(None, ("dom", "snap")),
            P(None, ("dom", "snap"), None),
        ),
        out_specs=(P("snap", "dom", None), P("snap", None)),
        check_vma=False,
    )
```
